32 devices in a mesh: rep: 8 (over y, x, core), fsdp: 4 (over z).
Axes of the slice: x: 2, y: 2, z: 4, core: 2. Of those that a mesh axis runs over, the one named last changes fastest.
Arguments:
- tokens: bfloat16 [4096, 1600], P(('rep', 'fsdp')), may hold values from -6 to 6
- cotangent: bfloat16 [4096, 1600], P(('rep', 'fsdp')), may hold values from -6 to 6
- lengths: int32 [32, 3], P(('rep', 'fsdp')), may hold values from 1 to 96, 128 in all within a row
- source_slot: int32 [32, 128], P(('rep', 'fsdp')), may hold values from 0 to 127, each once within a row
- norm_in: float32 [1600], replicated, may hold values from 0.5 to 1.5
- w_qkv: bfloat16 [1600, 2240], P('fsdp'), may hold values from -0.15625 to 0.15625
- w_mamba_in: bfloat16 [1600, 6400], P('fsdp'), may hold values from -0.15625 to 0.15625
- conv_weight: float32 [4, 3200], replicated, may hold values from -3 to 3
- conv_bias: float32 [3200], replicated, may hold values from -3 to 3
- x_proj: float32 [3200, 132], replicated, may hold values from -0.109375 to 0.109375
- dt_proj: float32 [100, 3200], replicated, may hold values from -0.625 to 0.625
- dt_bias: float32 [3200], replicated, may hold values from -5 to -1
- a_log: float32 [16, 3200], replicated, may hold values from 0 to 2.8
- d_skip: float32 [3200], replicated, may hold values from 0.5 to 1.5
- w_mamba_out: bfloat16 [3200, 1600], P('fsdp'), may hold values from -0.109375 to 0.109375
- norm_attn: float32 [1600], replicated, may hold values from 0.5 to 1.5
- norm_ssm: float32 [1600], replicated, may hold values from 0.5 to 1.5
- w_mix_out: bfloat16 [1600, 1600], P('fsdp'), may hold values from -0.15625 to 0.15625
- norm_ffn: float32 [1600], replicated, may hold values from 0.5 to 1.5
- w_gate: bfloat16 [1600, 5504], P('fsdp'), may hold values from -0.15625 to 0.15625
- w_up: bfloat16 [1600, 5504], P('fsdp'), may hold values from -0.15625 to 0.15625
- w_down: bfloat16 [5504, 1600], P('fsdp'), may hold values from -0.078125 to 0.078125
Outputs:
- mixed_out: bfloat16 [4096, 1600], P(('rep', 'fsdp'))
- grad_tokens: bfloat16 [4096, 1600], P(('rep', 'fsdp'))
- grad_norm_in: float32 [1600], replicated
- grad_w_qkv: float32 [1600, 2240], P('fsdp')
- grad_w_mamba_in: float32 [1600, 6400], P('fsdp')
- grad_conv_weight: float32 [4, 3200], replicated
- grad_conv_bias: float32 [3200], replicated
- grad_x_proj: float32 [3200, 132], replicated
- grad_dt_proj: float32 [100, 3200], replicated
- grad_dt_bias: float32 [3200], replicated
- grad_a_log: float32 [16, 3200], replicated
- grad_d_skip: float32 [3200], replicated
- grad_w_mamba_out: float32 [3200, 1600], P('fsdp')
- grad_norm_attn: float32 [1600], replicated
- grad_norm_ssm: float32 [1600], replicated
- grad_w_mix_out: float32 [1600, 1600], P('fsdp')
- grad_norm_ffn: float32 [1600], replicated
- grad_w_gate: float32 [1600, 5504], P('fsdp')
- grad_w_up: float32 [1600, 5504], P('fsdp')
- grad_w_down: float32 [5504, 1600], P('fsdp')
The draws below stay inside these ranges and needn't reach their ends.
Inputs may be any that keep to these rules, and one draw needn't show every extreme that they name: Each device's 3 lengths sum to 128, and the longest is exactly 96. `source_slot`: each row is a permutation of 0 to 127.
All inputs are finite; a program needn't handle non-finite values.
Results may differ from the reference program's by a relative error of at most 0.018.
Values may be sent and summed in bfloat16 or wider, within the bound.
A program may use at most 448 MiB of HBM per device.

```python
import math
import jax
import jax.numpy as jnp
import numpy as np
from jax import lax

D = 1600
HEADS = 25
KV_HEADS = 5
HEAD_DIM = 64
INNER = 3200
STATE = 16
DT_RANK = 100
CONV = 4
FF = 5504
WINDOW = 1024
SPAN = 8
NSEQ = 3
TOK_DEV = 128
MAX_LEN = 96
QKV = 2240
TOKENS = 4096
N_REP = 8
N_FSDP = 4


def block_levels(key, extent, cuts, least, high):
    loudness = 1.0
    for axis_at, shards_of in cuts:
        heights = jax.random.uniform(jax.random.fold_in(jax.random.fold_in(key, 6), axis_at), (shards_of,), jnp.float32, least / len(cuts), high / len(cuts))
        loudness = loudness * jnp.repeat(jnp.exp(heights), extent[axis_at] // shards_of).reshape((-1,) + (1,) * (len(extent) - 1 - axis_at))
    return loudness


def split_up(count, total, bound, slope):
    loads = [(1 << 20) // math.isqrt(standing ** slope) + 1 for standing in range(2, count + 1)]
    spare, holding = total - bound - (count - 1), [1] * (count - 1)
    while spare > 0:
        free = [i for i in range(count - 1) if holding[i] < bound]
        whole, left = sum([loads[i] for i in free]), spare
        for i in free:
            extra = min(bound - holding[i], max(1, left * loads[i] // whole), spare)
            holding[i] = holding[i] + extra
            spare = spare - extra
    return np.array([bound] + holding)


def ragged(key, count, total, bound, slope):
    if count == 2:
        one = jax.random.randint(key, (), max(1, total - bound), min(bound, total - 1) + 1)
        return jnp.stack([one, total - one])
    tallies = jnp.asarray(split_up(count, total, bound, slope), jnp.int32)
    couples = (count - 1) // 2
    donor, receiver = tallies[1:1 + 2 * couples:2], tallies[2:2 + 2 * couples:2]
    slack = jnp.minimum(donor - 1, bound - receiver)
    moved = jax.random.randint(jax.random.fold_in(key, 1), (couples,), 0, 1 << 20) % (slack + 1)
    tallies = tallies.at[1:1 + 2 * couples:2].set(donor - moved).at[2:2 + 2 * couples:2].set(receiver + moved)
    return tallies[jax.random.permutation(jax.random.fold_in(key, 2), count)]


def gaussian(own_key, dims, deviation, reach, shards=(), held_as=jnp.bfloat16):
    level = block_levels(own_key, dims, shards, -0.22, 0.18) if shards else 1.0
    array = jax.random.normal(own_key, dims, jnp.float32) * deviation * level
    return jnp.minimum(jnp.maximum(array, -reach), reach).astype(held_as)


def setup_inputs(seed: int = 0) -> dict:
    key_of = jax.random.split(jax.random.key(seed), 23)
    return {
        "tokens": gaussian(key_of[0], (TOKENS, D), 1.0, 6.0, ((0, 32),)),
        "cotangent": gaussian(key_of[1], (TOKENS, D), 1.0, 6.0, ((0, 32),)),
        "lengths": jax.vmap(lambda own: ragged(own, NSEQ, TOK_DEV, MAX_LEN, 2))(jax.random.split(key_of[2], (N_REP * N_FSDP))).reshape((N_REP * N_FSDP, NSEQ)).astype(jnp.int32),
        "source_slot": jax.vmap(lambda own: jax.random.permutation(own, TOK_DEV))(jax.random.split(key_of[3], (N_REP * N_FSDP))).reshape((N_REP * N_FSDP, TOK_DEV)).astype(jnp.int32),
        "norm_in": jnp.clip(1.0 + 0.1 * jax.random.normal(key_of[4], (D,), jnp.float32), 0.5, 1.5),
        "w_qkv": gaussian(key_of[5], (D, QKV), D ** -0.5, 0.15625, ((0, 4),)),
        "w_mamba_in": gaussian(key_of[6], (D, 2 * INNER), D ** -0.5, 0.15625, ((0, 4),)),
        "conv_weight": gaussian(key_of[7], (CONV, INNER), 0.5, 3.0, (), jnp.float32),
        "conv_bias": gaussian(key_of[8], (INNER,), 0.5, 3.0, (), jnp.float32),
        "x_proj": gaussian(key_of[9], (INNER, DT_RANK + 2 * STATE), INNER ** -0.5, 0.109375, (), jnp.float32),
        "dt_proj": gaussian(key_of[10], (DT_RANK, INNER), DT_RANK ** -0.5, 0.625, (), jnp.float32),
        "dt_bias": jnp.clip(jax.random.uniform(key_of[11], (INNER,), jnp.float32, -5.0, -1.0), -5.0, -1.0),
        "a_log": jnp.clip(jax.random.uniform(key_of[12], (STATE, INNER), jnp.float32, 0.0, 2.8), 0.0, 2.8),
        "d_skip": jnp.clip(jax.random.uniform(key_of[13], (INNER,), jnp.float32, 0.5, 1.5), 0.5, 1.5),
        "w_mamba_out": gaussian(key_of[14], (INNER, D), INNER ** -0.5, 0.109375, ((0, 4),)),
        "norm_attn": jnp.clip(1.0 + 0.1 * jax.random.normal(key_of[15], (D,), jnp.float32), 0.5, 1.5),
        "norm_ssm": jnp.clip(1.0 + 0.1 * jax.random.normal(key_of[16], (D,), jnp.float32), 0.5, 1.5),
        "w_mix_out": gaussian(key_of[17], (D, D), D ** -0.5, 0.15625, ((0, 4),)),
        "norm_ffn": jnp.clip(1.0 + 0.1 * jax.random.normal(key_of[18], (D,), jnp.float32), 0.5, 1.5),
        "w_gate": gaussian(key_of[19], (D, FF), D ** -0.5, 0.15625, ((0, 4),)),
        "w_up": gaussian(key_of[20], (D, FF), D ** -0.5, 0.15625, ((0, 4),)),
        "w_down": gaussian(key_of[21], (FF, D), FF ** -0.5, 0.078125, ((0, 4),)),
    }


epsilon = 1e-06
highest_precision = lax.Precision.HIGHEST

@jax.custom_vjp
def low(v):
    return lax.optimization_barrier(v.astype(jnp.bfloat16)).astype(jnp.float32)

@jax.custom_vjp
def lowered_backward(v):
    return v

def low_keep(v):
    return (low(v), None)

def low_pass(kept, grad):
    return (grad,)

def back_keep(v):
    return (v, None)

def back_low(kept, grad):
    return (low(grad),)
low.defvjp(low_keep, low_pass)
lowered_backward.defvjp(back_keep, back_low)

def matmul_high(left, right):
    return jnp.dot(left, right, precision=highest_precision, preferred_element_type=jnp.float32)

def rms_norm(value_rows, gain):
    return value_rows * lax.rsqrt(lax.optimization_barrier(jnp.mean(value_rows * value_rows, axis=-1, keepdims=True)) + epsilon) * gain

def segment_info(length_row, count):
    ends = jnp.cumsum(length_row, dtype=jnp.int32)
    positions = jnp.arange(count, dtype=jnp.int32)
    seg_ids = lax.optimization_barrier(jnp.sum((positions[:, None] >= ends[None, :-1]).astype(jnp.int32), axis=1))
    starts = ends - length_row
    first_flag = jnp.any(positions[:, None] == starts[None, :], axis=1).astype(jnp.float32)
    distance = positions[:, None] - positions[None, :]
    allowed = (seg_ids[:, None] == seg_ids[None, :]) & (distance >= 0) & (distance < WINDOW)
    return (seg_ids, first_flag, allowed)

def span_scan(inner_act, step_size, input_mix, output_mix, decay_rate, first_flag):
    count, channels = inner_act.shape
    blocks = count // SPAN

    def advance(carry_state, row_data):
        act_row, step_row, input_row, output_row, start_row = row_data
        carry_state = jnp.exp(step_row[None, :] * decay_rate) * carry_state * (1.0 - start_row) + input_row[:, None] * (step_row * act_row)[None, :]
        return (carry_state, lax.optimization_barrier(jnp.sum(carry_state * output_row[:, None], axis=0)))

    def block_scan(carry_state, block_data):
        return lax.scan(advance, carry_state, block_data)
    checked = jax.checkpoint(block_scan)
    block_data = tuple((jnp.reshape(item_arr, (blocks, SPAN) + item_arr.shape[1:]) for item_arr in (inner_act, step_size, input_mix, output_mix, first_flag)))
    zero_state = jnp.zeros((decay_rate.shape[0], channels), jnp.float32)
    unused, scanned = lax.scan(checked, zero_state, block_data)
    return scanned.reshape(count, channels)

def mamba_core(xs_in, gate_z, mamba_params, seg_ids, first_flag):
    conv_weight, conv_bias, x_proj, dt_proj, dt_bias, a_log, d_skip = mamba_params
    count = xs_in.shape[0]
    conv_sum = xs_in * conv_weight[CONV - 1] + conv_bias
    for shift_steps in range(1, CONV):
        shifted = jnp.concatenate([jnp.zeros((shift_steps, xs_in.shape[1]), jnp.float32), xs_in[:count - shift_steps]], axis=0)
        earlier = jnp.concatenate([jnp.full((shift_steps,), -1, jnp.int32), seg_ids[:count - shift_steps]], axis=0)
        same_seq = (earlier == seg_ids)[:, None]
        conv_sum = conv_sum + jnp.where(same_seq, shifted, 0.0) * conv_weight[CONV - 1 - shift_steps]
    inner_act = jax.nn.silu(conv_sum)
    projected = matmul_high(inner_act, x_proj)
    step_size = jax.nn.softplus(matmul_high(projected[:, :DT_RANK], dt_proj) + dt_bias)
    input_mix = projected[:, DT_RANK:DT_RANK + STATE]
    output_mix = projected[:, DT_RANK + STATE:]
    decay_rate = -jnp.exp(a_log)
    scanned = span_scan(inner_act, step_size, input_mix, output_mix, decay_rate, first_flag)
    return (scanned + d_skip * inner_act) * jax.nn.silu(gate_z)

def attention_mix(qkv_all, allowed):
    count = qkv_all.shape[0]
    group_size = HEADS // KV_HEADS
    query_width = HEADS * HEAD_DIM
    kv_width = KV_HEADS * HEAD_DIM
    query_rows = qkv_all[:, :query_width].reshape(count, KV_HEADS, group_size, HEAD_DIM)
    key_rows = qkv_all[:, query_width:query_width + kv_width].reshape(count, KV_HEADS, HEAD_DIM)
    value_rows = qkv_all[:, query_width + kv_width:].reshape(count, KV_HEADS, HEAD_DIM)
    scale_factor_scores = HEAD_DIM ** (-0.5)
    attention_scores = lowered_backward(jnp.einsum('jzhx,kzx->zhjk', query_rows, key_rows, precision=highest_precision) * scale_factor_scores)
    masked = jnp.where(allowed[None, None], attention_scores, -1e+30)
    probabilities = low(jax.nn.softmax(masked, axis=-1))
    attended_values = jnp.einsum('lpho,ole->hlpe', probabilities, value_rows, precision=highest_precision)
    return attended_values.reshape(count, query_width)

def device_forward(params, hidden_in, length_row):
    norm_in, w_qkv, w_mamba_in, conv_weight, conv_bias, x_proj, dt_proj, dt_bias, a_log, d_skip, w_mamba_out, norm_attn, norm_ssm, w_mix_out, norm_ffn, w_gate, w_up, w_down = params
    seg_ids, first_flag, allowed = segment_info(length_row, hidden_in.shape[0])
    normed = low(rms_norm(hidden_in, norm_in))
    qkv_all = low(lowered_backward(matmul_high(normed, w_qkv)))
    attended_values = lowered_backward(attention_mix(qkv_all, allowed))
    mamba_pair = lowered_backward(matmul_high(normed, w_mamba_in))
    mamba_params = (conv_weight, conv_bias, x_proj, dt_proj, dt_bias, a_log, d_skip)
    mixer_out = low(mamba_core(mamba_pair[:, :INNER], mamba_pair[:, INNER:], mamba_params, seg_ids, first_flag))
    ssm_out = lowered_backward(matmul_high(mixer_out, w_mamba_out))
    mixed = low((rms_norm(attended_values, norm_attn) + rms_norm(ssm_out, norm_ssm)) * 0.5)
    middle = hidden_in + lowered_backward(matmul_high(mixed, w_mix_out))
    ffn_in = low(rms_norm(middle, norm_ffn))
    gate_val = lowered_backward(matmul_high(ffn_in, w_gate))
    up_val = lowered_backward(matmul_high(ffn_in, w_up))
    hidden_ffn = low(jax.nn.silu(gate_val) * up_val)
    return middle + lowered_backward(matmul_high(hidden_ffn, w_down))

def reference(tokens, cotangent, lengths, source_slot, norm_in, w_qkv, w_mamba_in, conv_weight, conv_bias, x_proj, dt_proj, dt_bias, a_log, d_skip, w_mamba_out, norm_attn, norm_ssm, w_mix_out, norm_ffn, w_gate, w_up, w_down):
    devices_all = N_REP * N_FSDP
    block_rows = TOK_DEV // N_FSDP
    device_ids = jnp.arange(devices_all, dtype=jnp.int32)
    replica_ids = device_ids // N_FSDP
    member_ids = device_ids % N_FSDP
    source_ids = source_slot // block_rows
    row_index = (replica_ids[:, None] * (N_FSDP * TOK_DEV) + source_ids * TOK_DEV + member_ids[:, None] * block_rows + source_slot % block_rows).astype(jnp.int32)
    flat_index = row_index.reshape(-1)
    x_layout = jnp.take(tokens.astype(jnp.float32), flat_index, axis=0)
    cot_layout = jnp.take(cotangent.astype(jnp.float32), flat_index, axis=0)
    per_step = math.gcd(devices_all, 16)
    steps_all = devices_all // per_step
    x_steps = x_layout.reshape(steps_all, per_step, TOK_DEV, D)
    cot_steps = cot_layout.reshape(steps_all, per_step, TOK_DEV, D)
    len_steps = lengths.reshape(steps_all, per_step, NSEQ)
    params = tuple((weight_arg.astype(jnp.float32) for weight_arg in (norm_in, w_qkv, w_mamba_in, conv_weight, conv_bias, x_proj, dt_proj, dt_bias, a_log, d_skip, w_mamba_out, norm_attn, norm_ssm, w_mix_out, norm_ffn, w_gate, w_up, w_down)))

    def group_step(grad_sum, batch):
        x_batch, cot_batch, len_batch = batch

        def forward(param_set, x_inputs):

            def single(one_x, one_len):
                return device_forward(param_set, one_x, one_len)
            return jax.vmap(single)(x_inputs, len_batch)
        outputs, pullback = jax.vjp(forward, params, x_batch)
        grad_params, grad_inputs = pullback(cot_batch)
        return (jax.tree.map(jnp.add, grad_sum, grad_params), (outputs, grad_inputs))
    zero_grads = jax.tree.map(jnp.zeros_like, params)
    grad_total, (outputs, grad_inputs) = lax.scan(group_step, zero_grads, (x_steps, cot_steps, len_steps))
    out_rows = jnp.zeros((TOKENS, D), jnp.float32).at[flat_index].set(outputs.reshape(-1, D))
    grad_rows = jnp.zeros((TOKENS, D), jnp.float32).at[flat_index].set(grad_inputs.reshape(-1, D))
    g_norm_in, g_qkv, g_mamba_in, g_conv_weight, g_conv_bias, g_x_proj, g_dt_proj, g_dt_bias, g_a_log, g_d_skip, g_mamba_out, g_norm_attn, g_norm_ssm, g_mix_out, g_norm_ffn, g_gate, g_up, g_down = grad_total
    return (out_rows.astype(jnp.bfloat16), grad_rows.astype(jnp.bfloat16), g_norm_in, g_qkv, g_mamba_in, g_conv_weight, g_conv_bias, g_x_proj, g_dt_proj, g_dt_bias, g_a_log, g_d_skip, g_mamba_out, g_norm_attn, g_norm_ssm, g_mix_out, g_norm_ffn, g_gate, g_up, g_down)
```

```python
import functools

import jax
import jax.numpy as jnp
from jax import lax
from jax.experimental import pallas as pl
from jax.experimental.pallas import tpu as pltpu
from jax.sharding import PartitionSpec as P

HEADS = 25
KV_HEADS = 5
HEAD_DIM = 64
INNER = 3200
STATE = 16
DT_RANK = 100
CONV = 4
WINDOW = 1024
LANES = 128
PACKS = 8
LOG2_E = 1.4426950408889634

epsilon = 1e-06
bf16 = jnp.bfloat16
f32 = jnp.float32


def dot(left, right, precision=None):
    return jnp.dot(left, right, precision=precision, preferred_element_type=f32)


def dot_right_t(left, right):
    return lax.dot_general(left, right, (((1,), (1,)), ((), ())), preferred_element_type=f32)


def dot_left_t(left, right):
    return lax.dot_general(left, right, (((0,), (0,)), ((), ())), preferred_element_type=f32)


def rms_norm(value_rows, gain):
    return (
        value_rows
        * lax.rsqrt(jnp.mean(value_rows * value_rows, axis=-1, keepdims=True) + epsilon)
        * gain
    )


def mix_branches(attended_values, ssm_out, norm_attn, norm_ssm):
    return (rms_norm(attended_values, norm_attn) + rms_norm(ssm_out, norm_ssm)) * 0.5


def swiglu(gate_val, up_val):
    return jax.nn.silu(gate_val) * up_val


def hbm_spec():
    return pl.BlockSpec(memory_space=pl.ANY)


def vmem_spec():
    return pl.BlockSpec(memory_space=pltpu.VMEM)


SMALL_COST = pl.CostEstimate(flops=0, bytes_accessed=10**4, transcendentals=0)


def send(src, dst, sems, axis, target):
    copy = pltpu.make_async_remote_copy(
        src_ref=src,
        dst_ref=dst,
        send_sem=sems[0],
        recv_sem=sems[1],
        device_id={axis: target},
        device_id_type=pl.DeviceIdType.MESH,
    )
    copy.start()
    return copy


def meet(axis, others):
    barrier = pltpu.get_barrier_semaphore()
    for other in others:
        pl.semaphore_signal(
            barrier, inc=1, device_id={axis: other}, device_id_type=pl.DeviceIdType.MESH
        )
    pl.semaphore_wait(barrier, len(others))


def rep_kernel(rep, counts, square, *refs):
    n_gather, n_sum, n_all, n_trade = counts
    chips = rep // 2
    refs = list(refs)

    def take(n):
        taken = refs[:n]
        del refs[:n]
        return taken

    gathers, sums, alls, trades = (take(n) for n in counts)
    gathered, summed, all_summed, traded = (take(n) for n in counts)
    reduced = sums + alls
    buffers = [take(3) for _ in reduced]
    totals = summed + take(n_all)
    local, far, near, direct = refs

    me = lax.axis_index("rep")
    core = lax.rem(me, 2)
    chip = (me - core) // 2
    partner = 2 * chip + 1 - core
    ahead = [lax.rem(chip + k, chips) for k in range(chips)]
    behind = [lax.rem(chip + chips - k, chips) for k in range(chips)]
    if square:
        along_x, along_y = chip + 1 - 2 * lax.rem(chip, 2), lax.rem(chip + 2, 4)
        first = along_x + core * (along_y - along_x)
        second = along_y + core * (along_x - along_y)
        across = 3 - chip
        linked = [2 * first + core, 2 * second + core]
    else:
        linked = [2 * ahead[k] + core for k in range(1, chips)]
    if n_trade:
        meet("rep", [lax.rem(me + k, rep) for k in range(1, rep)])
    else:
        meet("rep", linked + [partner])

    kept, sent = [], []

    def keep(src, dst):
        copy = pltpu.make_async_copy(src, dst, local.at[len(kept)])
        copy.start()
        kept.append(copy)

    def far_send(src, dst, slot, k, target):
        copy = send(src, dst, (far.at[0, slot, k], far.at[1, slot, k]), "rep", 2 * target + core)
        sent.append(copy)
        return copy

    def near_send(src, dst, slot, k):
        copy = send(src, dst, (near.at[0, slot, k], near.at[1, slot, k]), "rep", partner)
        sent.append(copy)
        return copy

    def start_gather(source, out, slot):
        if square:
            far_copies = [
                far_send(source, out.at[me], slot, 1, first),
                far_send(source, out.at[me], slot, 2, second),
            ]
        else:
            far_copies = [
                far_send(source, out.at[me], slot, k, ahead[k]) for k in range(1, chips)
            ]
        near_copies = [near_send(source, out.at[me], slot, 0)]
        keep(source, out.at[me])
        return out, slot, far_copies, near_copies

    def pass_on(states):
        if square:
            for out, slot, far_copies, near_copies in states:
                block = out.at[2 * first + core]
                far_copies[0].wait_recv()
                far_copies.append(far_send(block, block, slot, 3, second))
                near_copies.append(near_send(block, block, slot, 1))
            for out, slot, far_copies, near_copies in states:
                for k, source in ((2, second), (3, across)):
                    block = out.at[2 * source + core]
                    far_copies[k - 1].wait_recv()
                    near_copies.append(near_send(block, block, slot, k))
        else:
            for out, slot, far_copies, near_copies in states:
                for k in range(1, chips):
                    block = out.at[2 * behind[k] + core]
                    far_copies[k - 1].wait_recv()
                    near_copies.append(near_send(block, block, slot, k))
        for _, _, _, near_copies in states:
            for copy in near_copies:
                copy.wait_recv()

    dests = [chip, first, across, second] if square else ahead
    partner_dests = [chip, second, across, first] if square else ahead
    order = [1, 2, 3, 0] if square else [*range(1, chips), 0]
    crossing = []
    for i, source in enumerate(reduced):
        from_partner = buffers[i][1]
        crossing.append(
            {
                k: near_send(source.at[2 * partner_dests[k] + 1 - core], from_partner.at[k], i, k)
                for k in order
            }
        )
    states = [
        start_gather(source, gathered[i], len(reduced) + n_all + i)
        for i, source in enumerate(gathers)
    ]
    trading = []
    for i, source in enumerate(trades):
        keep(source.at[me], traded[i].at[me])
        for k in range(1, rep):
            target = lax.rem(me + k, rep)
            copy = send(
                source.at[target],
                traded[i].at[me],
                (direct.at[0, i, k], direct.at[1, i, k]),
                "rep",
                target,
            )
            trading.append(copy)

    def of_chip(i, k):
        crossing[i][k].wait_recv()
        own = reduced[i][2 * dests[k] + core]
        return own.astype(f32) + buffers[i][1][k].astype(f32)

    crossed = []
    for i in range(len(reduced)):
        low, _, arrived = buffers[i]
        copies = []
        for k in (1, 2) if square else range(1, chips):
            low[k - 1] = of_chip(i, k).astype(low.dtype)
            target = first if square else ahead[k]
            copies.append(far_send(low.at[k - 1], arrived.at[k - 1], i, k, target))
        crossed.append(copies)
    if square:
        for i in range(len(reduced)):
            low, _, arrived = buffers[i]
            value = of_chip(i, 3)
            crossed[i][1].wait_recv()
            low[2] = (value + arrived[1].astype(f32)).astype(low.dtype)
            crossed[i].append(far_send(low.at[2], arrived.at[2], i, 3, second))
    for i in range(len(reduced)):
        arrived = buffers[i][2]
        total = of_chip(i, 0)
        for k in (1, 3) if square else range(1, chips):
            crossed[i][k - 1].wait_recv()
            total = total + arrived[k - 1].astype(f32)
        totals[i][...] = total
        if i >= n_sum:
            states.append(start_gather(totals[i], all_summed[i - n_sum], n_all + i))
    pass_on(states)
    for copy in trading:
        copy.wait()
    for copy in sent:
        copy.wait_send()
    for copy in kept:
        copy.wait()


def rep_exchange(rep, collective_id, gathers=(), sums=(), alls=(), trades=()):
    chips = rep // 2
    square = rep == 8 and not alls
    counts = (len(gathers), len(sums), len(alls), len(trades))
    reduced = (*sums, *alls)
    out_shape = [jax.ShapeDtypeStruct((rep,) + x.shape, x.dtype) for x in gathers]
    out_shape += [jax.ShapeDtypeStruct(x.shape[1:], f32) for x in sums]
    out_shape += [jax.ShapeDtypeStruct(x.shape, f32) for x in alls]
    out_shape += [jax.ShapeDtypeStruct(x.shape, x.dtype) for x in trades]
    scratch = []
    for x in reduced:
        scratch += [
            pltpu.VMEM((n,) + x.shape[1:], x.dtype) for n in (chips - 1, chips, chips - 1)
        ]
    scratch += [pltpu.VMEM(x.shape[1:], f32) for x in alls]
    n_local = sum(counts) - len(sums) + 1
    n_slots = len(reduced) + len(alls) + len(gathers) + 1
    scratch += [
        pltpu.SemaphoreType.DMA((n_local,)),
        pltpu.SemaphoreType.DMA((2, n_slots, chips)),
        pltpu.SemaphoreType.DMA((2, n_slots, chips)),
        pltpu.SemaphoreType.DMA((2, len(trades) + 1, rep)),
    ]
    return pl.pallas_call(
        functools.partial(rep_kernel, rep, counts, square),
        out_shape=out_shape,
        in_specs=[vmem_spec()] * sum(counts),
        out_specs=[hbm_spec()] * len(gathers)
        + [vmem_spec()] * len(sums)
        + [hbm_spec()] * (len(alls) + len(trades)),
        scratch_shapes=scratch,
        compiler_params=pltpu.CompilerParams(
            collective_id=collective_id,
            has_side_effects=True,
            vmem_limit_bytes=40 * 1024 * 1024,
        ),
        cost_estimate=SMALL_COST,
    )(*gathers, *sums, *alls, *trades)


def line_kernel(count, n_gather, n_trade, *refs):
    n_in = n_gather + n_trade
    ins, outs, (local, remote) = refs[:n_in], refs[n_in : 2 * n_in], refs[2 * n_in :]
    me = lax.axis_index("fsdp")
    others = [lax.rem(me + k, count) for k in range(1, count)]
    meet("fsdp", others)
    copies = []
    for i in range(n_in):
        own = ins[i] if i < n_gather else ins[i].at[me]
        copy = pltpu.make_async_copy(own, outs[i].at[me], local.at[i])
        copy.start()
        copies.append(copy)
        for k, other in enumerate(others):
            block = ins[i] if i < n_gather else ins[i].at[other]
            sems = (remote.at[0, i, k], remote.at[1, i, k])
            copies.append(send(block, outs[i].at[me], sems, "fsdp", other))
    for copy in copies:
        copy.wait()


def line_exchange(count, collective_id, gathers=(), trades=()):
    arrays = (*gathers, *trades)
    out_shape = [jax.ShapeDtypeStruct((count,) + x.shape, x.dtype) for x in gathers]
    out_shape += [jax.ShapeDtypeStruct(x.shape, x.dtype) for x in trades]
    return pl.pallas_call(
        functools.partial(line_kernel, count, len(gathers), len(trades)),
        out_shape=out_shape,
        in_specs=[vmem_spec()] * len(arrays),
        out_specs=[hbm_spec()] * len(arrays),
        scratch_shapes=[
            pltpu.SemaphoreType.DMA((len(arrays),)),
            pltpu.SemaphoreType.DMA((2, len(arrays), count)),
        ],
        compiler_params=pltpu.CompilerParams(collective_id=collective_id, has_side_effects=True),
        cost_estimate=SMALL_COST,
    )(*arrays)


def pair_kernel(own_ref, out_ref, local, send_sem, recv_sem):
    me = lax.axis_index("rep")
    core = lax.rem(me, 2)
    partner = me + 1 - 2 * core
    meet("rep", [partner])
    keep = pltpu.make_async_copy(own_ref, out_ref.at[:, core], local)
    keep.start()
    copy = send(own_ref, out_ref.at[:, core], (send_sem, recv_sem), "rep", partner)
    copy.wait()
    keep.wait()


def pair_gather(collective_id, own):
    groups, rows, width = own.shape
    return pl.pallas_call(
        pair_kernel,
        out_shape=jax.ShapeDtypeStruct((groups, 2, rows, width), own.dtype),
        in_specs=[vmem_spec()],
        out_specs=hbm_spec(),
        scratch_shapes=[pltpu.SemaphoreType.DMA] * 3,
        compiler_params=pltpu.CompilerParams(collective_id=collective_id, has_side_effects=True),
        cost_estimate=SMALL_COST,
    )(own)


def windows(width, pieces, start, step, rest):
    wide = min(-(-(rest + LANES - 1) // LANES) * LANES, width)
    me = lax.axis_index("rep")
    for i in range(pieces):
        at = start + i * step + me * rest
        aligned = jnp.minimum((at // LANES) * LANES, (width - wide) // LANES * LANES)
        yield pl.multiple_of(aligned, LANES), at - aligned, wide


def up16(size):
    return -(-size // 16) * 16


def copy_parts(rep, fsdp, source, out, place, start, total):
    rest = total // (rep * fsdp)
    rows = source.shape[0]
    for aligned, shift, wide in windows(source.shape[1], fsdp, start, rep * rest, rest):
        value = source[:, pl.ds(aligned, wide)].astype(f32)
        value = pltpu.roll(value, lax.rem(wide - shift, wide), 1)[:, :rest]
        if up16(rest) > rest:
            value = jnp.concatenate([value, jnp.zeros((rows, up16(rest) - rest), f32)], axis=1)
        out[:, place : place + up16(rest)] = value.astype(bf16)
        place += up16(rest)


def part_in_kernel(rep, fsdp, spots, qkv_ref, min_ref, out_ref):
    _, qkv_at, gate_at = spots
    rows, qkv_width = qkv_ref.shape
    qkv_part = qkv_width // rep
    out_ref[...] = jnp.zeros_like(out_ref)
    copy_parts(rep, fsdp, min_ref, out_ref, 0, 0, INNER)
    copy_parts(rep, fsdp, min_ref, out_ref, gate_at, INNER, INNER)
    value = qkv_ref[...].astype(f32)
    padded = -(-qkv_width // LANES) * LANES
    value = jnp.concatenate([value, jnp.zeros((rows, padded - qkv_width), f32)], axis=1)
    shift = padded - lax.axis_index("rep") * qkv_part
    value = pltpu.roll(value, lax.rem(shift, padded), 1)
    out_ref[:, qkv_at : qkv_at + qkv_part] = value[:, :qkv_part].astype(bf16)


def part_gate_up_kernel(rep, fsdp, gate_ref, up_ref, out_ref):
    copy_parts(rep, fsdp, gate_ref, out_ref, 0, 0, gate_ref.shape[1])
    copy_parts(rep, fsdp, up_ref, out_ref, out_ref.shape[1] // 2, 0, up_ref.shape[1])


def by_rows(kernel, sources, width):
    rows = sources[0].shape[0]
    block = 80 if rows % 80 == 0 else rows
    return pl.pallas_call(
        kernel,
        grid=(rows // block,),
        in_specs=[pl.BlockSpec((block, x.shape[1]), lambda i: (i, 0)) for x in sources],
        out_specs=pl.BlockSpec((block, width), lambda i: (i, 0)),
        out_shape=jax.ShapeDtypeStruct((rows, width), bf16),
        compiler_params=pltpu.CompilerParams(vmem_limit_bytes=40 * 1024 * 1024),
        cost_estimate=SMALL_COST,
    )(*sources)


def join_kernel(rep, layout, *refs):
    sources, outs = refs[: len(refs) - len(layout)], refs[len(refs) - len(layout) :]
    for out, entries in zip(outs, layout):
        for index, first, rest, place, pieces in entries:
            for i in range(pieces):
                start = first + i * up16(rest)
                for r in range(rep):
                    at = place + (i * rep + r) * rest
                    piece = sources[index][r, :, start : start + rest]
                    out[:, at : at + rest] = piece.astype(f32)


def join_rows_kernel(rep, pieces, rest, *refs):
    for source, out, rows in zip(refs[: len(rest)], refs[len(rest) :], rest):
        for i in range(pieces):
            for r in range(rep):
                at, start = (i * rep + r) * rows, i * up16(rows)
                out[at : at + rows, :] = source[r, start : start + rows, :].astype(f32)


def join_rows(rep, sources, totals, pieces=1):
    width = sources[0].shape[2]
    block = min(2 * LANES, width)
    return pl.pallas_call(
        functools.partial(join_rows_kernel, rep, pieces, tuple(n // rep // pieces for n in totals)),
        grid=(pl.cdiv(width, block),),
        in_specs=[
            pl.BlockSpec((rep, x.shape[1], block), lambda i: (0, 0, i)) for x in sources
        ],
        out_specs=[pl.BlockSpec((n, block), lambda i: (0, i)) for n in totals],
        out_shape=[jax.ShapeDtypeStruct((n, width), f32) for n in totals],
        compiler_params=pltpu.CompilerParams(vmem_limit_bytes=40 * 1024 * 1024),
        cost_estimate=SMALL_COST,
    )(*sources)


def join_columns(rep, sources, widths, layout):
    rows = sources[0].shape[1]
    block = next(n for n in (80, 40, 64, rows) if rows % n == 0)
    return pl.pallas_call(
        functools.partial(join_kernel, rep, layout),
        grid=(rows // block,),
        in_specs=[
            pl.BlockSpec((rep, block, x.shape[2]), lambda i: (0, i, 0)) for x in sources
        ],
        out_specs=[pl.BlockSpec((block, width), lambda i: (i, 0)) for width in widths],
        out_shape=[jax.ShapeDtypeStruct((rows, width), f32) for width in widths],
        compiler_params=pltpu.CompilerParams(vmem_limit_bytes=48 * 1024 * 1024),
        cost_estimate=SMALL_COST,
    )(*sources)


def spread_maps(maps_ref, wide_ref):
    count, packs, columns = maps_ref.shape

    def spread(i, _):
        for u in range(2):
            t = 2 * i + u
            maps = maps_ref[t]
            for n in range(columns):
                wide_ref[n, t] = jnp.broadcast_to(maps[:, n : n + 1], (packs, LANES))
        return 0

    lax.fori_loop(0, count // 2, spread, 0)


def scan_kernel(decay_step_ref, input_ref, maps_ref, rate_ref, out_ref, wide_ref):
    count, packs, _ = decay_step_ref.shape

    @pl.when(pl.program_id(1) == 0)
    def _():
        spread_maps(maps_ref, wide_ref)

    def step(i, states):
        for u in range(2):
            t = 2 * i + u
            decay_step, inputs = decay_step_ref[t], input_ref[t]
            out = jnp.zeros((packs, LANES), f32)
            new_states = []
            for n in range(STATE):
                decay = jnp.exp2(decay_step * rate_ref[n : n + 1, :])
                state = decay * states[n] + wide_ref[n, t] * inputs
                out = out + state * wide_ref[STATE + n, t]
                new_states.append(state)
            out_ref[t] = out
            states = tuple(new_states)
        return states

    lax.fori_loop(0, count // 2, step, (jnp.zeros((packs, LANES), f32),) * STATE)


def scan_forward(decay_step, inputs, maps, rate2):
    count, packs, channels = inputs.shape
    wide = pl.BlockSpec((count, PACKS, LANES), lambda g, i: (0, g, i))
    return pl.pallas_call(
        scan_kernel,
        grid=(packs // PACKS, pl.cdiv(channels, LANES)),
        in_specs=[
            wide,
            wide,
            pl.BlockSpec((count, PACKS, 2 * STATE), lambda g, i: (0, g, 0)),
            pl.BlockSpec((STATE, LANES), lambda g, i: (0, i)),
        ],
        out_specs=wide,
        out_shape=jax.ShapeDtypeStruct(inputs.shape, f32),
        scratch_shapes=[pltpu.VMEM((2 * STATE, count, PACKS, LANES), f32)],
        compiler_params=pltpu.CompilerParams(vmem_limit_bytes=40 * 1024 * 1024),
        cost_estimate=SMALL_COST,
    )(decay_step, inputs, maps, rate2)


def scan_back_kernel(
    channels,
    decay_step_ref,
    step_ref,
    input_ref,
    maps_ref,
    grad_ref,
    rate2_ref,
    rate_ref,
    grad_input_ref,
    grad_step_ref,
    grad_rate_ref,
    grad_maps_ref,
    states_ref,
    in_sum_ref,
    out_sum_ref,
    wide_ref,
):
    count, packs, _ = decay_step_ref.shape
    at = pl.program_id(1)
    valid = lax.broadcasted_iota(jnp.int32, (packs, LANES), 1) < channels - at * LANES
    valid_row = valid[:1]
    rate2 = [jnp.where(valid_row, rate2_ref[n : n + 1, :], 0.0) for n in range(STATE)]
    rate = [jnp.where(valid_row, rate_ref[n : n + 1, :], 0.0) for n in range(STATE)]

    @pl.when(at == 0)
    def _():
        spread_maps(maps_ref, wide_ref)
        in_sum_ref[...] = jnp.zeros_like(in_sum_ref)
        out_sum_ref[...] = jnp.zeros_like(out_sum_ref)

    def forward(i, states):
        for u in range(2):
            t = 2 * i + u
            decay_step = jnp.where(valid, decay_step_ref[t], 0.0)
            inputs = jnp.where(valid, input_ref[t], 0.0)
            new_states = []
            for n in range(STATE):
                state = jnp.exp2(decay_step * rate2[n]) * states[n] + wide_ref[n, t] * inputs
                states_ref[n, t] = state
                new_states.append(state)
            states = tuple(new_states)
        return states

    zero = jnp.zeros((packs, LANES), f32)
    lax.fori_loop(0, count // 2, forward, (zero,) * STATE)

    def backward(back_t, carried):
        grad_states, grad_rates = carried
        t = count - 1 - back_t
        decay_step = jnp.where(valid, decay_step_ref[t], 0.0)
        step = jnp.where(valid, step_ref[t], 0.0)
        inputs = jnp.where(valid, input_ref[t], 0.0)
        grad = jnp.where(valid, grad_ref[t], 0.0)
        grad_input, grad_step = zero, zero
        new_states, new_rates = [], []
        for n in range(STATE):
            state, in_map = states_ref[n, t], wide_ref[n, t]
            grad_state = grad * wide_ref[STATE + n, t] + grad_states[n]
            out_sum_ref[n, t] += grad * state
            in_sum_ref[n, t] += grad_state * inputs
            grad_input = grad_input + grad_state * in_map
            through = grad_state * (state - in_map * inputs)
            grad_step = grad_step + through * rate[n]
            new_rates.append(grad_rates[n] + through * step)
            new_states.append(jnp.exp2(decay_step * rate2[n]) * grad_state)
        grad_input_ref[t] = grad_input
        grad_step_ref[t] = grad_step
        return (tuple(new_states), tuple(new_rates))

    _, grad_rates = lax.fori_loop(0, count, backward, ((zero,) * STATE, (zero,) * STATE))
    for n in range(STATE):
        grad_rate_ref[n : n + 1, :] = jnp.sum(grad_rates[n], axis=0, keepdims=True)

    @pl.when(at == pl.num_programs(1) - 1)
    def _():
        column = lax.broadcasted_iota(jnp.int32, (LANES, LANES), 1)
        total = jnp.zeros((count * packs, LANES), f32)
        for n in range(STATE):
            for sums, place in ((in_sum_ref, n), (out_sum_ref, STATE + n)):
                total = total + jnp.dot(
                    sums[n].reshape(count * packs, LANES).astype(bf16),
                    (column == place).astype(bf16),
                    preferred_element_type=f32,
                )
        grad_maps_ref[...] = total.reshape(count, packs, LANES)


def scan_backward(decay_step, step, inputs, maps, grad, rate2, rate):
    count, packs, channels = inputs.shape
    groups = packs // PACKS
    wide = pl.BlockSpec((count, PACKS, LANES), lambda g, i: (0, g, i))
    row = pl.BlockSpec((STATE, LANES), lambda g, i: (0, i))
    scratch = pltpu.VMEM((STATE, count, PACKS, LANES), f32)
    grad_inputs, grad_step, grad_rate, grad_maps = pl.pallas_call(
        functools.partial(scan_back_kernel, channels),
        grid=(groups, pl.cdiv(channels, LANES)),
        in_specs=[
            wide,
            wide,
            wide,
            pl.BlockSpec((count, PACKS, 2 * STATE), lambda g, i: (0, g, 0)),
            wide,
            row,
            row,
        ],
        out_specs=[
            wide,
            wide,
            pl.BlockSpec((STATE, LANES), lambda g, i: (g, i)),
            pl.BlockSpec((count, PACKS, LANES), lambda g, i: (0, g, 0)),
        ],
        out_shape=[
            jax.ShapeDtypeStruct(inputs.shape, f32),
            jax.ShapeDtypeStruct(inputs.shape, f32),
            jax.ShapeDtypeStruct((groups * STATE, channels), f32),
            jax.ShapeDtypeStruct((count, packs, LANES), f32),
        ],
        scratch_shapes=[
            scratch,
            scratch,
            scratch,
            pltpu.VMEM((2 * STATE, count, PACKS, LANES), f32),
        ],
        compiler_params=pltpu.CompilerParams(vmem_limit_bytes=58 * 1024 * 1024),
        cost_estimate=SMALL_COST,
    )(decay_step, step, inputs, maps, grad, rate2, rate)
    grad_rate = jnp.sum(grad_rate.reshape(groups, STATE, channels), axis=0)
    return grad_inputs, grad_step, grad_rate, grad_maps.reshape(count * packs, LANES)


def split_heads(qkv_low):
    count = qkv_low.shape[0]
    group_size = HEADS // KV_HEADS
    query_width = HEADS * HEAD_DIM
    kv_width = KV_HEADS * HEAD_DIM
    query_rows = qkv_low[:, :query_width].reshape(count, KV_HEADS, group_size, HEAD_DIM)
    key_rows = qkv_low[:, query_width : query_width + kv_width].reshape(count, KV_HEADS, HEAD_DIM)
    value_rows = qkv_low[:, query_width + kv_width :].reshape(count, KV_HEADS, HEAD_DIM)
    return (query_rows, key_rows, value_rows)


def masked_scores(query_rows, key_rows, allowed):
    attention_scores = jnp.einsum(
        "jzhx,kzx->zhjk", query_rows, key_rows, preferred_element_type=f32
    ) * HEAD_DIM ** (-0.5)
    return jnp.where(allowed[None, None], attention_scores, -1e30)


def attention_forward(qkv_low, allowed):
    count = qkv_low.shape[0]
    query_rows, key_rows, value_rows = split_heads(qkv_low)
    attention_scores = masked_scores(query_rows, key_rows, allowed)
    row_max = jnp.max(attention_scores, axis=-1, keepdims=True)
    weights_exp = jnp.exp(attention_scores - row_max)
    row_total = jnp.sum(weights_exp, axis=-1, keepdims=True)
    lowered_probabilities = (weights_exp / row_total).astype(bf16)
    attended_values = jnp.einsum(
        "lpho,ole->hlpe", lowered_probabilities, value_rows, preferred_element_type=f32
    )
    return (attended_values.reshape(count, HEADS * HEAD_DIM), row_max + jnp.log(row_total))


def attention_backward(qkv_low, grad_low, log_total, allowed):
    count = qkv_low.shape[0]
    query_rows, key_rows, value_rows = split_heads(qkv_low)
    probabilities = jnp.exp(masked_scores(query_rows, key_rows, allowed) - log_total)
    head_gradient = grad_low.reshape(count, KV_HEADS, HEADS // KV_HEADS, HEAD_DIM)
    grad_probs = jnp.einsum(
        "jzhx,kzx->zhjk", head_gradient, value_rows, preferred_element_type=f32
    )
    score_gradient = (
        probabilities * (grad_probs - jnp.sum(grad_probs * probabilities, axis=-1, keepdims=True))
    ).astype(bf16)
    scale_factor_scores = HEAD_DIM ** (-0.5)
    grad_queries = (
        jnp.einsum("lpho,ole->hlpe", score_gradient, key_rows, preferred_element_type=f32)
        * scale_factor_scores
    )
    grad_keys = (
        jnp.einsum("wniv,iwne->vwe", score_gradient, query_rows, preferred_element_type=f32)
        * scale_factor_scores
    )
    grad_values = jnp.einsum(
        "wniv,iwne->vwe", probabilities.astype(bf16), head_gradient, preferred_element_type=f32
    )
    return jnp.concatenate(
        [
            grad_queries.reshape(count, -1),
            grad_keys.reshape(count, -1),
            grad_values.reshape(count, -1),
        ],
        axis=1,
    )


def tied(value, *others):
    return lax.optimization_barrier((value,) + others)[0]


def silu_and_slope(value):
    gate = jax.nn.sigmoid(value)
    return value * gate, gate * (1.0 + value * (1.0 - gate))


def shift_down(rows, amount):
    return jnp.concatenate([jnp.zeros((amount,) + rows.shape[1:], rows.dtype), rows[:-amount]], 0)


def shift_up(rows, amount):
    return jnp.concatenate([rows[amount:], jnp.zeros((amount,) + rows.shape[1:], rows.dtype)], 0)


def per_device(
    rep,
    fsdp,
    tokens,
    cotangent,
    lengths,
    source_slot,
    norm_in,
    w_qkv,
    w_mamba_in,
    conv_weight,
    conv_bias,
    x_proj,
    dt_proj,
    dt_bias,
    a_log,
    d_skip,
    w_mamba_out,
    norm_attn,
    norm_ssm,
    w_mix_out,
    norm_ffn,
    w_gate,
    w_up,
    w_down,
):
    count, width = tokens.shape
    block_rows = count // fsdp
    piece, ff_piece = INNER // (rep * fsdp), w_gate.shape[1] // (rep * fsdp)
    channels, ff_part = fsdp * up16(piece), fsdp * up16(ff_piece)
    qkv_part = w_qkv.shape[1] // rep
    group = rep * count
    high = lax.Precision.HIGH
    me, line = lax.axis_index("rep"), lax.axis_index("fsdp")

    def my_part(value, axis):
        rest = value.shape[axis] // (rep * fsdp)
        spare = [(0, up16(rest) - rest if i == axis else 0) for i in range(value.ndim)]
        return jnp.concatenate(
            [
                jnp.pad(lax.dynamic_slice_in_dim(value, (i * rep + me) * rest, rest, axis), spare)
                for i in range(fsdp)
            ],
            axis=axis,
        )

    def my_rows(value):
        rest = value.shape[0] // rep
        part = lax.dynamic_slice_in_dim(value, me * rest, rest, 0)
        return jnp.pad(part, ((0, up16(rest) - rest), (0, 0)))

    def line_gather(value):
        return lax.all_gather(value, "fsdp", axis=0, tiled=True)

    def line_scatter(value):
        return lax.psum_scatter(value, "fsdp", scatter_dimension=0, tiled=True)

    def swapped(rows):
        lead = count if rows.shape[0] == count else rep
        return rows.transpose(1, 0, 2).reshape(group, rows.shape[2])

    early_width = -(-(qkv_part + channels) // LANES) * LANES
    gate_at = -(-(channels + qkv_part) // LANES) * LANES
    in_width = -(-(gate_at + channels) // LANES) * LANES
    part_in = by_rows(
        functools.partial(part_in_kernel, rep, fsdp, (0, channels, gate_at)),
        (w_qkv, w_mamba_in),
        in_width,
    )
    full_in = line_gather(part_in)
    half = w_mix_out.shape[0] // 2
    part_mix = lax.dynamic_slice_in_dim(w_mix_out, lax.rem(me, 2) * half, half, 0)
    part_mout, part_down = my_rows(w_mamba_out), my_rows(w_down)

    received, cot_received = line_exchange(
        fsdp,
        0,
        trades=(
            tied(tokens, part_in).reshape(fsdp, block_rows, width),
            cotangent.reshape(fsdp, block_rows, width),
        ),
    )
    w_gate, w_up, part_mout, part_mix, part_down, received = lax.optimization_barrier(
        (w_gate, w_up, part_mout, part_mix, part_down, received)
    )
    full_mout, half_mix = line_gather(part_mout), line_gather(part_mix)
    part_gate_up = by_rows(
        functools.partial(part_gate_up_kernel, rep, fsdp), (w_gate, w_up), 2 * ff_part
    )
    full_gate_up, full_down = line_gather(part_gate_up), line_gather(part_down)
    slots = source_slot[0]
    picks = (slots[:, None] == jnp.arange(count, dtype=jnp.int32)[None, :]).astype(bf16)
    hidden_in = dot(picks, received.reshape(count, width))
    cot_rows = dot(picks, cot_received.reshape(count, width))
    cot_low = cot_rows.astype(bf16)

    ends = jnp.cumsum(lengths[0], dtype=jnp.int32)
    positions = jnp.arange(count, dtype=jnp.int32)
    passed = positions[:, None] >= ends[None, :-1]
    seg_ids = jnp.sum(passed.astype(jnp.int32), axis=1)
    in_seq = positions - jnp.max(jnp.where(passed, ends[None, :-1], 0), axis=1)
    distance = positions[:, None] - positions[None, :]
    allowed = (seg_ids[:, None] == seg_ids[None, :]) & (distance >= 0) & (distance < WINDOW)

    normed, norm_in_pull = jax.vjp(rms_norm, hidden_in, norm_in)
    marks = jnp.broadcast_to(in_seq[:, None].astype(bf16), (count, 64))
    normed_marked = jnp.concatenate([normed.astype(bf16), marks], axis=1)
    normed_sent, cot_all = rep_exchange(rep, 1, gathers=(normed_marked, cot_low))
    cot_all = cot_all.reshape(group, width)
    normed_all = normed_sent[:, :, :width].reshape(group, width)
    in_seq_all = normed_sent[:, :, width].astype(f32).T.reshape(group, 1)

    in_out = dot(swapped(normed_all.reshape(rep, count, width)), full_in)
    xs, gate_z = in_out[:, :channels], in_out[:, gate_at : gate_at + channels]
    qkv_sent = in_out[:, channels : channels + qkv_part].astype(bf16)
    qkv_sent = swapped(qkv_sent.reshape(count, rep, qkv_part))

    conv_w, conv_b = my_part(conv_weight, 1), my_part(conv_bias, 0)
    part_x_proj, part_dt_proj = my_part(x_proj, 0), my_part(dt_proj, 1)
    part_dt_bias, part_skip = my_part(dt_bias, 0), my_part(d_skip, 0)
    rate = -jnp.exp(my_part(a_log, 1))
    rate2 = rate * LOG2_E
    conv_sum = xs * conv_w[CONV - 1] + conv_b
    for k in range(1, CONV):
        earlier = jnp.where(in_seq_all >= k, shift_down(xs, k * rep), 0.0)
        conv_sum = conv_sum + earlier * conv_w[CONV - 1 - k]
    act, act_slope = silu_and_slope(conv_sum)
    proj_sent = dot(act, part_x_proj, high).reshape(count, rep, -1).transpose(1, 0, 2)
    proj, qkv_back = rep_exchange(
        rep, 2, alls=(proj_sent,), trades=(qkv_sent.reshape(rep, count, qkv_part),)
    )
    qkv_low = qkv_back.transpose(1, 0, 2).reshape(count, rep * qkv_part)
    proj = proj.transpose(1, 0, 2)
    dt_in = proj.reshape(group, -1)[:, :DT_RANK]
    maps = proj[:, :, DT_RANK:]
    dt_sum = dot(dt_in, part_dt_proj, high) + part_dt_bias
    step = jax.nn.softplus(dt_sum)
    decay_step = jnp.where(in_seq_all == 0.0, 1e30, step)
    inputs = step * act
    cube = (count, rep, channels)
    scanned = scan_forward(decay_step.reshape(cube), inputs.reshape(cube), maps, rate2)
    scanned = scanned.reshape(group, channels)
    silu_z, z_slope = silu_and_slope(gate_z)
    before_gate = scanned + part_skip * act
    mixer_low = swapped((before_gate * silu_z).astype(bf16).reshape(cube))
    ssm_part = dot(mixer_low, full_mout).astype(bf16).reshape(rep, count, width)
    (ssm_out,) = rep_exchange(rep, 3, sums=(ssm_part,))

    attended_values, log_total = attention_forward(qkv_low, allowed)
    half_mix, qkv_low = lax.optimization_barrier((half_mix, qkv_low))
    full_mix = pair_gather(9, half_mix.reshape(fsdp, half, width)).reshape(width, width)
    mixed, mix_pull = jax.vjp(mix_branches, attended_values, ssm_out, norm_attn, norm_ssm)
    mixed_low = mixed.astype(bf16)
    middle = hidden_in + dot(mixed_low, full_mix)
    ffn_in, ffn_pull = jax.vjp(rms_norm, middle, norm_ffn)
    ffn_all, mixed_all = rep_exchange(rep, 4, gathers=(ffn_in.astype(bf16), mixed_low))
    ffn_all, mixed_all = ffn_all.reshape(group, width), mixed_all.reshape(group, width)

    gate_up = dot(ffn_all, full_gate_up)
    hidden, swiglu_pull = jax.vjp(swiglu, gate_up[:, :ff_part], gate_up[:, ff_part:])
    hidden_low = hidden.astype(bf16)
    grad_hidden = dot_right_t(cot_all, full_down)
    grad_gate_up = jnp.concatenate(swiglu_pull(grad_hidden), axis=1).astype(bf16)
    ffn_sent = dot_right_t(grad_gate_up, full_gate_up).astype(bf16).reshape(rep, count, width)
    down_sent = dot(hidden_low, full_down).astype(bf16).reshape(rep, count, width)
    grad_ffn, down_out = rep_exchange(rep, 5, sums=(ffn_sent, down_sent))
    result = middle + down_out
    part_gate_up = dot_left_t(ffn_all, grad_gate_up).astype(bf16)
    part_down = dot_left_t(hidden_low, cot_all).astype(bf16)
    grad_ffn = tied(grad_ffn, part_gate_up, part_down)
    own_gate_up, own_down = line_scatter(part_gate_up), line_scatter(part_down)

    grad_middle_norm, grad_norm_ffn = ffn_pull(grad_ffn)
    grad_middle = cot_rows + grad_middle_norm
    middle_low = grad_middle.astype(bf16)
    grad_mixed = dot_right_t(middle_low, full_mix)
    grad_attended, grad_ssm, grad_norm_attn, grad_norm_ssm = mix_pull(grad_mixed)
    middle_sent = middle_low.reshape(count, rep, -1).transpose(1, 0, 2)
    qkv_grad = attention_backward(qkv_low, grad_attended.astype(bf16), log_total, allowed)
    qkv_grad = qkv_grad.astype(bf16).reshape(count, rep, -1).transpose(1, 0, 2)
    ssm_all, middle_cols, qkv_cols = rep_exchange(
        rep, 6, gathers=(grad_ssm.astype(bf16),), trades=(middle_sent, qkv_grad)
    )
    qkv_cols = qkv_cols.reshape(group, qkv_part)
    ssm_all = ssm_all.reshape(group, width)
    grad_mixer = dot_right_t(ssm_all, full_mout).reshape(rep, count, channels)
    grad_mixer = swapped(grad_mixer)
    part_mout = dot_left_t(mixer_low, ssm_all).astype(bf16)
    part_mix = dot_left_t(mixed_all, middle_cols.reshape(group, -1)).astype(bf16)

    grad_z = (grad_mixer * before_gate * z_slope).astype(bf16)
    grad_z = swapped(grad_z.reshape(cube))
    spare = early_width - qkv_part - channels
    early_grad = jnp.concatenate([qkv_cols, jnp.zeros((group, spare), bf16), grad_z], axis=1)
    part_early = dot_left_t(normed_all, early_grad).astype(bf16)
    grad_mixer = tied(grad_mixer, part_mout, part_mix, part_early)
    own_mout, own_mix = line_scatter(part_mout), line_scatter(part_mix)
    own_early = line_scatter(part_early)
    grad_before = grad_mixer * silu_z
    grad_skip = jnp.sum(grad_before * act, axis=0)
    grad_inputs, grad_step, grad_rate, grad_maps = scan_backward(
        *(item.reshape(cube) for item in (decay_step, step, inputs)),
        maps,
        grad_before.reshape(cube),
        rate2,
        rate,
    )
    grad_inputs = grad_inputs.reshape(group, channels)
    grad_step = grad_step.reshape(group, channels)
    grad_a_log = grad_rate * rate
    grad_step = grad_step + grad_inputs * act
    grad_dt = grad_step * jax.nn.sigmoid(dt_sum)
    grad_dt_bias = jnp.sum(grad_dt, axis=0)
    grad_dt_proj = dot_left_t(dt_in, grad_dt)
    proj_sent = jnp.concatenate(
        [dot_right_t(grad_dt, part_dt_proj), grad_maps[:, : 2 * STATE]], axis=1
    )
    proj_sent = proj_sent.reshape(count, rep, -1).transpose(1, 0, 2)
    (grad_proj,) = rep_exchange(rep, 7, alls=(proj_sent,))
    grad_proj = swapped(grad_proj)
    grad_x_proj = dot_left_t(act, grad_proj)
    grad_act = grad_before * part_skip + grad_inputs * step + dot_right_t(grad_proj, part_x_proj)
    grad_conv = grad_act * act_slope
    grad_conv_b = jnp.sum(grad_conv, axis=0)
    grad_conv_w = [jnp.sum(grad_conv * xs, axis=0)]
    grad_xs = grad_conv * conv_w[CONV - 1]
    for k in range(1, CONV):
        reached = jnp.where(in_seq_all >= k, grad_conv, 0.0)
        grad_conv_w.insert(0, jnp.sum(reached * shift_down(xs, k * rep), axis=0))
        grad_xs = grad_xs + shift_up(reached, k * rep) * conv_w[CONV - 1 - k]
    small = jnp.concatenate(
        [jnp.stack(grad_conv_w), grad_conv_b[None], grad_dt_bias[None], grad_skip[None]]
        + [grad_a_log, grad_dt_proj],
        axis=0,
    )
    small = jnp.pad(small, ((0, up16(small.shape[0]) - small.shape[0]), (0, 0))).astype(bf16)
    grad_xs = swapped(grad_xs.astype(bf16).reshape(cube))
    gap = jnp.zeros((group, gate_at - channels - qkv_part), bf16)
    end = jnp.zeros((group, in_width - gate_at - channels), bf16)
    in_grad = jnp.concatenate([grad_xs, qkv_cols, gap, grad_z, end], axis=1)
    normed_part = dot_right_t(in_grad, full_in).astype(bf16).reshape(rep, count, width)
    own_late = line_scatter(dot_left_t(normed_all, grad_xs).astype(bf16))
    (grad_normed,) = rep_exchange(rep, 8, sums=(normed_part,))
    grad_hidden_norm, grad_norm_in = norm_in_pull(grad_normed)
    grad_hidden_in = grad_middle + grad_hidden_norm

    def given_back(rows):
        return dot_left_t(picks, rows.astype(bf16)).astype(bf16).reshape(fsdp, block_rows, width)

    gains = jnp.stack([grad_norm_in, grad_norm_attn, grad_norm_ssm, grad_norm_ffn])
    gains = jnp.concatenate([gains, jnp.zeros((4, width), f32)], axis=0)
    gains, small, x_small, mixed_out, grad_tokens = line_exchange(
        fsdp,
        10,
        gathers=(gains, small, grad_x_proj.astype(bf16)),
        trades=(given_back(result), given_back(grad_hidden_in)),
    )
    gains, small, x_small = (
        jnp.sum(item.astype(f32), axis=0) for item in (gains, small, x_small)
    )

    own_gate_up = tied(own_gate_up, mixed_out)
    all_down, all_gate_up, all_mout, all_mix, all_early = rep_exchange(
        rep, 11, gathers=(own_down, own_gate_up, own_mout, own_mix, own_early)
    )
    own_late = tied(own_late, all_down)
    all_late, small, x_small, gains = rep_exchange(
        rep, 12, gathers=(own_late, small, x_small, gains)
    )
    gains = jnp.sum(gains, axis=0)
    sum_gate, sum_up = join_columns(
        rep,
        (all_gate_up,),
        (w_gate.shape[1], w_up.shape[1]),
        (((0, 0, ff_piece, 0, fsdp),), ((0, ff_part, ff_piece, 0, fsdp),)),
    )
    sum_mamba_in, sum_qkv, sum_mix = join_columns(
        rep,
        (all_late, all_early, all_mix),
        (w_mamba_in.shape[1], w_qkv.shape[1], width),
        (
            ((0, 0, piece, 0, fsdp), (1, early_width - channels, piece, INNER, fsdp)),
            ((1, 0, qkv_part, 0, 1),),
            ((2, 0, width // rep, 0, 1),),
        ),
    )
    (sum_down,) = join_rows(rep, (all_down,), (w_down.shape[0],))
    (sum_mout,) = join_rows(rep, (all_mout,), (w_mamba_out.shape[0],))

    (sum_x_proj,) = join_rows(rep, (x_small,), (x_proj.shape[0],), fsdp)
    (small,) = join_columns(rep, (small,), (INNER,), (((0, 0, piece, 0, fsdp),),))
    ends = [CONV, CONV + 1, CONV + 2, CONV + 3, CONV + 3 + STATE, CONV + 3 + STATE + DT_RANK]
    return (
        mixed_out.reshape(count, width),
        grad_tokens.reshape(count, width),
        gains[0],
        sum_qkv,
        sum_mamba_in,
        small[: ends[0]],
        small[ends[0]],
        sum_x_proj,
        small[ends[4] : ends[5]],
        small[ends[1]],
        small[ends[3] : ends[4]],
        small[ends[2]],
        sum_mout,
        gains[1],
        gains[2],
        sum_mix,
        gains[3],
        sum_gate,
        sum_up,
        sum_down,
    )


def solution(mesh):
    rows = P(("rep", "fsdp"), None)
    cut = P("fsdp", None)
    whole = P()
    return jax.shard_map(
        functools.partial(per_device, mesh.shape["rep"], mesh.shape["fsdp"]),
        mesh=mesh,
        in_specs=(rows,) * 4
        + (whole, cut, cut)
        + (whole,) * 7
        + (cut, whole, whole, cut, whole, cut, cut, cut),
        out_specs=(rows, rows, whole, cut, cut)
        + (whole,) * 7
        + (cut, whole, whole, cut, whole, cut, cut, cut),
        check_vma=False,
    )
```

```python
import functools

import jax
import jax.numpy as jnp
from jax import lax
from jax.experimental import pallas as pl
from jax.experimental.layout import Layout, with_layout_constraint
from jax.experimental.pallas import tpu as pltpu
from jax.sharding import PartitionSpec as P

HEADS = 25
KV_HEADS = 5
HEAD_DIM = 64
INNER = 3200
STATE = 16
DT_RANK = 100
CONV = 4
WINDOW = 1024
LANES = 128
PACKS = 8
LOG2_E = 1.4426950408889634

epsilon = 1e-06
bf16 = jnp.bfloat16
f32 = jnp.float32


def dot(left, right, precision=None):
    return jnp.dot(left, right, precision=precision, preferred_element_type=f32)


def dot_right_t(left, right):
    return lax.dot_general(left, right, (((1,), (1,)), ((), ())), preferred_element_type=f32)


def dot_left_t(left, right):
    return lax.dot_general(left, right, (((0,), (0,)), ((), ())), preferred_element_type=f32)


def rms_norm(value_rows, gain):
    return (
        value_rows
        * lax.rsqrt(jnp.mean(value_rows * value_rows, axis=-1, keepdims=True) + epsilon)
        * gain
    )


def mix_branches(attended_values, ssm_out, norm_attn, norm_ssm):
    return (rms_norm(attended_values, norm_attn) + rms_norm(ssm_out, norm_ssm)) * 0.5


def swiglu(gate_val, up_val):
    return jax.nn.silu(gate_val) * up_val


def hbm_spec():
    return pl.BlockSpec(memory_space=pl.ANY)


def vmem_spec():
    return pl.BlockSpec(memory_space=pltpu.VMEM)


SMALL_COST = pl.CostEstimate(flops=0, bytes_accessed=10**4, transcendentals=0)


def send(src, dst, sems, axis, target):
    copy = pltpu.make_async_remote_copy(
        src_ref=src,
        dst_ref=dst,
        send_sem=sems[0],
        recv_sem=sems[1],
        device_id={axis: target},
        device_id_type=pl.DeviceIdType.MESH,
    )
    copy.start()
    return copy


def meet(axis, others):
    barrier = pltpu.get_barrier_semaphore()
    for other in others:
        pl.semaphore_signal(
            barrier, inc=1, device_id={axis: other}, device_id_type=pl.DeviceIdType.MESH
        )
    pl.semaphore_wait(barrier, len(others))


def rep_kernel(rep, counts, square, *refs):
    n_gather, n_sum, n_all, n_trade = counts
    chips = rep // 2
    refs = list(refs)

    def take(n):
        taken = refs[:n]
        del refs[:n]
        return taken

    gathers, sums, alls, trades = (take(n) for n in counts)
    gathered, summed, all_summed, traded = (take(n) for n in counts)
    reduced = sums + alls
    buffers = [take(3) for _ in reduced]
    totals = summed + take(n_all)
    local, far, near, direct = refs

    me = lax.axis_index("rep")
    core = lax.rem(me, 2)
    chip = (me - core) // 2
    partner = 2 * chip + 1 - core
    ahead = [lax.rem(chip + k, chips) for k in range(chips)]
    behind = [lax.rem(chip + chips - k, chips) for k in range(chips)]
    if square:
        along_x, along_y = chip + 1 - 2 * lax.rem(chip, 2), lax.rem(chip + 2, 4)
        first = along_x + core * (along_y - along_x)
        second = along_y + core * (along_x - along_y)
        across = 3 - chip
        linked = [2 * first + core, 2 * second + core]
    else:
        linked = [2 * ahead[k] + core for k in range(1, chips)]
    if n_trade:
        meet("rep", [lax.rem(me + k, rep) for k in range(1, rep)])
    else:
        meet("rep", linked + [partner])

    kept, sent = [], []

    def keep(src, dst):
        copy = pltpu.make_async_copy(src, dst, local.at[len(kept)])
        copy.start()
        kept.append(copy)

    def far_send(src, dst, slot, k, target):
        copy = send(src, dst, (far.at[0, slot, k], far.at[1, slot, k]), "rep", 2 * target + core)
        sent.append(copy)
        return copy

    def near_send(src, dst, slot, k):
        copy = send(src, dst, (near.at[0, slot, k], near.at[1, slot, k]), "rep", partner)
        sent.append(copy)
        return copy

    def start_gather(source, out, slot):
        if square:
            far_copies = [
                far_send(source, out.at[me], slot, 1, first),
                far_send(source, out.at[me], slot, 2, second),
            ]
        else:
            far_copies = [
                far_send(source, out.at[me], slot, k, ahead[k]) for k in range(1, chips)
            ]
        near_copies = [near_send(source, out.at[me], slot, 0)]
        keep(source, out.at[me])
        return out, slot, far_copies, near_copies

    def pass_on(states):
        if square:
            for out, slot, far_copies, near_copies in states:
                block = out.at[2 * first + core]
                far_copies[0].wait_recv()
                far_copies.append(far_send(block, block, slot, 3, second))
                near_copies.append(near_send(block, block, slot, 1))
            for out, slot, far_copies, near_copies in states:
                for k, source in ((2, second), (3, across)):
                    block = out.at[2 * source + core]
                    far_copies[k - 1].wait_recv()
                    near_copies.append(near_send(block, block, slot, k))
        else:
            for out, slot, far_copies, near_copies in states:
                for k in range(1, chips):
                    block = out.at[2 * behind[k] + core]
                    far_copies[k - 1].wait_recv()
                    near_copies.append(near_send(block, block, slot, k))
        for _, _, _, near_copies in states:
            for copy in near_copies:
                copy.wait_recv()

    dests = [chip, first, across, second] if square else ahead
    partner_dests = [chip, second, across, first] if square else ahead
    order = [1, 2, 3, 0] if square else [*range(1, chips), 0]
    crossing = []
    for i, source in enumerate(reduced):
        from_partner = buffers[i][1]
        crossing.append(
            {
                k: near_send(source.at[2 * partner_dests[k] + 1 - core], from_partner.at[k], i, k)
                for k in order
            }
        )
    states = [
        start_gather(source, gathered[i], len(reduced) + n_all + i)
        for i, source in enumerate(gathers)
    ]
    trading = []
    for i, source in enumerate(trades):
        keep(source.at[me], traded[i].at[me])
        for k in range(1, rep):
            target = lax.rem(me + k, rep)
            copy = send(
                source.at[target],
                traded[i].at[me],
                (direct.at[0, i, k], direct.at[1, i, k]),
                "rep",
                target,
            )
            trading.append(copy)

    def of_chip(i, k):
        crossing[i][k].wait_recv()
        own = reduced[i][2 * dests[k] + core]
        return own.astype(f32) + buffers[i][1][k].astype(f32)

    crossed = []
    for i in range(len(reduced)):
        low, _, arrived = buffers[i]
        copies = []
        for k in (1, 2) if square else range(1, chips):
            low[k - 1] = of_chip(i, k).astype(low.dtype)
            target = first if square else ahead[k]
            copies.append(far_send(low.at[k - 1], arrived.at[k - 1], i, k, target))
        crossed.append(copies)
    if square:
        for i in range(len(reduced)):
            low, _, arrived = buffers[i]
            value = of_chip(i, 3)
            crossed[i][1].wait_recv()
            low[2] = (value + arrived[1].astype(f32)).astype(low.dtype)
            crossed[i].append(far_send(low.at[2], arrived.at[2], i, 3, second))
    for i in range(len(reduced)):
        arrived = buffers[i][2]
        total = of_chip(i, 0)
        for k in (1, 3) if square else range(1, chips):
            crossed[i][k - 1].wait_recv()
            total = total + arrived[k - 1].astype(f32)
        totals[i][...] = total
        if i >= n_sum:
            states.append(start_gather(totals[i], all_summed[i - n_sum], n_all + i))
    pass_on(states)
    for copy in trading:
        copy.wait()
    for copy in sent:
        copy.wait_send()
    for copy in kept:
        copy.wait()


def rep_exchange(rep, collective_id, gathers=(), sums=(), alls=(), trades=()):
    chips = rep // 2
    square = rep == 8 and not alls
    counts = (len(gathers), len(sums), len(alls), len(trades))
    reduced = (*sums, *alls)
    out_shape = [jax.ShapeDtypeStruct((rep,) + x.shape, x.dtype) for x in gathers]
    out_shape += [jax.ShapeDtypeStruct(x.shape[1:], f32) for x in sums]
    out_shape += [jax.ShapeDtypeStruct(x.shape, f32) for x in alls]
    out_shape += [jax.ShapeDtypeStruct(x.shape, x.dtype) for x in trades]
    scratch = []
    for x in reduced:
        scratch += [
            pltpu.VMEM((n,) + x.shape[1:], x.dtype) for n in (chips - 1, chips, chips - 1)
        ]
    scratch += [pltpu.VMEM(x.shape[1:], f32) for x in alls]
    n_local = sum(counts) - len(sums) + 1
    n_slots = len(reduced) + len(alls) + len(gathers) + 1
    scratch += [
        pltpu.SemaphoreType.DMA((n_local,)),
        pltpu.SemaphoreType.DMA((2, n_slots, chips)),
        pltpu.SemaphoreType.DMA((2, n_slots, chips)),
        pltpu.SemaphoreType.DMA((2, len(trades) + 1, rep)),
    ]
    return pl.pallas_call(
        functools.partial(rep_kernel, rep, counts, square),
        out_shape=out_shape,
        in_specs=[vmem_spec()] * sum(counts),
        out_specs=[hbm_spec()] * len(gathers)
        + [vmem_spec()] * len(sums)
        + [hbm_spec()] * (len(alls) + len(trades)),
        scratch_shapes=scratch,
        compiler_params=pltpu.CompilerParams(
            collective_id=collective_id,
            has_side_effects=True,
            vmem_limit_bytes=40 * 1024 * 1024,
        ),
        cost_estimate=SMALL_COST,
    )(*gathers, *sums, *alls, *trades)


def line_kernel(count, counts, *refs):
    n_gather, n_all, n_trade = counts
    n_in = sum(counts)
    ins, outs, scratch = refs[:n_in], refs[n_in : 2 * n_in], refs[2 * n_in :]
    arrived, totals = scratch[:n_all], scratch[n_all : 2 * n_all]
    local, remote = scratch[2 * n_all :]
    me = lax.axis_index("fsdp")
    others = [lax.rem(me + k, count) for k in range(1, count)]
    meet("fsdp", others)
    copies, coming = [], []

    def push(block, out, slot):
        return [
            send(block(other), out, (remote.at[0, slot, k], remote.at[1, slot, k]), "fsdp", other)
            for k, other in enumerate(others)
        ]

    def keep(block, out, slot):
        copy = pltpu.make_async_copy(block, out, local.at[slot])
        copy.start()
        copies.append(copy)

    for i in range(n_all):
        source = ins[n_gather + i]
        coming.append(push(lambda other: source.at[other], arrived[i].at[me], n_in + i))
    for i in range(n_in):
        if i < n_gather:
            keep(ins[i], outs[i].at[me], i)
            copies += push(lambda other: ins[i], outs[i].at[me], i)
        elif i >= n_gather + n_all:
            keep(ins[i].at[me], outs[i].at[me], i)
            copies += push(lambda other: ins[i].at[other], outs[i].at[me], i)
    for i in range(n_all):
        for copy in coming[i]:
            copy.wait()
        total = ins[n_gather + i][me].astype(f32)
        for other in others:
            total = total + arrived[i][other].astype(f32)
        totals[i][...] = total.astype(totals[i].dtype)
        out = outs[n_gather + i]
        keep(totals[i], out.at[me], n_gather + i)
        copies += push(lambda other: totals[i], out.at[me], n_gather + i)
    for copy in copies:
        copy.wait()


def line_exchange(count, collective_id, gathers=(), alls=(), trades=()):
    arrays = (*gathers, *alls, *trades)
    out_shape = [jax.ShapeDtypeStruct((count,) + x.shape, x.dtype) for x in gathers]
    out_shape += [jax.ShapeDtypeStruct(x.shape, x.dtype) for x in (*alls, *trades)]
    return pl.pallas_call(
        functools.partial(line_kernel, count, (len(gathers), len(alls), len(trades))),
        out_shape=out_shape,
        in_specs=[vmem_spec()] * len(arrays),
        out_specs=[hbm_spec()] * len(arrays),
        scratch_shapes=[pltpu.VMEM(x.shape, x.dtype) for x in alls]
        + [pltpu.VMEM(x.shape[1:], x.dtype) for x in alls]
        + [
            pltpu.SemaphoreType.DMA((len(arrays),)),
            pltpu.SemaphoreType.DMA((2, len(arrays) + len(alls), count)),
        ],
        compiler_params=pltpu.CompilerParams(collective_id=collective_id, has_side_effects=True),
        cost_estimate=SMALL_COST,
    )(*arrays)


def last_kernel(rep, fsdp, square, n_gather, *refs):
    chips = rep // 2
    gathers, refs = refs[:n_gather], refs[n_gather:]
    small, gains, trades, refs = refs[0], refs[1], refs[2:4], refs[4:]
    gathered, refs = refs[:n_gather], refs[n_gather:]
    small_out, gains_out, traded, refs = refs[0], refs[1], refs[2:4], refs[4:]
    arrived, total, lined, gains_in, gains_sum, local, far, near, remote = refs

    me, line = lax.axis_index("rep"), lax.axis_index("fsdp")
    core = lax.rem(me, 2)
    chip = (me - core) // 2
    partner = 2 * chip + 1 - core
    if square:
        along_x, along_y = chip + 1 - 2 * lax.rem(chip, 2), lax.rem(chip + 2, 4)
        first = along_x + core * (along_y - along_x)
        second = along_y + core * (along_x - along_y)
        hops, sources = [first, second], [first, second, 3 - chip]
    else:
        hops = [lax.rem(chip + k, chips) for k in range(1, chips)]
        sources = [lax.rem(chip + chips - k, chips) for k in range(1, chips)]
    others = [lax.rem(line + k, fsdp) for k in range(1, fsdp)]
    barrier = pltpu.get_barrier_semaphore()
    for axis, indices in (("rep", [2 * hop + core for hop in hops] + [partner]), ("fsdp", others)):
        for index in indices:
            pl.semaphore_signal(
                barrier, inc=1, device_id={axis: index}, device_id_type=pl.DeviceIdType.MESH
            )
    pl.semaphore_wait(barrier, len(hops) + 1 + len(others))

    kept, sent, waited = [], [], []

    def keep(src, dst):
        copy = pltpu.make_async_copy(src, dst, local.at[len(kept)])
        copy.start()
        kept.append(copy)

    def push(block, out, slot):
        copies = [
            send(block(other), out, (remote.at[0, slot, k], remote.at[1, slot, k]), "fsdp", other)
            for k, other in enumerate(others)
        ]
        return copies

    def hop_send(src, dst, slot, k, target):
        copy = send(src, dst, (far.at[0, slot, k], far.at[1, slot, k]), "rep", 2 * target + core)
        sent.append(copy)
        return copy

    def cross_send(src, dst, slot, k):
        copy = send(src, dst, (near.at[0, slot, k], near.at[1, slot, k]), "rep", partner)
        sent.append(copy)
        waited.append(copy)

    def start_gather(source, out, slot):
        far_copies = [
            hop_send(source, out.at[me], slot, k, hop) for k, hop in enumerate(hops)
        ]
        cross_send(source, out.at[me], slot, chips - 1)
        keep(source, out.at[me])
        return out, slot, far_copies

    def pass_on(state):
        out, slot, far_copies = state
        for k, source in enumerate(sources):
            block = out.at[2 * source + core]
            far_copies[k].wait_recv()
            if square and k == 0:
                far_copies.append(hop_send(block, block, slot, 2, second))
            cross_send(block, block, slot, k)

    small_copies = push(lambda other: small.at[other], arrived.at[line], 0)
    states = [start_gather(gains, gains_in, 0)]
    for i in range(n_gather):
        states.append(start_gather(gathers[i], gathered[i], 1 + i))
    for i in range(2):
        keep(trades[i].at[line], traded[i].at[line])
        waited += push(lambda other: trades[i].at[other], traded[i].at[line], 1 + i)
        sent += waited[-len(others) :]
    for copy in small_copies:
        copy.wait()
    value = small[line].astype(f32)
    for other in others:
        value = value + arrived[other].astype(f32)
    total[...] = value.astype(total.dtype)
    small_copies = push(lambda other: total, lined.at[line], 3)
    lined[line] = total[...]

    gains_state, states = states[0], states[1:]
    crossed = len(waited)
    pass_on(gains_state)
    for copy in waited[crossed:]:
        copy.wait_recv()
    for state in states:
        pass_on(state)
    for copy in small_copies:
        copy.wait()
    small_state = start_gather(lined, small_out, 1 + n_gather)
    kept[0].wait()
    waited.pop(0).wait_recv()
    gains_sum[...] = jnp.sum(gains_in[...], axis=0)
    keep(gains_sum, gains_out.at[line])
    gains_copies = push(lambda other: gains_sum, gains_out.at[line], 4)
    pass_on(small_state)
    for copy in waited[: crossed - 1] + waited[crossed - 1 + chips - 1 :]:
        copy.wait_recv()
    for copy in sent:
        copy.wait_send()
    for copy in gains_copies:
        copy.wait()
    for copy in kept[1:]:
        copy.wait()


def last_exchange(rep, fsdp, collective_id, gathers, small, gains, trades):
    n_gather, chips = len(gathers), rep // 2
    out_shape = [jax.ShapeDtypeStruct((rep,) + x.shape, x.dtype) for x in gathers]
    out_shape.append(jax.ShapeDtypeStruct((rep,) + small.shape, small.dtype))
    out_shape.append(jax.ShapeDtypeStruct((fsdp,) + gains.shape, gains.dtype))
    out_shape += [jax.ShapeDtypeStruct(x.shape, x.dtype) for x in trades]
    return pl.pallas_call(
        functools.partial(last_kernel, rep, fsdp, rep == 8, n_gather),
        out_shape=out_shape,
        in_specs=[vmem_spec()] * (n_gather + 4),
        out_specs=[hbm_spec()] * (n_gather + 4),
        scratch_shapes=[
            pltpu.VMEM(small.shape, small.dtype),
            pltpu.VMEM(small.shape[1:], small.dtype),
            pltpu.VMEM(small.shape, small.dtype),
            pltpu.VMEM((rep,) + gains.shape, gains.dtype),
            pltpu.VMEM(gains.shape, gains.dtype),
            pltpu.SemaphoreType.DMA((n_gather + 5,)),
            pltpu.SemaphoreType.DMA((2, n_gather + 2, chips)),
            pltpu.SemaphoreType.DMA((2, n_gather + 2, chips)),
            pltpu.SemaphoreType.DMA((2, 5, fsdp)),
        ],
        compiler_params=pltpu.CompilerParams(
            collective_id=collective_id,
            has_side_effects=True,
            vmem_limit_bytes=40 * 1024 * 1024,
        ),
        cost_estimate=SMALL_COST,
    )(*gathers, small, gains, *trades)


def pair_kernel(own_ref, out_ref, local, send_sem, recv_sem):
    me = lax.axis_index("rep")
    core = lax.rem(me, 2)
    partner = me + 1 - 2 * core
    meet("rep", [partner])
    keep = pltpu.make_async_copy(own_ref, out_ref.at[:, core], local)
    keep.start()
    copy = send(own_ref, out_ref.at[:, core], (send_sem, recv_sem), "rep", partner)
    copy.wait()
    keep.wait()


def pair_gather(collective_id, own):
    groups, rows, width = own.shape
    return pl.pallas_call(
        pair_kernel,
        out_shape=jax.ShapeDtypeStruct((groups, 2, rows, width), own.dtype),
        in_specs=[vmem_spec()],
        out_specs=hbm_spec(),
        scratch_shapes=[pltpu.SemaphoreType.DMA] * 3,
        compiler_params=pltpu.CompilerParams(collective_id=collective_id, has_side_effects=True),
        cost_estimate=SMALL_COST,
    )(own)


def windows(width, pieces, start, step, rest):
    wide = min(-(-(rest + LANES - 1) // LANES) * LANES, width)
    me = lax.axis_index("rep")
    for i in range(pieces):
        at = start + i * step + me * rest
        aligned = jnp.minimum((at // LANES) * LANES, (width - wide) // LANES * LANES)
        yield pl.multiple_of(aligned, LANES), at - aligned, wide


def up16(size):
    return -(-size // 16) * 16


def copy_parts(rep, fsdp, source, out, place, start, total):
    rest = total // (rep * fsdp)
    rows = source.shape[0]
    for aligned, shift, wide in windows(source.shape[1], fsdp, start, rep * rest, rest):
        value = source[:, pl.ds(aligned, wide)].astype(f32)
        value = pltpu.roll(value, lax.rem(wide - shift, wide), 1)[:, :rest]
        if up16(rest) > rest:
            value = jnp.concatenate([value, jnp.zeros((rows, up16(rest) - rest), f32)], axis=1)
        out[:, place : place + up16(rest)] = value.astype(bf16)
        place += up16(rest)


def part_in_kernel(rep, fsdp, spots, qkv_ref, min_ref, out_ref):
    _, qkv_at, gate_at = spots
    rows, qkv_width = qkv_ref.shape
    qkv_part = qkv_width // rep
    out_ref[...] = jnp.zeros_like(out_ref)
    copy_parts(rep, fsdp, min_ref, out_ref, 0, 0, INNER)
    copy_parts(rep, fsdp, min_ref, out_ref, gate_at, INNER, INNER)
    value = qkv_ref[...].astype(f32)
    padded = -(-qkv_width // LANES) * LANES
    value = jnp.concatenate([value, jnp.zeros((rows, padded - qkv_width), f32)], axis=1)
    shift = padded - lax.axis_index("rep") * qkv_part
    value = pltpu.roll(value, lax.rem(shift, padded), 1)
    out_ref[:, qkv_at : qkv_at + qkv_part] = value[:, :qkv_part].astype(bf16)


def part_gate_up_kernel(rep, fsdp, gate_ref, up_ref, out_ref):
    copy_parts(rep, fsdp, gate_ref, out_ref, 0, 0, gate_ref.shape[1])
    copy_parts(rep, fsdp, up_ref, out_ref, out_ref.shape[1] // 2, 0, up_ref.shape[1])


def by_rows(kernel, sources, width):
    rows = sources[0].shape[0]
    block = 80 if rows % 80 == 0 else rows
    return pl.pallas_call(
        kernel,
        grid=(rows // block,),
        in_specs=[pl.BlockSpec((block, x.shape[1]), lambda i: (i, 0)) for x in sources],
        out_specs=pl.BlockSpec((block, width), lambda i: (i, 0)),
        out_shape=jax.ShapeDtypeStruct((rows, width), bf16),
        compiler_params=pltpu.CompilerParams(vmem_limit_bytes=40 * 1024 * 1024),
        cost_estimate=SMALL_COST,
    )(*sources)


def join_kernel(rep, layout, *refs):
    sources, outs = refs[: len(refs) - len(layout)], refs[len(refs) - len(layout) :]
    for out, entries in zip(outs, layout):
        for index, first, rest, place, pieces in entries:
            for i in range(pieces):
                start = first + i * up16(rest)
                for r in range(rep):
                    at = place + (i * rep + r) * rest
                    piece = sources[index][r, :, start : start + rest]
                    out[:, at : at + rest] = piece.astype(f32)


def join_rows_kernel(rep, rows, flip, source, out):
    for r in range(rep):
        if flip:
            out[:, r * rows : (r + 1) * rows] = source[r].astype(f32).T[:, :rows]
        else:
            out[r * rows : (r + 1) * rows, :] = source[r, :rows, :].astype(f32)


def join_rows(rep, source, total, width, flip=False):
    block = 2 * LANES
    shape = (total, width)
    out_spec = pl.BlockSpec((total, block), lambda i: (0, i))
    if flip:
        shape = (width, total)
        out_spec = pl.BlockSpec((block, total), lambda i: (i, 0))
    return pl.pallas_call(
        functools.partial(join_rows_kernel, rep, total // rep, flip),
        grid=(pl.cdiv(width, block),),
        in_specs=[pl.BlockSpec((rep, source.shape[1], block), lambda i: (0, 0, i))],
        out_specs=out_spec,
        out_shape=jax.ShapeDtypeStruct(shape, f32),
        compiler_params=pltpu.CompilerParams(vmem_limit_bytes=40 * 1024 * 1024),
        cost_estimate=SMALL_COST,
    )(source)


def join_columns(rep, sources, widths, layout):
    rows = sources[0].shape[1]
    block = next(n for n in (80, 40, 64, rows) if rows % n == 0)
    return pl.pallas_call(
        functools.partial(join_kernel, rep, layout),
        grid=(rows // block,),
        in_specs=[
            pl.BlockSpec((rep, block, x.shape[2]), lambda i: (0, i, 0)) for x in sources
        ],
        out_specs=[pl.BlockSpec((block, width), lambda i: (i, 0)) for width in widths],
        out_shape=[jax.ShapeDtypeStruct((rows, width), f32) for width in widths],
        compiler_params=pltpu.CompilerParams(vmem_limit_bytes=48 * 1024 * 1024),
        cost_estimate=SMALL_COST,
    )(*sources)


def spread_maps(maps_ref, wide_ref, start):
    count, packs, columns = maps_ref.shape

    def spread(i, _):
        for u in range(2):
            t = 2 * i + u
            maps = maps_ref[t]
            for n in range(columns):
                wide_ref[n, start + t] = jnp.broadcast_to(maps[:, n : n + 1], (packs, LANES))
        return 0

    lax.fori_loop(0, count // 2, spread, 0)


def scan_kernel(
    channels,
    decay_step_ref,
    input_ref,
    maps_ref,
    rate_ref,
    _handed_ref,
    out_ref,
    decayed_ref,
    _handed_on_ref,
    wide_ref,
):
    count, packs, _ = decay_step_ref.shape
    valid = (
        lax.broadcasted_iota(jnp.int32, (packs, LANES), 1)
        < channels - pl.program_id(1) * LANES
    )
    rate = jnp.where(valid[:1], rate_ref[...], 0.0)

    @pl.when(pl.program_id(1) == 0)
    def _():
        spread_maps(maps_ref, wide_ref, 0)

    def step(i, states):
        for u in range(2):
            t = 2 * i + u
            decay_step = jnp.where(valid, decay_step_ref[t], 0.0)
            inputs = jnp.where(valid, input_ref[t], 0.0)
            out = jnp.zeros((packs, LANES), f32)
            new_states = []
            for n in range(STATE):
                decayed = jnp.exp2(decay_step * rate[n : n + 1]) * states[n]
                state = decayed + wide_ref[n, t] * inputs
                out = out + state * wide_ref[STATE + n, t]
                decayed_ref[n, t] = decayed
                new_states.append(state)
            out_ref[t] = out
            states = tuple(new_states)
        return states

    lax.fori_loop(0, count // 2, step, (jnp.zeros((packs, LANES), f32),) * STATE)


def scan_forward(decay_step, inputs, maps, rate, handed):
    count, packs, channels = inputs.shape
    wide = pl.BlockSpec((count, PACKS, LANES), lambda g, i: (0, g, i))
    return pl.pallas_call(
        functools.partial(scan_kernel, channels),
        grid=(packs // PACKS, pl.cdiv(channels, LANES)),
        in_specs=[
            wide,
            wide,
            pl.BlockSpec((count, PACKS, 2 * STATE), lambda g, i: (0, g, 0)),
            pl.BlockSpec((STATE, LANES), lambda g, i: (0, i)),
            hbm_spec(),
        ],
        out_specs=[
            wide,
            pl.BlockSpec((STATE, count, PACKS, LANES), lambda g, i: (0, 0, g, i)),
            hbm_spec(),
        ],
        input_output_aliases={4: 2},
        out_shape=[
            jax.ShapeDtypeStruct(inputs.shape, f32),
            jax.ShapeDtypeStruct(
                (STATE, count, packs, pl.cdiv(channels, LANES) * LANES), f32
            ),
            jax.ShapeDtypeStruct(handed.shape, handed.dtype),
        ],
        scratch_shapes=[pltpu.VMEM((2 * STATE, count, PACKS, LANES), f32)],
        compiler_params=pltpu.CompilerParams(vmem_limit_bytes=48 * 1024 * 1024),
        cost_estimate=SMALL_COST,
    )(decay_step, inputs, maps, rate, handed)


def spread_beside(rep, steps, source, out, local, far, near):
    chips, square = rep // 2, rep == 8
    me = lax.axis_index("rep")
    core = lax.rem(me, 2)
    chip = (me - core) // 2
    partner = 2 * chip + 1 - core
    if square:
        along_x, along_y = chip + 1 - 2 * lax.rem(chip, 2), lax.rem(chip + 2, 4)
        first = along_x + core * (along_y - along_x)
        second = along_y + core * (along_x - along_y)
        hops, sources = [first, second], [first, second, 3 - chip]
    else:
        hops = [lax.rem(chip + k, chips) for k in range(1, chips)]
        sources = [lax.rem(chip + chips - k, chips) for k in range(1, chips)]

    def copy_to(src, dst, sems, k, target):
        return pltpu.make_async_remote_copy(
            src_ref=src,
            dst_ref=dst,
            send_sem=sems.at[0, k],
            recv_sem=sems.at[1, k],
            device_id={"rep": target},
            device_id_type=pl.DeviceIdType.MESH,
        )

    def block(k):
        return out.at[2 * sources[k] + core]

    own = [copy_to(source, out.at[me], far, k, 2 * hop + core) for k, hop in enumerate(hops)]
    if square:
        own.append(copy_to(block(0), block(0), far, 2, 2 * second + core))
    crossing = [copy_to(block(k), block(k), near, k, partner) for k in range(chips - 1)]
    crossing.append(copy_to(source, out.at[me], near, chips - 1, partner))
    keep = pltpu.make_async_copy(source, out.at[me], local)

    @pl.when(steps[0])
    def _():
        meet("rep", [2 * hop + core for hop in hops] + [partner])
        for copy in own[: len(hops)]:
            copy.start()
        crossing[-1].start()
        keep.start()

    @pl.when(steps[1])
    def _():
        own[0].wait_recv()
        if square:
            own[2].start()
        crossing[0].start()

    @pl.when(steps[2])
    def _():
        for k in range(1, len(hops)):
            own[k].wait_recv()
            crossing[k].start()

    @pl.when(steps[3])
    def _():
        if square:
            own[2].wait_recv()
            crossing[2].start()
        for copy in crossing:
            copy.wait()
        for copy in own:
            copy.wait_send()
        keep.wait()


def scan_back_kernel(
    rep,
    channels,
    decay_step_ref,
    step_ref,
    input_ref,
    maps_ref,
    grad_ref,
    decayed_ref,
    rate_ref,
    beside_ref,
    grad_input_ref,
    grad_step_ref,
    grad_rate_ref,
    grad_maps_ref,
    beside_out_ref,
    carry_ref,
    rates_ref,
    in_sum_ref,
    out_sum_ref,
    both_sum_ref,
    wide_ref,
    local,
    far,
    near,
):
    count, packs, _ = decay_step_ref.shape
    at = (pl.program_id(0) * pl.num_programs(1) + pl.program_id(1)) * pl.num_programs(2)
    at = at + pl.program_id(2)
    last = pl.num_programs(0) * pl.num_programs(1) * pl.num_programs(2) - 1
    steps = [at == step for step in (0, 9 * last // 16, 11 * last // 16, last)]
    spread_beside(rep, steps, beside_ref, beside_out_ref, local, far, near)
    tile, chunk = pl.program_id(1), pl.program_id(2)
    start = (pl.num_programs(2) - 1 - chunk) * count
    valid = lax.broadcasted_iota(jnp.int32, (packs, LANES), 1) < channels - tile * LANES

    @pl.when(tile == 0)
    def _():
        spread_maps(maps_ref, wide_ref, start)
        zeros = jnp.zeros((STATE, count, packs, LANES), f32)
        in_sum_ref[:, pl.ds(start, count)] = zeros
        out_sum_ref[:, pl.ds(start, count)] = zeros
        both_sum_ref[pl.ds(start, count)] = zeros[0]

    @pl.when(chunk == 0)
    def _():
        carry_ref[...] = jnp.zeros_like(carry_ref)
        for n in range(STATE):
            rates_ref[n] = jnp.where(
                valid, jnp.broadcast_to(rate_ref[n : n + 1, :], (packs, LANES)), 0.0
            )

    def backward(back_t, carried):
        grad_states, grad_rates = carried
        t = count - 1 - back_t
        at = start + t
        decay_step = jnp.where(valid, decay_step_ref[t], 0.0)
        step = jnp.where(valid, step_ref[t], 0.0)
        inputs = jnp.where(valid, input_ref[t], 0.0)
        grad = jnp.where(valid, grad_ref[t], 0.0)
        both_sum_ref[at] += grad * inputs
        grad_input = grad_step = jnp.zeros((packs, LANES), f32)
        new_states, new_rates = [], []
        for n in range(STATE):
            decayed, rate = decayed_ref[n, t], rates_ref[n]
            grad_state = grad * wide_ref[STATE + n, at] + grad_states[n]
            out_sum_ref[n, at] += grad * decayed
            in_sum_ref[n, at] += grad_state * inputs
            grad_input = grad_input + grad_state * wide_ref[n, at]
            through = grad_state * decayed
            grad_step = grad_step + through * rate
            new_rates.append(grad_rates[n] + through * step)
            new_states.append(jnp.exp2(decay_step * rate) * grad_state)
        grad_input_ref[t] = grad_input
        grad_step_ref[t] = grad_step
        return (tuple(new_states), tuple(new_rates))

    carried = (
        tuple(carry_ref[n] for n in range(STATE)),
        tuple(carry_ref[STATE + n] for n in range(STATE)),
    )
    grad_states, grad_rates = lax.fori_loop(0, count, backward, carried)
    for n in range(STATE):
        carry_ref[n] = grad_states[n]
        carry_ref[STATE + n] = grad_rates[n]

    @pl.when(chunk == pl.num_programs(2) - 1)
    def _():
        for n in range(STATE):
            grad_rate_ref[n : n + 1, :] = jnp.sum(grad_rates[n], axis=0, keepdims=True)

    @pl.when(tile == pl.num_programs(1) - 1)
    def _():
        column = lax.broadcasted_iota(jnp.int32, (LANES, LANES), 1)
        here = pl.ds(start, count)

        def summed(value, place):
            return jnp.dot(
                value.reshape(count * packs, LANES).astype(bf16),
                (column == place).astype(bf16),
                preferred_element_type=f32,
            )

        total = summed(both_sum_ref[here], 2 * STATE)
        for n in range(STATE):
            total = total + summed(in_sum_ref[n, here], n)
            total = total + summed(out_sum_ref[n, here], STATE + n)
        grad_maps_ref[here] = total.reshape(count, packs, LANES)


def scan_backward(decay_step, step, inputs, maps, grad, decayed, rate, rep, collective_id, beside):
    count, packs, channels = inputs.shape
    groups, chunks = packs // PACKS, 4
    part = count // chunks
    wide = pl.BlockSpec((part, PACKS, LANES), lambda g, i, c: (chunks - 1 - c, g, i))
    row = pl.BlockSpec((STATE, LANES), lambda g, i, c: (0, i))
    sums = pltpu.VMEM((STATE, count, PACKS, LANES), f32)
    grad_inputs, grad_step, grad_rate, grad_maps, all_beside = pl.pallas_call(
        functools.partial(scan_back_kernel, rep, channels),
        grid=(groups, pl.cdiv(channels, LANES), chunks),
        in_specs=[
            wide,
            wide,
            wide,
            pl.BlockSpec((part, PACKS, 2 * STATE), lambda g, i, c: (chunks - 1 - c, g, 0)),
            wide,
            pl.BlockSpec(
                (STATE, part, PACKS, LANES), lambda g, i, c: (0, chunks - 1 - c, g, i)
            ),
            row,
            hbm_spec(),
        ],
        out_specs=[
            wide,
            wide,
            pl.BlockSpec((STATE, LANES), lambda g, i, c: (g, i)),
            pl.BlockSpec((count, PACKS, LANES), lambda g, i, c: (0, g, 0)),
            hbm_spec(),
        ],
        out_shape=[
            jax.ShapeDtypeStruct(inputs.shape, f32),
            jax.ShapeDtypeStruct(inputs.shape, f32),
            jax.ShapeDtypeStruct((groups * STATE, channels), f32),
            jax.ShapeDtypeStruct((count, packs, LANES), f32),
            jax.ShapeDtypeStruct((rep,) + beside.shape, beside.dtype),
        ],
        scratch_shapes=[
            pltpu.VMEM((2 * STATE, PACKS, LANES), f32),
            pltpu.VMEM((STATE, PACKS, LANES), f32),
            sums,
            sums,
            pltpu.VMEM((count, PACKS, LANES), f32),
            pltpu.VMEM((2 * STATE, count, PACKS, LANES), f32),
            pltpu.SemaphoreType.DMA,
            pltpu.SemaphoreType.DMA((2, rep // 2)),
            pltpu.SemaphoreType.DMA((2, rep // 2)),
        ],
        compiler_params=pltpu.CompilerParams(
            collective_id=collective_id,
            has_side_effects=True,
            vmem_limit_bytes=52 * 1024 * 1024,
        ),
        cost_estimate=SMALL_COST,
    )(decay_step, step, inputs, maps, grad, decayed, rate, beside)
    grad_rate = jnp.sum(grad_rate.reshape(groups, STATE, channels), axis=0)
    in_maps, both = grad_maps[:, :, :STATE], grad_maps[:, :, 2 * STATE : 2 * STATE + 1]
    out_maps = grad_maps[:, :, STATE : 2 * STATE] + maps[:, :, :STATE] * both
    grad_maps = jnp.concatenate([in_maps, out_maps], axis=2).reshape(count * packs, 2 * STATE)
    return grad_inputs, grad_step, grad_rate, grad_maps, all_beside


def split_heads(qkv_low):
    count = qkv_low.shape[0]
    group_size = HEADS // KV_HEADS
    query_width = HEADS * HEAD_DIM
    kv_width = KV_HEADS * HEAD_DIM
    query_rows = qkv_low[:, :query_width].reshape(count, KV_HEADS, group_size, HEAD_DIM)
    key_rows = qkv_low[:, query_width : query_width + kv_width].reshape(count, KV_HEADS, HEAD_DIM)
    value_rows = qkv_low[:, query_width + kv_width :].reshape(count, KV_HEADS, HEAD_DIM)
    return (query_rows, key_rows, value_rows)


def masked_scores(query_rows, key_rows, allowed):
    attention_scores = jnp.einsum(
        "jzhx,kzx->zhjk", query_rows, key_rows, preferred_element_type=f32
    ) * HEAD_DIM ** (-0.5)
    return jnp.where(allowed[None, None], attention_scores, -1e30)


def attention_forward(qkv_low, allowed):
    count = qkv_low.shape[0]
    query_rows, key_rows, value_rows = split_heads(qkv_low)
    attention_scores = masked_scores(query_rows, key_rows, allowed)
    row_max = jnp.max(attention_scores, axis=-1, keepdims=True)
    weights_exp = jnp.exp(attention_scores - row_max)
    row_total = jnp.sum(weights_exp, axis=-1, keepdims=True)
    lowered_probabilities = (weights_exp / row_total).astype(bf16)
    attended_values = jnp.einsum(
        "lpho,ole->hlpe", lowered_probabilities, value_rows, preferred_element_type=f32
    )
    return (attended_values.reshape(count, HEADS * HEAD_DIM), row_max + jnp.log(row_total))


def attention_backward(qkv_low, grad_low, log_total, allowed):
    count = qkv_low.shape[0]
    query_rows, key_rows, value_rows = split_heads(qkv_low)
    probabilities = jnp.exp(masked_scores(query_rows, key_rows, allowed) - log_total)
    head_gradient = grad_low.reshape(count, KV_HEADS, HEADS // KV_HEADS, HEAD_DIM)
    grad_probs = jnp.einsum(
        "jzhx,kzx->zhjk", head_gradient, value_rows, preferred_element_type=f32
    )
    score_gradient = (
        probabilities * (grad_probs - jnp.sum(grad_probs * probabilities, axis=-1, keepdims=True))
    ).astype(bf16)
    scale_factor_scores = HEAD_DIM ** (-0.5)
    grad_queries = (
        jnp.einsum("lpho,ole->hlpe", score_gradient, key_rows, preferred_element_type=f32)
        * scale_factor_scores
    )
    grad_keys = (
        jnp.einsum("wniv,iwne->vwe", score_gradient, query_rows, preferred_element_type=f32)
        * scale_factor_scores
    )
    grad_values = jnp.einsum(
        "wniv,iwne->vwe", probabilities.astype(bf16), head_gradient, preferred_element_type=f32
    )
    return jnp.concatenate(
        [
            grad_queries.reshape(count, -1),
            grad_keys.reshape(count, -1),
            grad_values.reshape(count, -1),
        ],
        axis=1,
    )


def tied(value, *others):
    return lax.optimization_barrier((value,) + others)[0]


def by_row(value):
    return with_layout_constraint(value, Layout(major_to_minor=(0, 1)))


def silu_and_slope(value):
    gate = jax.nn.sigmoid(value)
    return value * gate, gate * (1.0 + value * (1.0 - gate))


def shift_down(rows, amount):
    return jnp.concatenate([jnp.zeros((amount,) + rows.shape[1:], rows.dtype), rows[:-amount]], 0)


def shift_up(rows, amount):
    return jnp.concatenate([rows[amount:], jnp.zeros((amount,) + rows.shape[1:], rows.dtype)], 0)


def per_device(
    rep,
    fsdp,
    tokens,
    cotangent,
    lengths,
    source_slot,
    norm_in,
    w_qkv,
    w_mamba_in,
    conv_weight,
    conv_bias,
    x_proj,
    dt_proj,
    dt_bias,
    a_log,
    d_skip,
    w_mamba_out,
    norm_attn,
    norm_ssm,
    w_mix_out,
    norm_ffn,
    w_gate,
    w_up,
    w_down,
):
    count, width = tokens.shape
    block_rows = count // fsdp
    piece, ff_piece = INNER // (rep * fsdp), w_gate.shape[1] // (rep * fsdp)
    channels, ff_part = fsdp * up16(piece), fsdp * up16(ff_piece)
    qkv_part = w_qkv.shape[1] // rep
    group = rep * count
    high = lax.Precision.HIGH
    me, line = lax.axis_index("rep"), lax.axis_index("fsdp")

    def my_part(value, axis):
        rest = value.shape[axis] // (rep * fsdp)
        spare = [(0, up16(rest) - rest if i == axis else 0) for i in range(value.ndim)]
        return jnp.concatenate(
            [
                jnp.pad(lax.dynamic_slice_in_dim(value, (i * rep + me) * rest, rest, axis), spare)
                for i in range(fsdp)
            ],
            axis=axis,
        )

    def my_rows(value):
        rest = value.shape[0] // rep
        part = lax.dynamic_slice_in_dim(value, me * rest, rest, 0)
        return jnp.pad(part, ((0, up16(rest) - rest), (0, 0)))

    def line_gather(value):
        return lax.all_gather(value, "fsdp", axis=0, tiled=True)

    def line_scatter(value):
        return lax.psum_scatter(value, "fsdp", scatter_dimension=0, tiled=True)

    def swapped(rows):
        lead = count if rows.shape[0] == count else rep
        return rows.transpose(1, 0, 2).reshape(group, rows.shape[2])

    early_width = -(-(qkv_part + channels) // LANES) * LANES
    gate_at = -(-(channels + qkv_part) // LANES) * LANES
    in_width = -(-(gate_at + channels) // LANES) * LANES
    part_in = by_rows(
        functools.partial(part_in_kernel, rep, fsdp, (0, channels, gate_at)),
        (w_qkv, w_mamba_in),
        in_width,
    )
    full_in = line_gather(part_in)
    half = w_mix_out.shape[0] // 2
    part_mix = lax.dynamic_slice_in_dim(w_mix_out, lax.rem(me, 2) * half, half, 0)
    part_mout, part_down = my_rows(w_mamba_out), my_rows(w_down)

    received, cot_received = line_exchange(
        fsdp,
        0,
        trades=(
            tied(tokens, part_in).reshape(fsdp, block_rows, width),
            cotangent.reshape(fsdp, block_rows, width),
        ),
    )
    w_gate, w_up, part_mout, part_mix, part_down, received = lax.optimization_barrier(
        (w_gate, w_up, part_mout, part_mix, part_down, received)
    )
    mout_mix = line_gather(jnp.concatenate([part_mout, part_mix], axis=0))
    part_gate_up = by_rows(
        functools.partial(part_gate_up_kernel, rep, fsdp), (w_gate, w_up), 2 * ff_part
    )
    full_gate_up, full_down = line_gather(part_gate_up), line_gather(part_down)
    slots = source_slot[0]
    picks = (slots[:, None] == jnp.arange(count, dtype=jnp.int32)[None, :]).astype(bf16)
    hidden_in = dot(picks, received.reshape(count, width))
    cot_rows = dot(picks, cot_received.reshape(count, width))
    cot_low = cot_rows.astype(bf16)

    ends = jnp.cumsum(lengths[0], dtype=jnp.int32)
    positions = jnp.arange(count, dtype=jnp.int32)
    passed = positions[:, None] >= ends[None, :-1]
    seg_ids = jnp.sum(passed.astype(jnp.int32), axis=1)
    in_seq = positions - jnp.max(jnp.where(passed, ends[None, :-1], 0), axis=1)
    distance = positions[:, None] - positions[None, :]
    allowed = (seg_ids[:, None] == seg_ids[None, :]) & (distance >= 0) & (distance < WINDOW)

    normed, norm_in_pull = jax.vjp(rms_norm, hidden_in, norm_in)
    marks = jnp.broadcast_to(in_seq[:, None].astype(bf16), (count, 64))
    normed_marked = jnp.concatenate([normed.astype(bf16), marks], axis=1)
    normed_sent, cot_all = rep_exchange(rep, 1, gathers=(normed_marked, cot_low))
    cot_all = cot_all.reshape(group, width)
    normed_all = normed_sent[:, :, :width].reshape(group, width)
    in_seq_all = normed_sent[:, :, width].astype(f32).T.reshape(group, 1)

    in_out = dot(swapped(normed_all.reshape(rep, count, width)), full_in)
    xs, gate_z = in_out[:, :channels], in_out[:, gate_at : gate_at + channels]
    qkv_sent = in_out[:, channels : channels + qkv_part].astype(bf16)
    qkv_sent = swapped(qkv_sent.reshape(count, rep, qkv_part))

    conv_w, conv_b = my_part(conv_weight, 1), my_part(conv_bias, 0)
    part_x_proj, part_dt_proj = my_part(x_proj, 0), my_part(dt_proj, 1)
    part_dt_bias, part_skip = my_part(dt_bias, 0), my_part(d_skip, 0)
    rate = -jnp.exp(my_part(a_log, 1))
    conv_sum = xs * conv_w[CONV - 1] + conv_b
    for k in range(1, CONV):
        earlier = jnp.where(in_seq_all >= k, shift_down(xs, k * rep), 0.0)
        conv_sum = conv_sum + earlier * conv_w[CONV - 1 - k]
    act, act_slope = silu_and_slope(conv_sum)
    proj_sent = dot(act, part_x_proj, high).reshape(count, rep, -1).transpose(1, 0, 2)
    proj, qkv_back = rep_exchange(
        rep, 2, alls=(proj_sent,), trades=(qkv_sent.reshape(rep, count, qkv_part),)
    )
    qkv_low = qkv_back.transpose(1, 0, 2).reshape(count, rep * qkv_part)
    proj = proj.transpose(1, 0, 2)
    dt_in = proj.reshape(group, -1)[:, :DT_RANK]
    maps = proj[:, :, DT_RANK:]
    dt_sum = dot(dt_in, part_dt_proj, high) + part_dt_bias
    step = jax.nn.softplus(dt_sum)
    decay_step = jnp.where(in_seq_all == 0.0, 1e30, step * LOG2_E)
    inputs = step * act
    cube = (count, rep, channels)
    scanned, decayed, mout_mix = scan_forward(
        decay_step.reshape(cube), inputs.reshape(cube), maps, rate, mout_mix
    )
    scanned = scanned.reshape(group, channels)
    mout_mix = mout_mix.reshape(fsdp, -1, width)
    full_mout = mout_mix[:, : part_mout.shape[0]].reshape(-1, width)
    half_mix = mout_mix[:, part_mout.shape[0] :]
    silu_z, z_slope = silu_and_slope(gate_z)
    before_gate = scanned + part_skip * act
    mixer_low = swapped((before_gate * silu_z).astype(bf16).reshape(cube))
    ssm_part = by_row(dot(mixer_low, full_mout).astype(bf16)).reshape(rep, count, width)
    (ssm_out,) = rep_exchange(rep, 3, sums=(ssm_part,))

    attended_values, log_total = attention_forward(qkv_low, allowed)
    half_mix, qkv_low = lax.optimization_barrier((half_mix, qkv_low))
    full_mix = pair_gather(9, half_mix).reshape(width, width)
    mixed, mix_pull = jax.vjp(mix_branches, attended_values, ssm_out, norm_attn, norm_ssm)
    mixed_low = mixed.astype(bf16)
    middle = hidden_in + dot(mixed_low, full_mix)
    ffn_in, ffn_pull = jax.vjp(rms_norm, middle, norm_ffn)
    ffn_all, mixed_all = rep_exchange(rep, 4, gathers=(ffn_in.astype(bf16), mixed_low))
    ffn_all, mixed_all = ffn_all.reshape(group, width), mixed_all.reshape(group, width)

    gate_up = dot(ffn_all, full_gate_up)
    hidden, swiglu_pull = jax.vjp(swiglu, gate_up[:, :ff_part], gate_up[:, ff_part:])
    hidden_low = hidden.astype(bf16)
    grad_hidden = dot_right_t(cot_all, full_down)
    grad_gate_up = jnp.concatenate(swiglu_pull(grad_hidden), axis=1).astype(bf16)
    part_gate_up = dot_left_t(ffn_all, grad_gate_up).astype(bf16)
    own_gate_up = line_scatter(part_gate_up)
    grad_gate_up = tied(grad_gate_up, part_gate_up)
    ffn_sent = by_row(dot_right_t(grad_gate_up, full_gate_up).astype(bf16))
    part_down = dot_left_t(hidden_low, cot_all).astype(bf16)
    own_down = line_scatter(part_down)
    down_sent = by_row(dot(tied(hidden_low, part_down), full_down).astype(bf16))
    blocks = (rep, count, width)
    grad_ffn, down_out = rep_exchange(
        rep, 5, sums=(ffn_sent.reshape(blocks), down_sent.reshape(blocks))
    )
    result = middle + down_out

    grad_middle_norm, grad_norm_ffn = ffn_pull(grad_ffn)
    grad_middle = cot_rows + grad_middle_norm
    middle_low = grad_middle.astype(bf16)
    grad_mixed = dot_right_t(middle_low, full_mix)
    grad_attended, grad_ssm, grad_norm_attn, grad_norm_ssm = mix_pull(grad_mixed)
    middle_sent = middle_low.reshape(count, rep, -1).transpose(1, 0, 2)
    qkv_grad = attention_backward(qkv_low, grad_attended.astype(bf16), log_total, allowed)
    qkv_grad = qkv_grad.astype(bf16).reshape(count, rep, -1).transpose(1, 0, 2)
    ssm_all, middle_cols, qkv_cols = rep_exchange(
        rep, 6, gathers=(grad_ssm.astype(bf16),), trades=(middle_sent, qkv_grad)
    )
    qkv_cols = qkv_cols.reshape(group, qkv_part)
    ssm_all = tied(ssm_all, own_gate_up).reshape(group, width)
    grad_mixer = dot_right_t(ssm_all, full_mout).reshape(rep, count, channels)
    grad_mixer = swapped(grad_mixer)
    part_mout = dot_left_t(mixer_low, ssm_all).astype(bf16)
    part_mix = dot_left_t(mixed_all, middle_cols.reshape(group, -1)).astype(bf16)

    grad_z = (grad_mixer * before_gate * z_slope).astype(bf16)
    grad_z = swapped(grad_z.reshape(cube))
    spare = early_width - qkv_part - channels
    early_grad = jnp.concatenate([qkv_cols, jnp.zeros((group, spare), bf16), grad_z], axis=1)
    part_early = dot_left_t(normed_all, early_grad).astype(bf16)
    grad_mixer = tied(grad_mixer, part_mout, part_mix, part_early, own_down)
    own_mout, own_mix = line_scatter(part_mout), line_scatter(part_mix)
    own_early = line_scatter(part_early)
    grad_before = grad_mixer * silu_z
    grad_skip = jnp.sum(grad_before * act, axis=0)
    grad_inputs, grad_step, grad_rate, grad_maps, all_gate_up = scan_backward(
        *(item.reshape(cube) for item in (decay_step, step, inputs)),
        maps,
        grad_before.reshape(cube),
        decayed,
        rate,
        rep,
        7,
        own_gate_up,
    )
    grad_inputs = grad_inputs.reshape(group, channels)
    grad_step = grad_step.reshape(group, channels)
    grad_a_log = grad_rate * rate
    grad_step = grad_step + grad_inputs * act
    grad_dt = grad_step * jax.nn.sigmoid(dt_sum)
    grad_dt_bias = jnp.sum(grad_dt, axis=0)
    grad_dt_proj = dot_left_t(dt_in, grad_dt)
    proj_sent = jnp.concatenate(
        [dot_right_t(grad_dt, part_dt_proj), grad_maps], axis=1
    )
    proj_sent = proj_sent.reshape(count, rep, -1).transpose(1, 0, 2)
    (grad_proj,) = rep_exchange(rep, 11, alls=(proj_sent,))
    grad_proj = swapped(tied(grad_proj, own_mout, own_mix))
    grad_x_proj = dot_left_t(grad_proj, act)
    grad_act = grad_before * part_skip + grad_inputs * step + dot_right_t(grad_proj, part_x_proj)
    grad_conv = grad_act * act_slope
    grad_conv_b = jnp.sum(grad_conv, axis=0)
    grad_conv_w = [jnp.sum(grad_conv * xs, axis=0)]
    grad_xs = grad_conv * conv_w[CONV - 1]
    for k in range(1, CONV):
        reached = jnp.where(in_seq_all >= k, grad_conv, 0.0)
        grad_conv_w.insert(0, jnp.sum(reached * shift_down(xs, k * rep), axis=0))
        grad_xs = grad_xs + shift_up(reached, k * rep) * conv_w[CONV - 1 - k]
    small = jnp.concatenate(
        [jnp.stack(grad_conv_w), grad_conv_b[None], grad_dt_bias[None], grad_skip[None]]
        + [grad_a_log, grad_dt_proj, grad_x_proj],
        axis=0,
    )
    n_small = fsdp * up16(-(-small.shape[0] // fsdp))
    small = jnp.pad(small, ((0, n_small - small.shape[0]), (0, 0))).astype(bf16)
    grad_xs = swapped(grad_xs.astype(bf16).reshape(cube))
    gap = jnp.zeros((group, gate_at - channels - qkv_part), bf16)
    end = jnp.zeros((group, in_width - gate_at - channels), bf16)
    in_grad = jnp.concatenate([grad_xs, qkv_cols, gap, grad_z, end], axis=1)
    normed_part = by_row(dot_right_t(in_grad, full_in).astype(bf16)).reshape(blocks)
    own_late = line_scatter(dot_left_t(normed_all, grad_xs).astype(bf16))
    (grad_normed,) = rep_exchange(rep, 8, sums=(normed_part,))
    grad_hidden_norm, grad_norm_in = norm_in_pull(grad_normed)
    grad_hidden_in = grad_middle + grad_hidden_norm

    def given_back(rows):
        return dot_left_t(picks, rows.astype(bf16)).astype(bf16).reshape(fsdp, block_rows, width)

    gains = jnp.stack([grad_norm_in, grad_norm_attn, grad_norm_ssm, grad_norm_ffn])
    gains = jnp.concatenate([gains, jnp.zeros((4, width), f32)], axis=0)
    (
        all_mout,
        all_mix,
        all_early,
        all_late,
        all_down,
        small,
        gains,
        mixed_out,
        grad_tokens,
    ) = last_exchange(
        rep,
        fsdp,
        10,
        (own_mout, own_mix, own_early, own_late, own_down),
        small.reshape(fsdp, -1, channels),
        gains,
        (given_back(result), given_back(grad_hidden_in)),
    )
    gains, small = jnp.sum(gains, axis=0), small.reshape(rep, n_small, channels)
    all_gate_up = tied(all_gate_up, all_late)
    sum_gate, sum_up = join_columns(
        rep,
        (all_gate_up,),
        (w_gate.shape[1], w_up.shape[1]),
        (((0, 0, ff_piece, 0, fsdp),), ((0, ff_part, ff_piece, 0, fsdp),)),
    )
    sum_mamba_in, sum_qkv, sum_mix = join_columns(
        rep,
        (all_late, all_early, all_mix),
        (w_mamba_in.shape[1], w_qkv.shape[1], width),
        (
            ((0, 0, piece, 0, fsdp), (1, early_width - channels, piece, INNER, fsdp)),
            ((1, 0, qkv_part, 0, 1),),
            ((2, 0, width // rep, 0, 1),),
        ),
    )
    sum_down = join_rows(rep, all_down, w_down.shape[0], width, flip=True).T
    sum_mout = join_rows(rep, all_mout, w_mamba_out.shape[0], width)

    (small,) = join_columns(rep, (small,), (INNER,), (((0, 0, piece, 0, fsdp),),))
    ends = [CONV, CONV + 1, CONV + 2, CONV + 3, CONV + 3 + STATE, CONV + 3 + STATE + DT_RANK]
    ends.append(ends[-1] + x_proj.shape[1])
    return (
        mixed_out.reshape(count, width),
        grad_tokens.reshape(count, width),
        gains[0],
        sum_qkv,
        sum_mamba_in,
        small[: ends[0]],
        small[ends[0]],
        small[ends[5] : ends[6]].T,
        small[ends[4] : ends[5]],
        small[ends[1]],
        small[ends[3] : ends[4]],
        small[ends[2]],
        sum_mout,
        gains[1],
        gains[2],
        sum_mix,
        gains[3],
        sum_gate,
        sum_up,
        sum_down,
    )


def solution(mesh):
    rows = P(("rep", "fsdp"), None)
    cut = P("fsdp", None)
    whole = P()
    return jax.shard_map(
        functools.partial(per_device, mesh.shape["rep"], mesh.shape["fsdp"]),
        mesh=mesh,
        in_specs=(rows,) * 4
        + (whole, cut, cut)
        + (whole,) * 7
        + (cut, whole, whole, cut, whole, cut, cut, cut),
        out_specs=(rows, rows, whole, cut, cut)
        + (whole,) * 7
        + (cut, whole, whole, cut, whole, cut, cut, cut),
        check_vma=False,
    )
```

```python
import functools

import jax
import jax.numpy as jnp
from jax import lax
from jax.experimental import pallas as pl
from jax.experimental.layout import Layout, with_layout_constraint
from jax.experimental.pallas import tpu as pltpu
from jax.sharding import PartitionSpec as P

HEADS = 25
KV_HEADS = 5
HEAD_DIM = 64
INNER = 3200
STATE = 16
DT_RANK = 100
CONV = 4
WINDOW = 1024
LANES = 128
PACKS = 8
LOG2_E = 1.4426950408889634

epsilon = 1e-06
bf16 = jnp.bfloat16
f32 = jnp.float32


def dot(left, right, precision=None):
    return jnp.dot(left, right, precision=precision, preferred_element_type=f32)


def dot_right_t(left, right):
    return lax.dot_general(left, right, (((1,), (1,)), ((), ())), preferred_element_type=f32)


def dot_left_t(left, right):
    return lax.dot_general(left, right, (((0,), (0,)), ((), ())), preferred_element_type=f32)


def rms_norm(value_rows, gain):
    return (
        value_rows
        * lax.rsqrt(jnp.mean(value_rows * value_rows, axis=-1, keepdims=True) + epsilon)
        * gain
    )


def mix_branches(attended_values, ssm_out, norm_attn, norm_ssm):
    return (rms_norm(attended_values, norm_attn) + rms_norm(ssm_out, norm_ssm)) * 0.5


def swiglu(gate_val, up_val):
    return jax.nn.silu(gate_val) * up_val


def hbm_spec():
    return pl.BlockSpec(memory_space=pl.ANY)


def vmem_spec():
    return pl.BlockSpec(memory_space=pltpu.VMEM)


SMALL_COST = pl.CostEstimate(flops=0, bytes_accessed=10**4, transcendentals=0)


def send(src, dst, sems, axis, target):
    copy = pltpu.make_async_remote_copy(
        src_ref=src,
        dst_ref=dst,
        send_sem=sems[0],
        recv_sem=sems[1],
        device_id={axis: target},
        device_id_type=pl.DeviceIdType.MESH,
    )
    copy.start()
    return copy


def meet(axis, others):
    barrier = pltpu.get_barrier_semaphore()
    for other in others:
        pl.semaphore_signal(
            barrier, inc=1, device_id={axis: other}, device_id_type=pl.DeviceIdType.MESH
        )
    pl.semaphore_wait(barrier, len(others))


def rep_kernel(rep, counts, square, *refs):
    n_gather, n_sum, n_all, n_trade = counts
    chips = rep // 2
    refs = list(refs)

    def take(n):
        taken = refs[:n]
        del refs[:n]
        return taken

    gathers, sums, alls, trades = (take(n) for n in counts)
    gathered, summed, all_summed, traded = (take(n) for n in counts)
    reduced = sums + alls
    buffers = [take(3) for _ in reduced]
    totals = summed + take(n_all)
    local, far, near, direct = refs

    me = lax.axis_index("rep")
    core = lax.rem(me, 2)
    chip = (me - core) // 2
    partner = 2 * chip + 1 - core
    ahead = [lax.rem(chip + k, chips) for k in range(chips)]
    behind = [lax.rem(chip + chips - k, chips) for k in range(chips)]
    if square:
        along_x, along_y = chip + 1 - 2 * lax.rem(chip, 2), lax.rem(chip + 2, 4)
        first = along_x + core * (along_y - along_x)
        second = along_y + core * (along_x - along_y)
        across = 3 - chip
        linked = [2 * first + core, 2 * second + core]
    else:
        linked = [2 * ahead[k] + core for k in range(1, chips)]
    if n_trade:
        meet("rep", [lax.rem(me + k, rep) for k in range(1, rep)])
    else:
        meet("rep", linked + [partner])

    kept, sent = [], []

    def keep(src, dst):
        copy = pltpu.make_async_copy(src, dst, local.at[len(kept)])
        copy.start()
        kept.append(copy)

    def far_send(src, dst, slot, k, target):
        copy = send(src, dst, (far.at[0, slot, k], far.at[1, slot, k]), "rep", 2 * target + core)
        sent.append(copy)
        return copy

    def near_send(src, dst, slot, k):
        copy = send(src, dst, (near.at[0, slot, k], near.at[1, slot, k]), "rep", partner)
        sent.append(copy)
        return copy

    def start_gather(source, out, slot):
        if square:
            far_copies = [
                far_send(source, out.at[me], slot, 1, first),
                far_send(source, out.at[me], slot, 2, second),
            ]
        else:
            far_copies = [
                far_send(source, out.at[me], slot, k, ahead[k]) for k in range(1, chips)
            ]
        near_copies = [near_send(source, out.at[me], slot, 0)]
        keep(source, out.at[me])
        return out, slot, far_copies, near_copies

    def pass_on(states):
        if square:
            for out, slot, far_copies, near_copies in states:
                block = out.at[2 * first + core]
                far_copies[0].wait_recv()
                far_copies.append(far_send(block, block, slot, 3, second))
                near_copies.append(near_send(block, block, slot, 1))
            for out, slot, far_copies, near_copies in states:
                for k, source in ((2, second), (3, across)):
                    block = out.at[2 * source + core]
                    far_copies[k - 1].wait_recv()
                    near_copies.append(near_send(block, block, slot, k))
        else:
            for out, slot, far_copies, near_copies in states:
                for k in range(1, chips):
                    block = out.at[2 * behind[k] + core]
                    far_copies[k - 1].wait_recv()
                    near_copies.append(near_send(block, block, slot, k))
        for _, _, _, near_copies in states:
            for copy in near_copies:
                copy.wait_recv()

    dests = [chip, first, across, second] if square else ahead
    partner_dests = [chip, second, across, first] if square else ahead
    order = [1, 2, 3, 0] if square else [*range(1, chips), 0]
    crossing = []
    for i, source in enumerate(reduced):
        from_partner = buffers[i][1]
        crossing.append(
            {
                k: near_send(source.at[2 * partner_dests[k] + 1 - core], from_partner.at[k], i, k)
                for k in order
            }
        )
    states = [
        start_gather(source, gathered[i], len(reduced) + n_all + i)
        for i, source in enumerate(gathers)
    ]
    trading = []
    for i, source in enumerate(trades):
        keep(source.at[me], traded[i].at[me])
        for k in range(1, rep):
            target = lax.rem(me + k, rep)
            copy = send(
                source.at[target],
                traded[i].at[me],
                (direct.at[0, i, k], direct.at[1, i, k]),
                "rep",
                target,
            )
            trading.append(copy)

    def of_chip(i, k):
        crossing[i][k].wait_recv()
        own = reduced[i][2 * dests[k] + core]
        return own.astype(f32) + buffers[i][1][k].astype(f32)

    crossed = []
    for i in range(len(reduced)):
        low, _, arrived = buffers[i]
        copies = []
        for k in (1, 2) if square else range(1, chips):
            low[k - 1] = of_chip(i, k).astype(low.dtype)
            target = first if square else ahead[k]
            copies.append(far_send(low.at[k - 1], arrived.at[k - 1], i, k, target))
        crossed.append(copies)
    if square:
        for i in range(len(reduced)):
            low, _, arrived = buffers[i]
            value = of_chip(i, 3)
            crossed[i][1].wait_recv()
            low[2] = (value + arrived[1].astype(f32)).astype(low.dtype)
            crossed[i].append(far_send(low.at[2], arrived.at[2], i, 3, second))
    for i in range(len(reduced)):
        arrived = buffers[i][2]
        total = of_chip(i, 0)
        for k in (1, 3) if square else range(1, chips):
            crossed[i][k - 1].wait_recv()
            total = total + arrived[k - 1].astype(f32)
        totals[i][...] = total
        if i >= n_sum:
            states.append(start_gather(totals[i], all_summed[i - n_sum], n_all + i))
    pass_on(states)
    for copy in trading:
        copy.wait()
    for copy in sent:
        copy.wait_send()
    for copy in kept:
        copy.wait()


def rep_exchange(rep, collective_id, gathers=(), sums=(), alls=(), trades=()):
    chips = rep // 2
    square = rep == 8 and not alls
    counts = (len(gathers), len(sums), len(alls), len(trades))
    reduced = (*sums, *alls)
    out_shape = [jax.ShapeDtypeStruct((rep,) + x.shape, x.dtype) for x in gathers]
    out_shape += [jax.ShapeDtypeStruct(x.shape[1:], f32) for x in sums]
    out_shape += [jax.ShapeDtypeStruct(x.shape, f32) for x in alls]
    out_shape += [jax.ShapeDtypeStruct(x.shape, x.dtype) for x in trades]
    scratch = []
    for x in reduced:
        scratch += [
            pltpu.VMEM((n,) + x.shape[1:], x.dtype) for n in (chips - 1, chips, chips - 1)
        ]
    scratch += [pltpu.VMEM(x.shape[1:], f32) for x in alls]
    n_local = sum(counts) - len(sums) + 1
    n_slots = len(reduced) + len(alls) + len(gathers) + 1
    scratch += [
        pltpu.SemaphoreType.DMA((n_local,)),
        pltpu.SemaphoreType.DMA((2, n_slots, chips)),
        pltpu.SemaphoreType.DMA((2, n_slots, chips)),
        pltpu.SemaphoreType.DMA((2, len(trades) + 1, rep)),
    ]
    return pl.pallas_call(
        functools.partial(rep_kernel, rep, counts, square),
        out_shape=out_shape,
        in_specs=[vmem_spec()] * sum(counts),
        out_specs=[hbm_spec()] * len(gathers)
        + [vmem_spec()] * len(sums)
        + [hbm_spec()] * (len(alls) + len(trades)),
        scratch_shapes=scratch,
        compiler_params=pltpu.CompilerParams(
            collective_id=collective_id,
            has_side_effects=True,
            vmem_limit_bytes=40 * 1024 * 1024,
        ),
        cost_estimate=SMALL_COST,
    )(*gathers, *sums, *alls, *trades)


def line_kernel(count, counts, *refs):
    n_gather, n_all, n_trade = counts
    n_in = sum(counts)
    ins, outs, scratch = refs[:n_in], refs[n_in : 2 * n_in], refs[2 * n_in :]
    arrived, totals = scratch[:n_all], scratch[n_all : 2 * n_all]
    local, remote = scratch[2 * n_all :]
    me = lax.axis_index("fsdp")
    others = [lax.rem(me + k, count) for k in range(1, count)]
    meet("fsdp", others)
    copies, coming = [], []

    def push(block, out, slot):
        return [
            send(block(other), out, (remote.at[0, slot, k], remote.at[1, slot, k]), "fsdp", other)
            for k, other in enumerate(others)
        ]

    def keep(block, out, slot):
        copy = pltpu.make_async_copy(block, out, local.at[slot])
        copy.start()
        copies.append(copy)

    for i in range(n_all):
        source = ins[n_gather + i]
        coming.append(push(lambda other: source.at[other], arrived[i].at[me], n_in + i))
    for i in range(n_in):
        if i < n_gather:
            keep(ins[i], outs[i].at[me], i)
            copies += push(lambda other: ins[i], outs[i].at[me], i)
        elif i >= n_gather + n_all:
            keep(ins[i].at[me], outs[i].at[me], i)
            copies += push(lambda other: ins[i].at[other], outs[i].at[me], i)
    for i in range(n_all):
        for copy in coming[i]:
            copy.wait()
        total = ins[n_gather + i][me].astype(f32)
        for other in others:
            total = total + arrived[i][other].astype(f32)
        totals[i][...] = total.astype(totals[i].dtype)
        out = outs[n_gather + i]
        keep(totals[i], out.at[me], n_gather + i)
        copies += push(lambda other: totals[i], out.at[me], n_gather + i)
    for copy in copies:
        copy.wait()


def line_exchange(count, collective_id, gathers=(), alls=(), trades=()):
    arrays = (*gathers, *alls, *trades)
    out_shape = [jax.ShapeDtypeStruct((count,) + x.shape, x.dtype) for x in gathers]
    out_shape += [jax.ShapeDtypeStruct(x.shape, x.dtype) for x in (*alls, *trades)]
    return pl.pallas_call(
        functools.partial(line_kernel, count, (len(gathers), len(alls), len(trades))),
        out_shape=out_shape,
        in_specs=[vmem_spec()] * len(arrays),
        out_specs=[hbm_spec()] * len(arrays),
        scratch_shapes=[pltpu.VMEM(x.shape, x.dtype) for x in alls]
        + [pltpu.VMEM(x.shape[1:], x.dtype) for x in alls]
        + [
            pltpu.SemaphoreType.DMA((len(arrays),)),
            pltpu.SemaphoreType.DMA((2, len(arrays) + len(alls), count)),
        ],
        compiler_params=pltpu.CompilerParams(collective_id=collective_id, has_side_effects=True),
        cost_estimate=SMALL_COST,
    )(*arrays)


def remote_copy(src, dst, sems, axis, target):
    return pltpu.make_async_remote_copy(
        src_ref=src,
        dst_ref=dst,
        send_sem=sems[0],
        recv_sem=sems[1],
        device_id={axis: target},
        device_id_type=pl.DeviceIdType.MESH,
    )


class Gathers:
    def __init__(self, rep):
        chips, self.square = rep // 2, rep == 8
        self.me = lax.axis_index("rep")
        self.core = lax.rem(self.me, 2)
        chip = (self.me - self.core) // 2
        self.partner = 2 * chip + 1 - self.core
        if self.square:
            along_x, along_y = chip + 1 - 2 * lax.rem(chip, 2), lax.rem(chip + 2, 4)
            first = along_x + self.core * (along_y - along_x)
            second = along_y + self.core * (along_x - along_y)
            hops, sources = [first, second], [first, second, 3 - chip]
        else:
            hops = [lax.rem(chip + k, chips) for k in range(1, chips)]
            sources = [lax.rem(chip + chips - k, chips) for k in range(1, chips)]
        self.hops = [2 * hop + self.core for hop in hops]
        self.sources = [2 * source + self.core for source in sources]

    def plan(self, source, out, far, near, local, i):
        blocks = [out.at[origin] for origin in self.sources]

        def over(sems, src, dst, k, target):
            return remote_copy(src, dst, (sems.at[0, i, k], sems.at[1, i, k]), "rep", target)

        own = [over(far, source, out.at[self.me], k, hop) for k, hop in enumerate(self.hops)]
        if self.square:
            own.append(over(far, blocks[0], blocks[0], 2, self.hops[1]))
        across = [over(near, block, block, k, self.partner) for k, block in enumerate(blocks)]
        across.append(over(near, source, out.at[self.me], len(blocks), self.partner))
        return own, across, pltpu.make_async_copy(source, out.at[self.me], local.at[i])

    def begin(self, plan):
        own, across, keep = plan
        for copy in own[: len(self.hops)]:
            copy.start()
        across[-1].start()
        keep.start()

    def first_hop(self, plan):
        own, across, _ = plan
        own[0].wait_recv()
        if self.square:
            own[2].start()
        across[0].start()

    def second_hop(self, plan):
        own, across, _ = plan
        for k in range(1, len(self.hops)):
            own[k].wait_recv()
            across[k].start()

    def relayed(self, plan):
        own, across, _ = plan
        if self.square:
            own[2].wait_recv()
            across[2].start()

    def end(self, plan):
        own, across, keep = plan
        for copy in across:
            copy.wait()
        for copy in own:
            copy.wait_send()
        keep.wait()


def last_kernel(rep, fsdp, square, n_gather, layout, down_rows, *refs):
    parts_gate_up, parts_down, refs = refs[0], refs[1], refs[2:]
    gathers, refs = refs[:n_gather], refs[n_gather:]
    small, gains, trades, refs = refs[0], refs[1], refs[2:4], refs[4:]
    joined_gate, joined_up, joined_down, refs = refs[0], refs[1], refs[2], refs[3:]
    gathered, refs = refs[:n_gather], refs[n_gather:]
    small_out, gains_out, traded, refs = refs[0], refs[1], refs[2:4], refs[4:]
    arrived, total, lined, gains_in, gains_sum, local, far, near, keeping, remote = refs

    line = lax.axis_index("fsdp")
    others = [lax.rem(line + k, fsdp) for k in range(1, fsdp)]
    along = Gathers(rep)

    def push(block, out, slot):
        return [
            remote_copy(
                block(other), out, (remote.at[0, slot, k], remote.at[1, slot, k]), "fsdp", other
            )
            for k, other in enumerate(others)
        ]

    gains_plan = along.plan(gains, gains_in, far, near, local, 0)
    plans = [
        along.plan(gathers[i], gathered[i], far, near, local, 1 + i) for i in range(n_gather)
    ]
    small_plan = along.plan(lined, small_out, far, near, local, 1 + n_gather)
    small_in = push(lambda other: small.at[other], arrived.at[line], 0)
    small_back = push(lambda other: total, lined.at[line], 3)
    gains_push = push(lambda other: gains_sum, gains_out.at[line], 4)
    gains_keep = pltpu.make_async_copy(gains_sum, gains_out.at[line], keeping.at[2])
    traffic = []
    for i in range(2):
        source = trades[i]
        traffic += push(lambda other: source.at[other], traded[i].at[line], 1 + i)
        traffic.append(
            pltpu.make_async_copy(source.at[line], traded[i].at[line], keeping.at[i])
        )
    step, steps = pl.program_id(0), pl.num_programs(0)

    @pl.when(step == 0)
    def _():
        barrier = pltpu.get_barrier_semaphore()
        met = [("rep", index) for index in (*along.hops, along.partner)]
        met += [("fsdp", index) for index in others]
        for axis, index in met:
            pl.semaphore_signal(
                barrier, inc=1, device_id={axis: index}, device_id_type=pl.DeviceIdType.MESH
            )
        pl.semaphore_wait(barrier, len(met))
        for copy in small_in:
            copy.start()
        along.begin(gains_plan)
        for plan in plans:
            along.begin(plan)
        for copy in traffic:
            copy.start()

    join_kernel(rep, layout, parts_gate_up, joined_gate, joined_up)
    join_rows_kernel(rep, down_rows, True, parts_down, joined_down)

    @pl.when(step == steps - 1)
    def _():
        for copy in small_in:
            copy.wait()
        value = small[line].astype(f32)
        for other in others:
            value = value + arrived[other].astype(f32)
        total[...] = value.astype(total.dtype)
        for copy in small_back:
            copy.start()
        lined[line] = total[...]
        for plan in (gains_plan, *plans):
            along.first_hop(plan)
        for plan in (gains_plan, *plans):
            along.second_hop(plan)
        along.relayed(gains_plan)
        along.end(gains_plan)
        gains_sum[...] = jnp.sum(gains_in[...], axis=0)
        for copy in gains_push:
            copy.start()
        gains_keep.start()
        for copy in small_back:
            copy.wait()
        along.begin(small_plan)
        for plan in plans:
            along.relayed(plan)
        along.first_hop(small_plan)
        along.second_hop(small_plan)
        along.relayed(small_plan)
        for plan in (*plans, small_plan):
            along.end(plan)
        for copy in (*traffic, *gains_push, gains_keep):
            copy.wait()


def last_exchange(rep, fsdp, collective_id, ffn, gathers, small, gains, trades):
    n_gather, chips = len(gathers), rep // 2
    parts_gate_up, parts_down, ff_width, ff_rows = ffn
    rows, ff_part, width = parts_gate_up.shape[1], parts_gate_up.shape[2] // 2, gains.shape[1]
    block, columns = next(n for n in (80, 40, 64, rows) if rows % n == 0), 2 * LANES
    steps, row_steps = pl.cdiv(width, columns), rows // block
    rest = ff_width // rep // fsdp
    layout = (((0, 0, rest, 0, fsdp),), ((0, ff_part, rest, 0, fsdp),))

    def row_at(i):
        return lax.div(i * row_steps, steps)

    out_shape = [jax.ShapeDtypeStruct((rows, ff_width), bf16)] * 2
    out_shape.append(jax.ShapeDtypeStruct((width, ff_rows), bf16))
    out_shape += [jax.ShapeDtypeStruct((rep,) + x.shape, x.dtype) for x in gathers]
    out_shape.append(jax.ShapeDtypeStruct((rep,) + small.shape, small.dtype))
    out_shape.append(jax.ShapeDtypeStruct((fsdp,) + gains.shape, gains.dtype))
    out_shape += [jax.ShapeDtypeStruct(x.shape, x.dtype) for x in trades]
    return pl.pallas_call(
        functools.partial(
            last_kernel, rep, fsdp, rep == 8, n_gather, layout, ff_rows // rep
        ),
        grid=(steps,),
        out_shape=out_shape,
        in_specs=[
            pl.BlockSpec((rep, block, 2 * ff_part), lambda i: (0, row_at(i), 0)),
            pl.BlockSpec((rep, parts_down.shape[1], columns), lambda i: (0, 0, i)),
        ]
        + [vmem_spec()] * (n_gather + 4),
        out_specs=[pl.BlockSpec((block, ff_width), lambda i: (row_at(i), 0))] * 2
        + [pl.BlockSpec((columns, ff_rows), lambda i: (i, 0))]
        + [hbm_spec()] * (n_gather + 4),
        scratch_shapes=[
            pltpu.VMEM(small.shape, small.dtype),
            pltpu.VMEM(small.shape[1:], small.dtype),
            pltpu.VMEM(small.shape, small.dtype),
            pltpu.VMEM((rep,) + gains.shape, gains.dtype),
            pltpu.VMEM(gains.shape, gains.dtype),
            pltpu.SemaphoreType.DMA((n_gather + 2,)),
            pltpu.SemaphoreType.DMA((2, n_gather + 2, chips)),
            pltpu.SemaphoreType.DMA((2, n_gather + 2, chips)),
            pltpu.SemaphoreType.DMA((3,)),
            pltpu.SemaphoreType.DMA((2, 5, fsdp)),
        ],
        compiler_params=pltpu.CompilerParams(
            collective_id=collective_id,
            has_side_effects=True,
            vmem_limit_bytes=48 * 1024 * 1024,
        ),
        cost_estimate=SMALL_COST,
    )(parts_gate_up, parts_down, *gathers, small, gains, *trades)


def hand_kernel(_value, _after, _out):
    pass


def hand_on(value, after):
    return pl.pallas_call(
        hand_kernel,
        out_shape=jax.ShapeDtypeStruct(value.shape, value.dtype),
        in_specs=[hbm_spec()] * 2,
        out_specs=hbm_spec(),
        input_output_aliases={0: 0},
        cost_estimate=SMALL_COST,
    )(value, after)


def windows(width, pieces, start, step, rest):
    wide = min(-(-(rest + LANES - 1) // LANES) * LANES, width)
    me = lax.axis_index("rep")
    for i in range(pieces):
        at = start + i * step + me * rest
        aligned = jnp.minimum((at // LANES) * LANES, (width - wide) // LANES * LANES)
        yield pl.multiple_of(aligned, LANES), at - aligned, wide


def up16(size):
    return -(-size // 16) * 16


def copy_parts(rep, fsdp, source, out, place, start, total):
    rest = total // (rep * fsdp)
    rows = source.shape[0]
    for aligned, shift, wide in windows(source.shape[1], fsdp, start, rep * rest, rest):
        value = source[:, pl.ds(aligned, wide)].astype(f32)
        value = pltpu.roll(value, lax.rem(wide - shift, wide), 1)[:, :rest]
        if up16(rest) > rest:
            value = jnp.concatenate([value, jnp.zeros((rows, up16(rest) - rest), f32)], axis=1)
        out[:, place : place + up16(rest)] = value.astype(bf16)
        place += up16(rest)


def part_in_kernel(rep, fsdp, spots, qkv_ref, min_ref, out_ref):
    _, qkv_at, gate_at = spots
    rows, qkv_width = qkv_ref.shape
    qkv_part = qkv_width // rep
    out_ref[...] = jnp.zeros_like(out_ref)
    copy_parts(rep, fsdp, min_ref, out_ref, 0, 0, INNER)
    copy_parts(rep, fsdp, min_ref, out_ref, gate_at, INNER, INNER)
    value = qkv_ref[...].astype(f32)
    padded = -(-qkv_width // LANES) * LANES
    value = jnp.concatenate([value, jnp.zeros((rows, padded - qkv_width), f32)], axis=1)
    shift = padded - lax.axis_index("rep") * qkv_part
    value = pltpu.roll(value, lax.rem(shift, padded), 1)
    out_ref[:, qkv_at : qkv_at + qkv_part] = value[:, :qkv_part].astype(bf16)


def part_gate_up_kernel(rep, fsdp, gate_ref, up_ref, out_ref):
    copy_parts(rep, fsdp, gate_ref, out_ref, 0, 0, gate_ref.shape[1])
    copy_parts(rep, fsdp, up_ref, out_ref, out_ref.shape[1] // 2, 0, up_ref.shape[1])


def by_rows(kernel, sources, width):
    rows = sources[0].shape[0]
    block = 80 if rows % 80 == 0 else rows
    return pl.pallas_call(
        kernel,
        grid=(rows // block,),
        in_specs=[pl.BlockSpec((block, x.shape[1]), lambda i: (i, 0)) for x in sources],
        out_specs=pl.BlockSpec((block, width), lambda i: (i, 0)),
        out_shape=jax.ShapeDtypeStruct((rows, width), bf16),
        compiler_params=pltpu.CompilerParams(vmem_limit_bytes=40 * 1024 * 1024),
        cost_estimate=SMALL_COST,
    )(*sources)


def join_kernel(rep, layout, *refs):
    sources, outs = refs[: len(refs) - len(layout)], refs[len(refs) - len(layout) :]
    for out, entries in zip(outs, layout):
        for index, first, rest, place, pieces in entries:
            for i in range(pieces):
                start = first + i * up16(rest)
                for r in range(rep):
                    at = place + (i * rep + r) * rest
                    piece = sources[index][r, :, start : start + rest]
                    out[:, at : at + rest] = piece.astype(out.dtype)


def join_rows_kernel(rep, rows, flip, source, out):
    for r in range(rep):
        if flip:
            out[:, r * rows : (r + 1) * rows] = source[r].astype(f32).T[:, :rows].astype(out.dtype)
        else:
            out[r * rows : (r + 1) * rows, :] = source[r, :rows, :].astype(f32)


def join_rows(rep, source, total, width, flip=False):
    block = 2 * LANES
    shape = (total, width)
    out_spec = pl.BlockSpec((total, block), lambda i: (0, i))
    if flip:
        shape = (width, total)
        out_spec = pl.BlockSpec((block, total), lambda i: (i, 0))
    return pl.pallas_call(
        functools.partial(join_rows_kernel, rep, total // rep, flip),
        grid=(pl.cdiv(width, block),),
        in_specs=[pl.BlockSpec((rep, source.shape[1], block), lambda i: (0, 0, i))],
        out_specs=out_spec,
        out_shape=jax.ShapeDtypeStruct(shape, f32),
        compiler_params=pltpu.CompilerParams(vmem_limit_bytes=40 * 1024 * 1024),
        cost_estimate=SMALL_COST,
    )(source)


def join_columns(rep, sources, widths, layout):
    rows = sources[0].shape[1]
    block = next(n for n in (80, 40, 64, rows) if rows % n == 0)
    return pl.pallas_call(
        functools.partial(join_kernel, rep, layout),
        grid=(rows // block,),
        in_specs=[
            pl.BlockSpec((rep, block, x.shape[2]), lambda i: (0, i, 0)) for x in sources
        ],
        out_specs=[pl.BlockSpec((block, width), lambda i: (i, 0)) for width in widths],
        out_shape=[jax.ShapeDtypeStruct((rows, width), f32) for width in widths],
        compiler_params=pltpu.CompilerParams(vmem_limit_bytes=48 * 1024 * 1024),
        cost_estimate=SMALL_COST,
    )(*sources)


def spread_beside(rep, steps, pairs, local, far, near):
    along = Gathers(rep)
    plans = [along.plan(*pair, far, near, local, i) for i, pair in enumerate(pairs)]

    @pl.when(steps[0])
    def _():
        meet("rep", [*along.hops, along.partner])
        for plan in plans:
            along.begin(plan)

    @pl.when(steps[1])
    def _():
        for plan in plans:
            along.first_hop(plan)

    @pl.when(steps[2])
    def _():
        for plan in plans:
            along.second_hop(plan)

    def finish():
        for plan in plans:
            along.relayed(plan)
        for plan in plans:
            along.end(plan)

    return finish


def spread_maps(maps_ref, wide_ref, start):
    count, packs, columns = maps_ref.shape

    def spread(i, _):
        for u in range(2):
            t = 2 * i + u
            maps = maps_ref[t]
            for n in range(columns):
                wide_ref[n, start + t] = jnp.broadcast_to(maps[:, n : n + 1], (packs, LANES))
        return 0

    lax.fori_loop(0, count // 2, spread, 0)


def scan_kernel(
    rep,
    channels,
    decay_step_ref,
    input_ref,
    maps_ref,
    rate_ref,
    beside_ref,
    out_ref,
    decayed_ref,
    beside_out_ref,
    wide_ref,
    local,
    far,
    near,
):
    count, packs, _ = decay_step_ref.shape
    valid = (
        lax.broadcasted_iota(jnp.int32, (packs, LANES), 1)
        < channels - pl.program_id(1) * LANES
    )
    rate = jnp.where(valid[:1], rate_ref[...], 0.0)
    at = pl.program_id(0) * pl.num_programs(1) + pl.program_id(1)
    last = pl.num_programs(0) * pl.num_programs(1) - 1
    steps = [at == step for step in (0, 2 * last // 3, last)]
    finish = spread_beside(rep, steps, [(beside_ref, beside_out_ref)], local, far, near)

    @pl.when(pl.program_id(1) == 0)
    def _():
        spread_maps(maps_ref, wide_ref, 0)

    def step(i, states):
        for u in range(2):
            t = 2 * i + u
            decay_step = jnp.where(valid, decay_step_ref[t], 0.0)
            inputs = jnp.where(valid, input_ref[t], 0.0)
            out = jnp.zeros((packs, LANES), f32)
            new_states = []
            for n in range(STATE):
                decayed = jnp.exp2(decay_step * rate[n : n + 1]) * states[n]
                state = decayed + wide_ref[n, t] * inputs
                out = out + state * wide_ref[STATE + n, t]
                decayed_ref[n, t] = decayed
                new_states.append(state)
            out_ref[t] = out
            states = tuple(new_states)
        return states

    lax.fori_loop(0, count // 2, step, (jnp.zeros((packs, LANES), f32),) * STATE)
    pl.when(at == last)(finish)


def scan_forward(decay_step, inputs, maps, rate, rep, collective_id, beside):
    count, packs, channels = inputs.shape
    wide = pl.BlockSpec((count, PACKS, LANES), lambda g, i: (0, g, i))
    return pl.pallas_call(
        functools.partial(scan_kernel, rep, channels),
        grid=(packs // PACKS, pl.cdiv(channels, LANES)),
        in_specs=[
            wide,
            wide,
            pl.BlockSpec((count, PACKS, 2 * STATE), lambda g, i: (0, g, 0)),
            pl.BlockSpec((STATE, LANES), lambda g, i: (0, i)),
            hbm_spec(),
        ],
        out_specs=[
            wide,
            pl.BlockSpec((STATE, count, PACKS, LANES), lambda g, i: (0, 0, g, i)),
            hbm_spec(),
        ],
        out_shape=[
            jax.ShapeDtypeStruct(inputs.shape, f32),
            jax.ShapeDtypeStruct(
                (STATE, count, packs, pl.cdiv(channels, LANES) * LANES), f32
            ),
            jax.ShapeDtypeStruct((rep,) + beside.shape, beside.dtype),
        ],
        scratch_shapes=[
            pltpu.VMEM((2 * STATE, count, PACKS, LANES), f32),
            pltpu.SemaphoreType.DMA((1,)),
            pltpu.SemaphoreType.DMA((2, 1, rep // 2)),
            pltpu.SemaphoreType.DMA((2, 1, rep // 2)),
        ],
        compiler_params=pltpu.CompilerParams(
            collective_id=collective_id,
            has_side_effects=True,
            vmem_limit_bytes=48 * 1024 * 1024,
        ),
        cost_estimate=SMALL_COST,
    )(decay_step, inputs, maps, rate, beside)


def scan_back_kernel(
    rep,
    channels,
    decay_step_ref,
    step_ref,
    input_ref,
    maps_ref,
    grad_ref,
    decayed_ref,
    rate_ref,
    beside_ref,
    beside2_ref,
    grad_input_ref,
    grad_step_ref,
    grad_rate_ref,
    grad_maps_ref,
    beside_out_ref,
    beside2_out_ref,
    carry_ref,
    rates_ref,
    in_sum_ref,
    out_sum_ref,
    both_sum_ref,
    wide_ref,
    local,
    far,
    near,
):
    count, packs, _ = decay_step_ref.shape
    at = (pl.program_id(0) * pl.num_programs(1) + pl.program_id(1)) * pl.num_programs(2)
    at = at + pl.program_id(2)
    last = pl.num_programs(0) * pl.num_programs(1) * pl.num_programs(2) - 1
    steps = [at == step for step in (0, 10 * last // 16, 14 * last // 16)]
    pairs = [(beside_ref, beside_out_ref), (beside2_ref, beside2_out_ref)]
    finish = spread_beside(rep, steps, pairs, local, far, near)
    tile, chunk = pl.program_id(1), pl.program_id(2)
    start = (pl.num_programs(2) - 1 - chunk) * count
    valid = lax.broadcasted_iota(jnp.int32, (packs, LANES), 1) < channels - tile * LANES

    @pl.when(tile == 0)
    def _():
        spread_maps(maps_ref, wide_ref, start)
        zeros = jnp.zeros((STATE, count, packs, LANES), f32)
        in_sum_ref[:, pl.ds(start, count)] = zeros
        out_sum_ref[:, pl.ds(start, count)] = zeros
        both_sum_ref[pl.ds(start, count)] = zeros[0]

    @pl.when(chunk == 0)
    def _():
        carry_ref[...] = jnp.zeros_like(carry_ref)
        for n in range(STATE):
            rates_ref[n] = jnp.where(
                valid, jnp.broadcast_to(rate_ref[n : n + 1, :], (packs, LANES)), 0.0
            )

    def backward(back_t, carried):
        grad_states, grad_rates = carried
        t = count - 1 - back_t
        at = start + t
        decay_step = jnp.where(valid, decay_step_ref[t], 0.0)
        step = jnp.where(valid, step_ref[t], 0.0)
        inputs = jnp.where(valid, input_ref[t], 0.0)
        grad = jnp.where(valid, grad_ref[t], 0.0)
        both_sum_ref[at] += grad * inputs
        grad_input = grad_step = jnp.zeros((packs, LANES), f32)
        new_states, new_rates = [], []
        for n in range(STATE):
            decayed, rate = decayed_ref[n, t], rates_ref[n]
            grad_state = grad * wide_ref[STATE + n, at] + grad_states[n]
            out_sum_ref[n, at] += grad * decayed
            in_sum_ref[n, at] += grad_state * inputs
            grad_input = grad_input + grad_state * wide_ref[n, at]
            through = grad_state * decayed
            grad_step = grad_step + through * rate
            new_rates.append(grad_rates[n] + through * step)
            new_states.append(jnp.exp2(decay_step * rate) * grad_state)
        grad_input_ref[t] = grad_input
        grad_step_ref[t] = grad_step
        return (tuple(new_states), tuple(new_rates))

    carried = (
        tuple(carry_ref[n] for n in range(STATE)),
        tuple(carry_ref[STATE + n] for n in range(STATE)),
    )
    grad_states, grad_rates = lax.fori_loop(0, count, backward, carried)
    for n in range(STATE):
        carry_ref[n] = grad_states[n]
        carry_ref[STATE + n] = grad_rates[n]

    @pl.when(chunk == pl.num_programs(2) - 1)
    def _():
        for n in range(STATE):
            grad_rate_ref[n : n + 1, :] = jnp.sum(grad_rates[n], axis=0, keepdims=True)

    @pl.when(tile == pl.num_programs(1) - 1)
    def _():
        column = lax.broadcasted_iota(jnp.int32, (LANES, LANES), 1)
        here = pl.ds(start, count)

        def summed(value, place):
            return jnp.dot(
                value.reshape(count * packs, LANES).astype(bf16),
                (column == place).astype(bf16),
                preferred_element_type=f32,
            )

        total = summed(both_sum_ref[here], 2 * STATE)
        for n in range(STATE):
            total = total + summed(in_sum_ref[n, here], n)
            total = total + summed(out_sum_ref[n, here], STATE + n)
        grad_maps_ref[here] = total.reshape(count, packs, LANES)

    pl.when(at == last)(finish)


def scan_backward(decay_step, step, inputs, maps, grad, decayed, rate, rep, collective_id, beside):
    count, packs, channels = inputs.shape
    groups, chunks = packs // PACKS, 4
    part = count // chunks
    wide = pl.BlockSpec((part, PACKS, LANES), lambda g, i, c: (chunks - 1 - c, g, i))
    row = pl.BlockSpec((STATE, LANES), lambda g, i, c: (0, i))
    sums = pltpu.VMEM((STATE, count, PACKS, LANES), f32)
    grad_inputs, grad_step, grad_rate, grad_maps, *all_beside = pl.pallas_call(
        functools.partial(scan_back_kernel, rep, channels),
        grid=(groups, pl.cdiv(channels, LANES), chunks),
        in_specs=[
            wide,
            wide,
            wide,
            pl.BlockSpec((part, PACKS, 2 * STATE), lambda g, i, c: (chunks - 1 - c, g, 0)),
            wide,
            pl.BlockSpec(
                (STATE, part, PACKS, LANES), lambda g, i, c: (0, chunks - 1 - c, g, i)
            ),
            row,
        ]
        + [hbm_spec()] * 2,
        out_specs=[
            wide,
            wide,
            pl.BlockSpec((STATE, LANES), lambda g, i, c: (g, i)),
            pl.BlockSpec((count, PACKS, LANES), lambda g, i, c: (0, g, 0)),
        ]
        + [hbm_spec()] * 2,
        out_shape=[
            jax.ShapeDtypeStruct(inputs.shape, f32),
            jax.ShapeDtypeStruct(inputs.shape, f32),
            jax.ShapeDtypeStruct((groups * STATE, channels), f32),
            jax.ShapeDtypeStruct((count, packs, LANES), f32),
        ]
        + [jax.ShapeDtypeStruct((rep,) + x.shape, x.dtype) for x in beside],
        scratch_shapes=[
            pltpu.VMEM((2 * STATE, PACKS, LANES), f32),
            pltpu.VMEM((STATE, PACKS, LANES), f32),
            sums,
            sums,
            pltpu.VMEM((count, PACKS, LANES), f32),
            pltpu.VMEM((2 * STATE, count, PACKS, LANES), f32),
            pltpu.SemaphoreType.DMA((2,)),
            pltpu.SemaphoreType.DMA((2, 2, rep // 2)),
            pltpu.SemaphoreType.DMA((2, 2, rep // 2)),
        ],
        compiler_params=pltpu.CompilerParams(
            collective_id=collective_id,
            has_side_effects=True,
            vmem_limit_bytes=52 * 1024 * 1024,
        ),
        cost_estimate=SMALL_COST,
    )(decay_step, step, inputs, maps, grad, decayed, rate, *beside)
    grad_rate = jnp.sum(grad_rate.reshape(groups, STATE, channels), axis=0)
    in_maps, both = grad_maps[:, :, :STATE], grad_maps[:, :, 2 * STATE : 2 * STATE + 1]
    out_maps = grad_maps[:, :, STATE : 2 * STATE] + maps[:, :, :STATE] * both
    grad_maps = jnp.concatenate([in_maps, out_maps], axis=2).reshape(count * packs, 2 * STATE)
    return grad_inputs, grad_step, grad_rate, grad_maps, all_beside


def split_heads(qkv_low):
    count = qkv_low.shape[0]
    group_size = HEADS // KV_HEADS
    query_width = HEADS * HEAD_DIM
    kv_width = KV_HEADS * HEAD_DIM
    query_rows = qkv_low[:, :query_width].reshape(count, KV_HEADS, group_size, HEAD_DIM)
    key_rows = qkv_low[:, query_width : query_width + kv_width].reshape(count, KV_HEADS, HEAD_DIM)
    value_rows = qkv_low[:, query_width + kv_width :].reshape(count, KV_HEADS, HEAD_DIM)
    return (query_rows, key_rows, value_rows)


def masked_scores(query_rows, key_rows, allowed):
    attention_scores = jnp.einsum(
        "jzhx,kzx->zhjk", query_rows, key_rows, preferred_element_type=f32
    ) * HEAD_DIM ** (-0.5)
    return jnp.where(allowed[None, None], attention_scores, -1e30)


def attention_forward(qkv_low, allowed):
    count = qkv_low.shape[0]
    query_rows, key_rows, value_rows = split_heads(qkv_low)
    attention_scores = masked_scores(query_rows, key_rows, allowed)
    row_max = jnp.max(attention_scores, axis=-1, keepdims=True)
    weights_exp = jnp.exp(attention_scores - row_max)
    row_total = jnp.sum(weights_exp, axis=-1, keepdims=True)
    lowered_probabilities = (weights_exp / row_total).astype(bf16)
    attended_values = jnp.einsum(
        "lpho,ole->hlpe", lowered_probabilities, value_rows, preferred_element_type=f32
    )
    return (attended_values.reshape(count, HEADS * HEAD_DIM), row_max + jnp.log(row_total))


def attention_backward(qkv_low, grad_low, log_total, allowed):
    count = qkv_low.shape[0]
    query_rows, key_rows, value_rows = split_heads(qkv_low)
    probabilities = jnp.exp(masked_scores(query_rows, key_rows, allowed) - log_total)
    head_gradient = grad_low.reshape(count, KV_HEADS, HEADS // KV_HEADS, HEAD_DIM)
    grad_probs = jnp.einsum(
        "jzhx,kzx->zhjk", head_gradient, value_rows, preferred_element_type=f32
    )
    score_gradient = (
        probabilities * (grad_probs - jnp.sum(grad_probs * probabilities, axis=-1, keepdims=True))
    ).astype(bf16)
    scale_factor_scores = HEAD_DIM ** (-0.5)
    grad_queries = (
        jnp.einsum("lpho,ole->hlpe", score_gradient, key_rows, preferred_element_type=f32)
        * scale_factor_scores
    )
    grad_keys = (
        jnp.einsum("wniv,iwne->vwe", score_gradient, query_rows, preferred_element_type=f32)
        * scale_factor_scores
    )
    grad_values = jnp.einsum(
        "wniv,iwne->vwe", probabilities.astype(bf16), head_gradient, preferred_element_type=f32
    )
    return jnp.concatenate(
        [
            grad_queries.reshape(count, -1),
            grad_keys.reshape(count, -1),
            grad_values.reshape(count, -1),
        ],
        axis=1,
    )


def tied(value, *others):
    return lax.optimization_barrier((value,) + others)[0]


def by_row(value):
    return with_layout_constraint(value, Layout(major_to_minor=(0, 1)))


def silu_and_slope(value):
    gate = jax.nn.sigmoid(value)
    return value * gate, gate * (1.0 + value * (1.0 - gate))


def shift_down(rows, amount):
    return jnp.concatenate([jnp.zeros((amount,) + rows.shape[1:], rows.dtype), rows[:-amount]], 0)


def shift_up(rows, amount):
    return jnp.concatenate([rows[amount:], jnp.zeros((amount,) + rows.shape[1:], rows.dtype)], 0)


def per_device(
    rep,
    fsdp,
    tokens,
    cotangent,
    lengths,
    source_slot,
    norm_in,
    w_qkv,
    w_mamba_in,
    conv_weight,
    conv_bias,
    x_proj,
    dt_proj,
    dt_bias,
    a_log,
    d_skip,
    w_mamba_out,
    norm_attn,
    norm_ssm,
    w_mix_out,
    norm_ffn,
    w_gate,
    w_up,
    w_down,
):
    count, width = tokens.shape
    block_rows = count // fsdp
    piece, ff_piece = INNER // (rep * fsdp), w_gate.shape[1] // (rep * fsdp)
    channels, ff_part = fsdp * up16(piece), fsdp * up16(ff_piece)
    qkv_part = w_qkv.shape[1] // rep
    group = rep * count
    high = lax.Precision.HIGH
    me, line = lax.axis_index("rep"), lax.axis_index("fsdp")

    def my_part(value, axis):
        rest = value.shape[axis] // (rep * fsdp)
        spare = [(0, up16(rest) - rest if i == axis else 0) for i in range(value.ndim)]
        return jnp.concatenate(
            [
                jnp.pad(lax.dynamic_slice_in_dim(value, (i * rep + me) * rest, rest, axis), spare)
                for i in range(fsdp)
            ],
            axis=axis,
        )

    def my_rows(value):
        rest = value.shape[0] // rep
        part = lax.dynamic_slice_in_dim(value, me * rest, rest, 0)
        return jnp.pad(part, ((0, up16(rest) - rest), (0, 0)))

    def line_gather(value):
        return lax.all_gather(value, "fsdp", axis=0, tiled=True)

    def line_scatter(value):
        return lax.psum_scatter(value, "fsdp", scatter_dimension=0, tiled=True)

    def swapped(rows):
        lead = count if rows.shape[0] == count else rep
        return rows.transpose(1, 0, 2).reshape(group, rows.shape[2])

    early_width = -(-(qkv_part + channels) // LANES) * LANES
    gate_at = -(-(channels + qkv_part) // LANES) * LANES
    in_width = -(-(gate_at + channels) // LANES) * LANES
    part_in = by_rows(
        functools.partial(part_in_kernel, rep, fsdp, (0, channels, gate_at)),
        (w_qkv, w_mamba_in),
        in_width,
    )
    full_in = line_gather(part_in)
    mix_part = width // rep
    part_mix = lax.dynamic_slice_in_dim(w_mix_out, me * mix_part, mix_part, 1)
    mix_size = part_mix.size
    part_mix = jnp.pad(part_mix.reshape(-1), (0, -mix_size % (16 * width))).reshape(-1, width)
    part_mout, part_down = my_rows(w_mamba_out), my_rows(w_down)

    received, cot_received = line_exchange(
        fsdp,
        0,
        trades=(
            tied(tokens, part_in).reshape(fsdp, block_rows, width),
            cotangent.reshape(fsdp, block_rows, width),
        ),
    )
    w_gate, w_up, part_mout, part_mix, part_down, received = lax.optimization_barrier(
        (w_gate, w_up, part_mout, part_mix, part_down, received)
    )
    mout_mix = line_gather(jnp.concatenate([part_mout, part_mix], axis=0))
    part_gate_up = by_rows(
        functools.partial(part_gate_up_kernel, rep, fsdp), (w_gate, w_up), 2 * ff_part
    )
    full_gate_up, full_down = line_gather(part_gate_up), line_gather(part_down)
    slots = source_slot[0]
    picks = (slots[:, None] == jnp.arange(count, dtype=jnp.int32)[None, :]).astype(bf16)
    hidden_in = dot(picks, received.reshape(count, width))
    cot_rows = dot(picks, cot_received.reshape(count, width))
    cot_low = cot_rows.astype(bf16)

    ends = jnp.cumsum(lengths[0], dtype=jnp.int32)
    positions = jnp.arange(count, dtype=jnp.int32)
    passed = positions[:, None] >= ends[None, :-1]
    seg_ids = jnp.sum(passed.astype(jnp.int32), axis=1)
    in_seq = positions - jnp.max(jnp.where(passed, ends[None, :-1], 0), axis=1)
    distance = positions[:, None] - positions[None, :]
    allowed = (seg_ids[:, None] == seg_ids[None, :]) & (distance >= 0) & (distance < WINDOW)

    normed, norm_in_pull = jax.vjp(rms_norm, hidden_in, norm_in)
    marks = jnp.broadcast_to(in_seq[:, None].astype(bf16), (count, 64))
    normed_marked = jnp.concatenate([normed.astype(bf16), marks], axis=1)
    normed_sent, cot_all = rep_exchange(rep, 1, gathers=(normed_marked, cot_low))
    cot_all = cot_all.reshape(group, width)
    normed_all = normed_sent[:, :, :width].reshape(group, width)
    in_seq_all = normed_sent[:, :, width].astype(f32).T.reshape(group, 1)

    in_out = dot(swapped(normed_all.reshape(rep, count, width)), full_in)
    mout_mix = hand_on(mout_mix, in_out)
    mout_mix = mout_mix.reshape(fsdp, -1, width)
    full_mout = mout_mix[:, : part_mout.shape[0]].reshape(-1, width)
    mix_t = mout_mix[:, part_mout.shape[0] :].reshape(fsdp, -1)[:, :mix_size]
    mix_t = mix_t.reshape(width, mix_part).T
    xs, gate_z = in_out[:, :channels], in_out[:, gate_at : gate_at + channels]
    qkv_sent = in_out[:, channels : channels + qkv_part].astype(bf16)
    qkv_sent = swapped(qkv_sent.reshape(count, rep, qkv_part))

    conv_w, conv_b = my_part(conv_weight, 1), my_part(conv_bias, 0)
    part_x_proj, part_dt_proj = my_part(x_proj, 0), my_part(dt_proj, 1)
    part_dt_bias, part_skip = my_part(dt_bias, 0), my_part(d_skip, 0)
    rate = -jnp.exp(my_part(a_log, 1))
    conv_sum = xs * conv_w[CONV - 1] + conv_b
    for k in range(1, CONV):
        earlier = jnp.where(in_seq_all >= k, shift_down(xs, k * rep), 0.0)
        conv_sum = conv_sum + earlier * conv_w[CONV - 1 - k]
    act, act_slope = silu_and_slope(conv_sum)
    proj_sent = dot(act, part_x_proj, high).reshape(count, rep, -1).transpose(1, 0, 2)
    proj, qkv_back = rep_exchange(
        rep, 2, alls=(proj_sent,), trades=(qkv_sent.reshape(rep, count, qkv_part),)
    )
    qkv_low = qkv_back.transpose(1, 0, 2).reshape(count, rep * qkv_part)
    proj = proj.transpose(1, 0, 2)
    dt_in = proj.reshape(group, -1)[:, :DT_RANK]
    maps = proj[:, :, DT_RANK:]
    dt_sum = dot(dt_in, part_dt_proj, high) + part_dt_bias
    step = jax.nn.softplus(dt_sum)
    decay_step = jnp.where(in_seq_all == 0.0, 1e30, step * LOG2_E)
    inputs = step * act
    cube = (count, rep, channels)
    scanned, decayed, mix_t = scan_forward(
        decay_step.reshape(cube), inputs.reshape(cube), maps, rate, rep, 9, mix_t
    )
    mix_t = mix_t.reshape(width, width)
    scanned = scanned.reshape(group, channels)
    silu_z, z_slope = silu_and_slope(gate_z)
    before_gate = scanned + part_skip * act
    mixer_low = swapped((before_gate * silu_z).astype(bf16).reshape(cube))
    ssm_part = by_row(dot(mixer_low, full_mout).astype(bf16)).reshape(rep, count, width)
    (ssm_out,) = rep_exchange(rep, 3, sums=(ssm_part,))

    attended_values, log_total = attention_forward(qkv_low, allowed)
    mixed, mix_pull = jax.vjp(mix_branches, attended_values, ssm_out, norm_attn, norm_ssm)
    mixed_low = mixed.astype(bf16)
    middle = hidden_in + dot_right_t(mixed_low, mix_t)
    ffn_in, ffn_pull = jax.vjp(rms_norm, middle, norm_ffn)
    ffn_all, mixed_all = rep_exchange(rep, 4, gathers=(ffn_in.astype(bf16), mixed_low))
    ffn_all, mixed_all = ffn_all.reshape(group, width), mixed_all.reshape(group, width)

    gate_up = dot(ffn_all, full_gate_up)
    hidden, swiglu_pull = jax.vjp(swiglu, gate_up[:, :ff_part], gate_up[:, ff_part:])
    hidden_low = hidden.astype(bf16)
    grad_hidden = dot_right_t(cot_all, full_down)
    grad_gate_up = jnp.concatenate(swiglu_pull(grad_hidden), axis=1).astype(bf16)
    part_gate_up = dot_left_t(ffn_all, grad_gate_up).astype(bf16)
    own_gate_up = line_scatter(part_gate_up)
    grad_gate_up = tied(grad_gate_up, part_gate_up)
    ffn_sent = by_row(dot_right_t(grad_gate_up, full_gate_up).astype(bf16))
    part_down = dot_left_t(hidden_low, cot_all).astype(bf16)
    own_down = line_scatter(part_down)
    down_sent = by_row(dot(tied(hidden_low, part_down), full_down).astype(bf16))
    blocks = (rep, count, width)
    grad_ffn, down_out = rep_exchange(
        rep, 5, sums=(ffn_sent.reshape(blocks), down_sent.reshape(blocks))
    )
    result = middle + down_out

    grad_middle_norm, grad_norm_ffn = ffn_pull(grad_ffn)
    grad_middle = cot_rows + grad_middle_norm
    middle_low = grad_middle.astype(bf16)
    grad_mixed = dot(middle_low, mix_t)
    grad_attended, grad_ssm, grad_norm_attn, grad_norm_ssm = mix_pull(grad_mixed)
    middle_sent = middle_low.reshape(count, rep, -1).transpose(1, 0, 2)
    qkv_grad = attention_backward(qkv_low, grad_attended.astype(bf16), log_total, allowed)
    qkv_grad = qkv_grad.astype(bf16).reshape(count, rep, -1).transpose(1, 0, 2)
    ssm_all, middle_cols, qkv_cols = rep_exchange(
        rep, 6, gathers=(grad_ssm.astype(bf16),), trades=(middle_sent, qkv_grad)
    )
    qkv_cols = qkv_cols.reshape(group, qkv_part)
    ssm_all = tied(ssm_all, own_gate_up).reshape(group, width)
    grad_mixer = dot_right_t(ssm_all, full_mout).reshape(rep, count, channels)
    grad_mixer = swapped(grad_mixer)
    part_mout = dot_left_t(mixer_low, ssm_all).astype(bf16)
    part_mix = dot_left_t(mixed_all, middle_cols.reshape(group, -1)).astype(bf16)

    grad_z = (grad_mixer * before_gate * z_slope).astype(bf16)
    grad_z = swapped(grad_z.reshape(cube))
    spare = early_width - qkv_part - channels
    early_grad = jnp.concatenate([qkv_cols, jnp.zeros((group, spare), bf16), grad_z], axis=1)
    part_early = dot_left_t(normed_all, early_grad).astype(bf16)
    grad_mixer = tied(grad_mixer, part_mout, part_mix, part_early, own_down)
    own_mout, own_mix = line_scatter(part_mout), line_scatter(part_mix)
    own_early = line_scatter(part_early)
    grad_before = grad_mixer * silu_z
    grad_skip = jnp.sum(grad_before * act, axis=0)
    grad_inputs, grad_step, grad_rate, grad_maps, (all_gate_up, all_down) = scan_backward(
        *(item.reshape(cube) for item in (decay_step, step, inputs)),
        maps,
        grad_before.reshape(cube),
        decayed,
        rate,
        rep,
        7,
        (own_gate_up, own_down),
    )
    grad_inputs = grad_inputs.reshape(group, channels)
    grad_step = grad_step.reshape(group, channels)
    grad_a_log = grad_rate * rate
    grad_step = grad_step + grad_inputs * act
    grad_dt = grad_step * jax.nn.sigmoid(dt_sum)
    grad_dt_bias = jnp.sum(grad_dt, axis=0)
    grad_dt_proj = dot_left_t(dt_in, grad_dt)
    proj_sent = jnp.concatenate(
        [dot_right_t(grad_dt, part_dt_proj), grad_maps], axis=1
    )
    proj_sent = proj_sent.reshape(count, rep, -1).transpose(1, 0, 2)
    (grad_proj,) = rep_exchange(rep, 11, alls=(proj_sent,))
    grad_proj = swapped(tied(grad_proj, own_mout, own_mix))
    grad_x_proj = dot_left_t(grad_proj, act)
    grad_act = grad_before * part_skip + grad_inputs * step + dot_right_t(grad_proj, part_x_proj)
    grad_conv = grad_act * act_slope
    grad_conv_b = jnp.sum(grad_conv, axis=0)
    grad_conv_w = [jnp.sum(grad_conv * xs, axis=0)]
    grad_xs = grad_conv * conv_w[CONV - 1]
    for k in range(1, CONV):
        reached = jnp.where(in_seq_all >= k, grad_conv, 0.0)
        grad_conv_w.insert(0, jnp.sum(reached * shift_down(xs, k * rep), axis=0))
        grad_xs = grad_xs + shift_up(reached, k * rep) * conv_w[CONV - 1 - k]
    small = jnp.concatenate(
        [jnp.stack(grad_conv_w), grad_conv_b[None], grad_dt_bias[None], grad_skip[None]]
        + [grad_a_log, grad_dt_proj, grad_x_proj],
        axis=0,
    )
    n_small = fsdp * up16(-(-small.shape[0] // fsdp))
    small = jnp.pad(small, ((0, n_small - small.shape[0]), (0, 0))).astype(bf16)
    grad_xs = swapped(grad_xs.astype(bf16).reshape(cube))
    gap = jnp.zeros((group, gate_at - channels - qkv_part), bf16)
    end = jnp.zeros((group, in_width - gate_at - channels), bf16)
    in_grad = jnp.concatenate([grad_xs, qkv_cols, gap, grad_z, end], axis=1)
    normed_part = by_row(dot_right_t(in_grad, full_in).astype(bf16)).reshape(blocks)
    own_late = line_scatter(dot_left_t(normed_all, grad_xs).astype(bf16))
    (grad_normed,) = rep_exchange(rep, 8, sums=(normed_part,))
    grad_hidden_norm, grad_norm_in = norm_in_pull(grad_normed)
    grad_hidden_in = grad_middle + grad_hidden_norm

    def given_back(rows):
        return dot_left_t(picks, rows.astype(bf16)).astype(bf16).reshape(fsdp, block_rows, width)

    gains = jnp.stack([grad_norm_in, grad_norm_attn, grad_norm_ssm, grad_norm_ffn])
    gains = jnp.concatenate([gains, jnp.zeros((4, width), f32)], axis=0)
    (
        sum_gate,
        sum_up,
        sum_down,
        all_mout,
        all_mix,
        all_early,
        all_late,
        small,
        gains,
        mixed_out,
        grad_tokens,
    ) = last_exchange(
        rep,
        fsdp,
        10,
        (all_gate_up, all_down, w_gate.shape[1], w_down.shape[0]),
        (own_mout, own_mix, own_early, own_late),
        small.reshape(fsdp, -1, channels),
        gains,
        (given_back(result), given_back(grad_hidden_in)),
    )
    gains, small = jnp.sum(gains, axis=0), small.reshape(rep, n_small, channels)
    sum_mamba_in, sum_qkv, sum_mix = join_columns(
        rep,
        (all_late, all_early, all_mix),
        (w_mamba_in.shape[1], w_qkv.shape[1], width),
        (
            ((0, 0, piece, 0, fsdp), (1, early_width - channels, piece, INNER, fsdp)),
            ((1, 0, qkv_part, 0, 1),),
            ((2, 0, width // rep, 0, 1),),
        ),
    )
    sum_mout = join_rows(rep, all_mout, w_mamba_out.shape[0], width)

    (small,) = join_columns(rep, (small,), (INNER,), (((0, 0, piece, 0, fsdp),),))
    ends = [CONV, CONV + 1, CONV + 2, CONV + 3, CONV + 3 + STATE, CONV + 3 + STATE + DT_RANK]
    ends.append(ends[-1] + x_proj.shape[1])
    return (
        mixed_out.reshape(count, width),
        grad_tokens.reshape(count, width),
        gains[0],
        sum_qkv,
        sum_mamba_in,
        small[: ends[0]],
        small[ends[0]],
        small[ends[5] : ends[6]].T,
        small[ends[4] : ends[5]],
        small[ends[1]],
        small[ends[3] : ends[4]],
        small[ends[2]],
        sum_mout,
        gains[1],
        gains[2],
        sum_mix,
        gains[3],
        sum_gate.astype(f32),
        sum_up.astype(f32),
        sum_down.astype(f32).T,
    )


def solution(mesh):
    rows = P(("rep", "fsdp"), None)
    cut = P("fsdp", None)
    whole = P()
    return jax.shard_map(
        functools.partial(per_device, mesh.shape["rep"], mesh.shape["fsdp"]),
        mesh=mesh,
        in_specs=(rows,) * 4
        + (whole, cut, cut)
        + (whole,) * 7
        + (cut, whole, whole, cut, whole, cut, cut, cut),
        out_specs=(rows, rows, whole, cut, cut)
        + (whole,) * 7
        + (cut, whole, whole, cut, whole, cut, cut, cut),
        check_vma=False,
    )
```

```python
import functools

import jax
import jax.numpy as jnp
from jax import lax
from jax.experimental import pallas as pl
from jax.experimental.layout import Layout, with_layout_constraint
from jax.experimental.pallas import tpu as pltpu
from jax.sharding import PartitionSpec as P

HEADS = 25
KV_HEADS = 5
HEAD_DIM = 64
INNER = 3200
STATE = 16
DT_RANK = 100
CONV = 4
WINDOW = 1024
LANES = 128
PACKS = 8
LOG2_E = 1.4426950408889634

epsilon = 1e-06
bf16 = jnp.bfloat16
f32 = jnp.float32


def dot(left, right, precision=None):
    return jnp.dot(left, right, precision=precision, preferred_element_type=f32)


def dot_right_t(left, right):
    return lax.dot_general(left, right, (((1,), (1,)), ((), ())), preferred_element_type=f32)


def dot_left_t(left, right):
    return lax.dot_general(left, right, (((0,), (0,)), ((), ())), preferred_element_type=f32)


def rms_norm(value_rows, gain):
    return (
        value_rows
        * lax.rsqrt(jnp.mean(value_rows * value_rows, axis=-1, keepdims=True) + epsilon)
        * gain
    )


def mix_branches(attended_values, ssm_out, norm_attn, norm_ssm):
    return (rms_norm(attended_values, norm_attn) + rms_norm(ssm_out, norm_ssm)) * 0.5


def swiglu(gate_val, up_val):
    return jax.nn.silu(gate_val) * up_val


def hbm_spec():
    return pl.BlockSpec(memory_space=pl.ANY)


def vmem_spec():
    return pl.BlockSpec(memory_space=pltpu.VMEM)


SMALL_COST = pl.CostEstimate(flops=0, bytes_accessed=10**4, transcendentals=0)


def send(src, dst, sems, axis, target):
    copy = pltpu.make_async_remote_copy(
        src_ref=src,
        dst_ref=dst,
        send_sem=sems[0],
        recv_sem=sems[1],
        device_id={axis: target},
        device_id_type=pl.DeviceIdType.MESH,
    )
    copy.start()
    return copy


def meet(axis, others):
    barrier = pltpu.get_barrier_semaphore()
    for other in others:
        pl.semaphore_signal(
            barrier, inc=1, device_id={axis: other}, device_id_type=pl.DeviceIdType.MESH
        )
    pl.semaphore_wait(barrier, len(others))


def rep_kernel(rep, counts, square, *refs):
    n_gather, n_sum, n_all, n_trade = counts
    chips = rep // 2
    refs = list(refs)

    def take(n):
        taken = refs[:n]
        del refs[:n]
        return taken

    gathers, sums, alls, trades = (take(n) for n in counts)
    gathered, summed, all_summed, traded = (take(n) for n in counts)
    reduced = sums + alls
    buffers = [take(3) for _ in reduced]
    totals = summed + take(n_all)
    local, far, near, direct = refs

    me = lax.axis_index("rep")
    core = lax.rem(me, 2)
    chip = (me - core) // 2
    partner = 2 * chip + 1 - core
    ahead = [lax.rem(chip + k, chips) for k in range(chips)]
    behind = [lax.rem(chip + chips - k, chips) for k in range(chips)]
    if square:
        along_x, along_y = chip + 1 - 2 * lax.rem(chip, 2), lax.rem(chip + 2, 4)
        first = along_x + core * (along_y - along_x)
        second = along_y + core * (along_x - along_y)
        across = 3 - chip
        linked = [2 * first + core, 2 * second + core]
    else:
        linked = [2 * ahead[k] + core for k in range(1, chips)]
    if n_trade:
        meet("rep", [lax.rem(me + k, rep) for k in range(1, rep)])
    else:
        meet("rep", linked + [partner])

    kept, sent = [], []

    def keep(src, dst):
        copy = pltpu.make_async_copy(src, dst, local.at[len(kept)])
        copy.start()
        kept.append(copy)

    def far_send(src, dst, slot, k, target):
        copy = send(src, dst, (far.at[0, slot, k], far.at[1, slot, k]), "rep", 2 * target + core)
        sent.append(copy)
        return copy

    def near_send(src, dst, slot, k):
        copy = send(src, dst, (near.at[0, slot, k], near.at[1, slot, k]), "rep", partner)
        sent.append(copy)
        return copy

    def start_gather(source, out, slot):
        if square:
            far_copies = [
                far_send(source, out.at[me], slot, 1, first),
                far_send(source, out.at[me], slot, 2, second),
            ]
        else:
            far_copies = [
                far_send(source, out.at[me], slot, k, ahead[k]) for k in range(1, chips)
            ]
        near_copies = [near_send(source, out.at[me], slot, 0)]
        keep(source, out.at[me])
        return out, slot, far_copies, near_copies

    def pass_on(states):
        if square:
            for out, slot, far_copies, near_copies in states:
                block = out.at[2 * first + core]
                far_copies[0].wait_recv()
                far_copies.append(far_send(block, block, slot, 3, second))
                near_copies.append(near_send(block, block, slot, 1))
            for out, slot, far_copies, near_copies in states:
                for k, source in ((2, second), (3, across)):
                    block = out.at[2 * source + core]
                    far_copies[k - 1].wait_recv()
                    near_copies.append(near_send(block, block, slot, k))
        else:
            for out, slot, far_copies, near_copies in states:
                for k in range(1, chips):
                    block = out.at[2 * behind[k] + core]
                    far_copies[k - 1].wait_recv()
                    near_copies.append(near_send(block, block, slot, k))
        for _, _, _, near_copies in states:
            for copy in near_copies:
                copy.wait_recv()

    dests = [chip, first, across, second] if square else ahead
    partner_dests = [chip, second, across, first] if square else ahead
    order = [1, 2, 3, 0] if square else [*range(1, chips), 0]
    crossing = []
    for i, source in enumerate(reduced):
        from_partner = buffers[i][1]
        crossing.append(
            {
                k: near_send(source.at[2 * partner_dests[k] + 1 - core], from_partner.at[k], i, k)
                for k in order
            }
        )
    states = [
        start_gather(source, gathered[i], len(reduced) + n_all + i)
        for i, source in enumerate(gathers)
    ]
    trading = []
    for i, source in enumerate(trades):
        keep(source.at[me], traded[i].at[me])
        for k in range(1, rep):
            target = lax.rem(me + k, rep)
            copy = send(
                source.at[target],
                traded[i].at[me],
                (direct.at[0, i, k], direct.at[1, i, k]),
                "rep",
                target,
            )
            trading.append(copy)

    def of_chip(i, k):
        crossing[i][k].wait_recv()
        own = reduced[i][2 * dests[k] + core]
        return own.astype(f32) + buffers[i][1][k].astype(f32)

    crossed = []
    for i in range(len(reduced)):
        low, _, arrived = buffers[i]
        copies = []
        for k in (1, 2) if square else range(1, chips):
            low[k - 1] = of_chip(i, k).astype(low.dtype)
            target = first if square else ahead[k]
            copies.append(far_send(low.at[k - 1], arrived.at[k - 1], i, k, target))
        crossed.append(copies)
    if square:
        for i in range(len(reduced)):
            low, _, arrived = buffers[i]
            value = of_chip(i, 3)
            crossed[i][1].wait_recv()
            low[2] = (value + arrived[1].astype(f32)).astype(low.dtype)
            crossed[i].append(far_send(low.at[2], arrived.at[2], i, 3, second))
    for i in range(len(reduced)):
        arrived = buffers[i][2]
        total = of_chip(i, 0)
        for k in (1, 3) if square else range(1, chips):
            crossed[i][k - 1].wait_recv()
            total = total + arrived[k - 1].astype(f32)
        totals[i][...] = total.astype(totals[i].dtype)
        if i >= n_sum:
            states.append(start_gather(totals[i], all_summed[i - n_sum], n_all + i))
    pass_on(states)
    for copy in trading:
        copy.wait()
    for copy in sent:
        copy.wait_send()
    for copy in kept:
        copy.wait()


def rep_exchange(rep, collective_id, gathers=(), sums=(), alls=(), trades=()):
    chips = rep // 2
    square = rep == 8 and not alls
    counts = (len(gathers), len(sums), len(alls), len(trades))
    reduced = (*sums, *alls)
    out_shape = [jax.ShapeDtypeStruct((rep,) + x.shape, x.dtype) for x in gathers]
    out_shape += [jax.ShapeDtypeStruct(x.shape[1:], f32) for x in sums]
    out_shape += [jax.ShapeDtypeStruct(x.shape, x.dtype) for x in (*alls, *trades)]
    scratch = []
    for x in reduced:
        scratch += [
            pltpu.VMEM((n,) + x.shape[1:], x.dtype) for n in (chips - 1, chips, chips - 1)
        ]
    scratch += [pltpu.VMEM(x.shape[1:], x.dtype) for x in alls]
    n_local = sum(counts) - len(sums) + 1
    n_slots = len(reduced) + len(alls) + len(gathers) + 1
    scratch += [
        pltpu.SemaphoreType.DMA((n_local,)),
        pltpu.SemaphoreType.DMA((2, n_slots, chips)),
        pltpu.SemaphoreType.DMA((2, n_slots, chips)),
        pltpu.SemaphoreType.DMA((2, len(trades) + 1, rep)),
    ]
    return pl.pallas_call(
        functools.partial(rep_kernel, rep, counts, square),
        out_shape=out_shape,
        in_specs=[vmem_spec()] * sum(counts),
        out_specs=[hbm_spec()] * len(gathers)
        + [vmem_spec()] * len(sums)
        + [hbm_spec()] * (len(alls) + len(trades)),
        scratch_shapes=scratch,
        compiler_params=pltpu.CompilerParams(
            collective_id=collective_id,
            has_side_effects=True,
            vmem_limit_bytes=40 * 1024 * 1024,
        ),
        cost_estimate=SMALL_COST,
    )(*gathers, *sums, *alls, *trades)


def line_kernel(count, counts, *refs):
    n_gather, n_all, n_trade = counts
    n_in = sum(counts)
    ins, outs, scratch = refs[:n_in], refs[n_in : 2 * n_in], refs[2 * n_in :]
    arrived, totals = scratch[:n_all], scratch[n_all : 2 * n_all]
    local, remote = scratch[2 * n_all :]
    me = lax.axis_index("fsdp")
    others = [lax.rem(me + k, count) for k in range(1, count)]
    meet("fsdp", others)
    copies, coming = [], []

    def push(block, out, slot):
        return [
            send(block(other), out, (remote.at[0, slot, k], remote.at[1, slot, k]), "fsdp", other)
            for k, other in enumerate(others)
        ]

    def keep(block, out, slot):
        copy = pltpu.make_async_copy(block, out, local.at[slot])
        copy.start()
        copies.append(copy)

    for i in range(n_all):
        source = ins[n_gather + i]
        coming.append(push(lambda other: source.at[other], arrived[i].at[me], n_in + i))
    for i in range(n_in):
        if i < n_gather:
            keep(ins[i], outs[i].at[me], i)
            copies += push(lambda other: ins[i], outs[i].at[me], i)
        elif i >= n_gather + n_all:
            keep(ins[i].at[me], outs[i].at[me], i)
            copies += push(lambda other: ins[i].at[other], outs[i].at[me], i)
    for i in range(n_all):
        for copy in coming[i]:
            copy.wait()
        total = ins[n_gather + i][me].astype(f32)
        for other in others:
            total = total + arrived[i][other].astype(f32)
        totals[i][...] = total.astype(totals[i].dtype)
        out = outs[n_gather + i]
        keep(totals[i], out.at[me], n_gather + i)
        copies += push(lambda other: totals[i], out.at[me], n_gather + i)
    for copy in copies:
        copy.wait()


def line_exchange(count, collective_id, gathers=(), alls=(), trades=()):
    arrays = (*gathers, *alls, *trades)
    out_shape = [jax.ShapeDtypeStruct((count,) + x.shape, x.dtype) for x in gathers]
    out_shape += [jax.ShapeDtypeStruct(x.shape, x.dtype) for x in (*alls, *trades)]
    return pl.pallas_call(
        functools.partial(line_kernel, count, (len(gathers), len(alls), len(trades))),
        out_shape=out_shape,
        in_specs=[vmem_spec()] * len(arrays),
        out_specs=[hbm_spec()] * len(arrays),
        scratch_shapes=[pltpu.VMEM(x.shape, x.dtype) for x in alls]
        + [pltpu.VMEM(x.shape[1:], x.dtype) for x in alls]
        + [
            pltpu.SemaphoreType.DMA((len(arrays),)),
            pltpu.SemaphoreType.DMA((2, len(arrays) + len(alls), count)),
        ],
        compiler_params=pltpu.CompilerParams(collective_id=collective_id, has_side_effects=True),
        cost_estimate=SMALL_COST,
    )(*arrays)


def remote_copy(src, dst, sems, axis, target):
    return pltpu.make_async_remote_copy(
        src_ref=src,
        dst_ref=dst,
        send_sem=sems[0],
        recv_sem=sems[1],
        device_id={axis: target},
        device_id_type=pl.DeviceIdType.MESH,
    )


class Gathers:
    def __init__(self, rep):
        chips, self.square = rep // 2, rep == 8
        self.me = lax.axis_index("rep")
        self.core = lax.rem(self.me, 2)
        chip = (self.me - self.core) // 2
        self.partner = 2 * chip + 1 - self.core
        if self.square:
            along_x, along_y = chip + 1 - 2 * lax.rem(chip, 2), lax.rem(chip + 2, 4)
            first = along_x + self.core * (along_y - along_x)
            second = along_y + self.core * (along_x - along_y)
            hops, sources = [first, second], [first, second, 3 - chip]
        else:
            hops = [lax.rem(chip + k, chips) for k in range(1, chips)]
            sources = [lax.rem(chip + chips - k, chips) for k in range(1, chips)]
        self.hops = [2 * hop + self.core for hop in hops]
        self.sources = [2 * source + self.core for source in sources]

    def plan(self, source, out, far, near, local, i):
        blocks = [out.at[origin] for origin in self.sources]

        def over(sems, src, dst, k, target):
            return remote_copy(src, dst, (sems.at[0, i, k], sems.at[1, i, k]), "rep", target)

        own = [over(far, source, out.at[self.me], k, hop) for k, hop in enumerate(self.hops)]
        if self.square:
            own.append(over(far, blocks[0], blocks[0], 2, self.hops[1]))
        across = [over(near, block, block, k, self.partner) for k, block in enumerate(blocks)]
        across.append(over(near, source, out.at[self.me], len(blocks), self.partner))
        return own, across, pltpu.make_async_copy(source, out.at[self.me], local.at[i])

    def begin(self, plan):
        own, across, keep = plan
        for copy in own[: len(self.hops)]:
            copy.start()
        across[-1].start()
        keep.start()

    def first_hop(self, plan):
        own, across, _ = plan
        own[0].wait_recv()
        if self.square:
            own[2].start()
        across[0].start()

    def second_hop(self, plan):
        own, across, _ = plan
        for k in range(1, len(self.hops)):
            own[k].wait_recv()
            across[k].start()

    def relayed(self, plan):
        own, across, _ = plan
        if self.square:
            own[2].wait_recv()
            across[2].start()

    def end(self, plan):
        own, across, keep = plan
        for copy in across:
            copy.wait()
        for copy in own:
            copy.wait_send()
        keep.wait()


def last_kernel(rep, fsdp, square, n_gather, layout, down_rows, *refs):
    parts_gate_up, parts_down, refs = refs[0], refs[1], refs[2:]
    gathers, refs = refs[:n_gather], refs[n_gather:]
    small, gains, trades, refs = refs[0], refs[1], refs[2:4], refs[4:]
    joined_gate, joined_up, joined_down, refs = refs[0], refs[1], refs[2], refs[3:]
    gathered, refs = refs[:n_gather], refs[n_gather:]
    small_out, gains_out, traded, refs = refs[0], refs[1], refs[2:4], refs[4:]
    arrived, total, lined, gains_in, gains_sum, local, far, near, keeping, remote = refs

    line = lax.axis_index("fsdp")
    others = [lax.rem(line + k, fsdp) for k in range(1, fsdp)]
    along = Gathers(rep)

    def push(block, out, slot):
        return [
            remote_copy(
                block(other), out, (remote.at[0, slot, k], remote.at[1, slot, k]), "fsdp", other
            )
            for k, other in enumerate(others)
        ]

    gains_plan = along.plan(gains, gains_in, far, near, local, 0)
    plans = [
        along.plan(gathers[i], gathered[i], far, near, local, 1 + i) for i in range(n_gather)
    ]
    small_plan = along.plan(lined, small_out, far, near, local, 1 + n_gather)
    small_in = push(lambda other: small.at[other], arrived.at[line], 0)
    small_back = push(lambda other: total, lined.at[line], 3)
    gains_push = push(lambda other: gains_sum, gains_out.at[line], 4)
    gains_keep = pltpu.make_async_copy(gains_sum, gains_out.at[line], keeping.at[2])
    traffic = []
    for i in range(2):
        source = trades[i]
        traffic += push(lambda other: source.at[other], traded[i].at[line], 1 + i)
        traffic.append(
            pltpu.make_async_copy(source.at[line], traded[i].at[line], keeping.at[i])
        )
    step, steps = pl.program_id(0), pl.num_programs(0)

    @pl.when(step == 0)
    def _():
        barrier = pltpu.get_barrier_semaphore()
        met = [("rep", index) for index in (*along.hops, along.partner)]
        met += [("fsdp", index) for index in others]
        for axis, index in met:
            pl.semaphore_signal(
                barrier, inc=1, device_id={axis: index}, device_id_type=pl.DeviceIdType.MESH
            )
        pl.semaphore_wait(barrier, len(met))
        for copy in small_in:
            copy.start()
        along.begin(gains_plan)
        for plan in plans:
            along.begin(plan)
        for copy in traffic:
            copy.start()

    join_kernel(rep, layout, parts_gate_up, joined_gate, joined_up)
    join_rows_kernel(rep, down_rows, True, parts_down, joined_down)

    @pl.when(step == steps - 1)
    def _():
        for copy in small_in:
            copy.wait()
        value = small[line].astype(f32)
        for other in others:
            value = value + arrived[other].astype(f32)
        total[...] = value.astype(total.dtype)
        for copy in small_back:
            copy.start()
        lined[line] = total[...]
        for plan in (gains_plan, *plans):
            along.first_hop(plan)
        for plan in (gains_plan, *plans):
            along.second_hop(plan)
        along.relayed(gains_plan)
        along.end(gains_plan)
        gains_sum[...] = jnp.sum(gains_in[...], axis=0)
        for copy in gains_push:
            copy.start()
        gains_keep.start()
        for copy in small_back:
            copy.wait()
        along.begin(small_plan)
        for plan in plans:
            along.relayed(plan)
        along.first_hop(small_plan)
        along.second_hop(small_plan)
        along.relayed(small_plan)
        for plan in (*plans, small_plan):
            along.end(plan)
        for copy in (*traffic, *gains_push, gains_keep):
            copy.wait()


def last_exchange(rep, fsdp, collective_id, ffn, gathers, small, gains, trades):
    n_gather, chips = len(gathers), rep // 2
    parts_gate_up, parts_down, ff_width, ff_rows = ffn
    rows, ff_part, width = parts_gate_up.shape[1], parts_gate_up.shape[2] // 2, gains.shape[1]
    block, columns = next(n for n in (80, 40, 64, rows) if rows % n == 0), 2 * LANES
    steps, row_steps = pl.cdiv(width, columns), rows // block
    rest = ff_width // rep // fsdp
    layout = (((0, 0, rest, 0, fsdp),), ((0, ff_part, rest, 0, fsdp),))

    def row_at(i):
        return lax.div(i * row_steps, steps)

    out_shape = [jax.ShapeDtypeStruct((rows, ff_width), bf16)] * 2
    out_shape.append(jax.ShapeDtypeStruct((width, ff_rows), bf16))
    out_shape += [jax.ShapeDtypeStruct((rep,) + x.shape, x.dtype) for x in gathers]
    out_shape.append(jax.ShapeDtypeStruct((rep,) + small.shape, small.dtype))
    out_shape.append(jax.ShapeDtypeStruct((fsdp,) + gains.shape, gains.dtype))
    out_shape += [jax.ShapeDtypeStruct(x.shape, x.dtype) for x in trades]
    return pl.pallas_call(
        functools.partial(
            last_kernel, rep, fsdp, rep == 8, n_gather, layout, ff_rows // rep
        ),
        grid=(steps,),
        out_shape=out_shape,
        in_specs=[
            pl.BlockSpec((rep, block, 2 * ff_part), lambda i: (0, row_at(i), 0)),
            pl.BlockSpec((rep, parts_down.shape[1], columns), lambda i: (0, 0, i)),
        ]
        + [vmem_spec()] * (n_gather + 4),
        out_specs=[pl.BlockSpec((block, ff_width), lambda i: (row_at(i), 0))] * 2
        + [pl.BlockSpec((columns, ff_rows), lambda i: (i, 0))]
        + [hbm_spec()] * (n_gather + 4),
        scratch_shapes=[
            pltpu.VMEM(small.shape, small.dtype),
            pltpu.VMEM(small.shape[1:], small.dtype),
            pltpu.VMEM(small.shape, small.dtype),
            pltpu.VMEM((rep,) + gains.shape, gains.dtype),
            pltpu.VMEM(gains.shape, gains.dtype),
            pltpu.SemaphoreType.DMA((n_gather + 2,)),
            pltpu.SemaphoreType.DMA((2, n_gather + 2, chips)),
            pltpu.SemaphoreType.DMA((2, n_gather + 2, chips)),
            pltpu.SemaphoreType.DMA((3,)),
            pltpu.SemaphoreType.DMA((2, 5, fsdp)),
        ],
        compiler_params=pltpu.CompilerParams(
            collective_id=collective_id,
            has_side_effects=True,
            vmem_limit_bytes=48 * 1024 * 1024,
        ),
        cost_estimate=SMALL_COST,
    )(parts_gate_up, parts_down, *gathers, small, gains, *trades)


def hand_kernel(_value, _after, _out):
    pass


def hand_on(value, after):
    return pl.pallas_call(
        hand_kernel,
        out_shape=jax.ShapeDtypeStruct(value.shape, value.dtype),
        in_specs=[hbm_spec()] * 2,
        out_specs=hbm_spec(),
        input_output_aliases={0: 0},
        cost_estimate=SMALL_COST,
    )(value, after)


def windows(width, pieces, start, step, rest):
    wide = min(-(-(rest + LANES - 1) // LANES) * LANES, width)
    me = lax.axis_index("rep")
    for i in range(pieces):
        at = start + i * step + me * rest
        aligned = jnp.minimum((at // LANES) * LANES, (width - wide) // LANES * LANES)
        yield pl.multiple_of(aligned, LANES), at - aligned, wide


def up16(size):
    return -(-size // 16) * 16


def copy_parts(rep, fsdp, source, out, place, start, total):
    rest = total // (rep * fsdp)
    rows = source.shape[0]
    for aligned, shift, wide in windows(source.shape[1], fsdp, start, rep * rest, rest):
        value = source[:, pl.ds(aligned, wide)].astype(f32)
        value = pltpu.roll(value, lax.rem(wide - shift, wide), 1)[:, :rest]
        if up16(rest) > rest:
            value = jnp.concatenate([value, jnp.zeros((rows, up16(rest) - rest), f32)], axis=1)
        out[:, place : place + up16(rest)] = value.astype(bf16)
        place += up16(rest)


def part_in_kernel(rep, fsdp, spots, qkv_ref, min_ref, out_ref):
    _, qkv_at, gate_at = spots
    rows, qkv_width = qkv_ref.shape
    qkv_part = qkv_width // rep
    out_ref[...] = jnp.zeros_like(out_ref)
    copy_parts(rep, fsdp, min_ref, out_ref, 0, 0, INNER)
    copy_parts(rep, fsdp, min_ref, out_ref, gate_at, INNER, INNER)
    value = qkv_ref[...].astype(f32)
    padded = -(-qkv_width // LANES) * LANES
    value = jnp.concatenate([value, jnp.zeros((rows, padded - qkv_width), f32)], axis=1)
    shift = padded - lax.axis_index("rep") * qkv_part
    value = pltpu.roll(value, lax.rem(shift, padded), 1)
    out_ref[:, qkv_at : qkv_at + qkv_part] = value[:, :qkv_part].astype(bf16)


def part_gate_up_kernel(rep, fsdp, gate_ref, up_ref, out_ref):
    copy_parts(rep, fsdp, gate_ref, out_ref, 0, 0, gate_ref.shape[1])
    copy_parts(rep, fsdp, up_ref, out_ref, out_ref.shape[1] // 2, 0, up_ref.shape[1])


def by_rows(kernel, sources, width):
    rows = sources[0].shape[0]
    block = 80 if rows % 80 == 0 else rows
    return pl.pallas_call(
        kernel,
        grid=(rows // block,),
        in_specs=[pl.BlockSpec((block, x.shape[1]), lambda i: (i, 0)) for x in sources],
        out_specs=pl.BlockSpec((block, width), lambda i: (i, 0)),
        out_shape=jax.ShapeDtypeStruct((rows, width), bf16),
        compiler_params=pltpu.CompilerParams(vmem_limit_bytes=40 * 1024 * 1024),
        cost_estimate=SMALL_COST,
    )(*sources)


def join_kernel(rep, layout, *refs):
    sources, outs = refs[: len(refs) - len(layout)], refs[len(refs) - len(layout) :]
    for out, entries in zip(outs, layout):
        for index, first, rest, place, pieces in entries:
            for i in range(pieces):
                start = first + i * up16(rest)
                for r in range(rep):
                    at = place + (i * rep + r) * rest
                    piece = sources[index][r, :, start : start + rest]
                    out[:, at : at + rest] = piece.astype(out.dtype)


def join_rows_kernel(rep, rows, flip, source, out):
    for r in range(rep):
        if flip:
            out[:, r * rows : (r + 1) * rows] = source[r].astype(f32).T[:, :rows].astype(out.dtype)
        else:
            out[r * rows : (r + 1) * rows, :] = source[r, :rows, :].astype(f32)


def join_rows(rep, source, total, width, flip=False):
    block = 2 * LANES
    shape = (total, width)
    out_spec = pl.BlockSpec((total, block), lambda i: (0, i))
    if flip:
        shape = (width, total)
        out_spec = pl.BlockSpec((block, total), lambda i: (i, 0))
    return pl.pallas_call(
        functools.partial(join_rows_kernel, rep, total // rep, flip),
        grid=(pl.cdiv(width, block),),
        in_specs=[pl.BlockSpec((rep, source.shape[1], block), lambda i: (0, 0, i))],
        out_specs=out_spec,
        out_shape=jax.ShapeDtypeStruct(shape, f32),
        compiler_params=pltpu.CompilerParams(vmem_limit_bytes=40 * 1024 * 1024),
        cost_estimate=SMALL_COST,
    )(source)


def join_columns(rep, sources, widths, layout):
    rows = sources[0].shape[1]
    block = next(n for n in (80, 40, 64, rows) if rows % n == 0)
    return pl.pallas_call(
        functools.partial(join_kernel, rep, layout),
        grid=(rows // block,),
        in_specs=[
            pl.BlockSpec((rep, block, x.shape[2]), lambda i: (0, i, 0)) for x in sources
        ],
        out_specs=[pl.BlockSpec((block, width), lambda i: (i, 0)) for width in widths],
        out_shape=[jax.ShapeDtypeStruct((rows, width), f32) for width in widths],
        compiler_params=pltpu.CompilerParams(vmem_limit_bytes=48 * 1024 * 1024),
        cost_estimate=SMALL_COST,
    )(*sources)


def spread_beside(rep, steps, pairs, local, far, near):
    along = Gathers(rep)
    plans = [along.plan(*pair, far, near, local, i) for i, pair in enumerate(pairs)]

    @pl.when(steps[0])
    def _():
        meet("rep", [*along.hops, along.partner])
        for plan in plans:
            along.begin(plan)

    @pl.when(steps[1])
    def _():
        for plan in plans:
            along.first_hop(plan)

    @pl.when(steps[2])
    def _():
        for plan in plans:
            along.second_hop(plan)

    def finish():
        for plan in plans:
            along.relayed(plan)
        for plan in plans:
            along.end(plan)

    return finish


def spread_maps(maps_ref, wide_ref, start):
    count, packs, columns = maps_ref.shape

    def spread(i, _):
        for u in range(2):
            t = 2 * i + u
            maps = maps_ref[t]
            for n in range(columns):
                wide_ref[n, start + t] = jnp.broadcast_to(maps[:, n : n + 1], (packs, LANES))
        return 0

    lax.fori_loop(0, count // 2, spread, 0)


def scan_kernel(
    rep,
    channels,
    decay_step_ref,
    input_ref,
    maps_ref,
    rate_ref,
    beside_ref,
    out_ref,
    decayed_ref,
    beside_out_ref,
    wide_ref,
    local,
    far,
    near,
):
    count, packs, _ = decay_step_ref.shape
    valid = (
        lax.broadcasted_iota(jnp.int32, (packs, LANES), 1)
        < channels - pl.program_id(1) * LANES
    )
    rate = jnp.where(valid[:1], rate_ref[...], 0.0)
    at = pl.program_id(0) * pl.num_programs(1) + pl.program_id(1)
    last = pl.num_programs(0) * pl.num_programs(1) - 1
    steps = [at == step for step in (0, 2 * last // 3, last)]
    finish = spread_beside(rep, steps, [(beside_ref, beside_out_ref)], local, far, near)

    @pl.when(pl.program_id(1) == 0)
    def _():
        spread_maps(maps_ref, wide_ref, 0)

    def step(i, states):
        for u in range(2):
            t = 2 * i + u
            decay_step = jnp.where(valid, decay_step_ref[t], 0.0)
            inputs = jnp.where(valid, input_ref[t], 0.0)
            out = jnp.zeros((packs, LANES), f32)
            new_states = []
            for n in range(STATE):
                decayed = jnp.exp2(decay_step * rate[n : n + 1]) * states[n]
                state = decayed + wide_ref[n, t] * inputs
                out = out + state * wide_ref[STATE + n, t]
                decayed_ref[n, t] = decayed
                new_states.append(state)
            out_ref[t] = out
            states = tuple(new_states)
        return states

    lax.fori_loop(0, count // 2, step, (jnp.zeros((packs, LANES), f32),) * STATE)
    pl.when(at == last)(finish)


def scan_forward(decay_step, inputs, maps, rate, rep, collective_id, beside):
    count, packs, channels = inputs.shape
    wide = pl.BlockSpec((count, PACKS, LANES), lambda g, i: (0, g, i))
    return pl.pallas_call(
        functools.partial(scan_kernel, rep, channels),
        grid=(packs // PACKS, pl.cdiv(channels, LANES)),
        in_specs=[
            wide,
            wide,
            pl.BlockSpec((count, PACKS, 2 * STATE), lambda g, i: (0, g, 0)),
            pl.BlockSpec((STATE, LANES), lambda g, i: (0, i)),
            hbm_spec(),
        ],
        out_specs=[
            wide,
            pl.BlockSpec((STATE, count, PACKS, LANES), lambda g, i: (0, 0, g, i)),
            hbm_spec(),
        ],
        out_shape=[
            jax.ShapeDtypeStruct(inputs.shape, f32),
            jax.ShapeDtypeStruct(
                (STATE, count, packs, pl.cdiv(channels, LANES) * LANES), f32
            ),
            jax.ShapeDtypeStruct((rep,) + beside.shape, beside.dtype),
        ],
        scratch_shapes=[
            pltpu.VMEM((2 * STATE, count, PACKS, LANES), f32),
            pltpu.SemaphoreType.DMA((1,)),
            pltpu.SemaphoreType.DMA((2, 1, rep // 2)),
            pltpu.SemaphoreType.DMA((2, 1, rep // 2)),
        ],
        compiler_params=pltpu.CompilerParams(
            collective_id=collective_id,
            has_side_effects=True,
            vmem_limit_bytes=48 * 1024 * 1024,
        ),
        cost_estimate=SMALL_COST,
    )(decay_step, inputs, maps, rate, beside)


def scan_back_kernel(
    rep,
    channels,
    decay_step_ref,
    step_ref,
    input_ref,
    maps_ref,
    grad_ref,
    decayed_ref,
    rate_ref,
    beside_ref,
    beside2_ref,
    grad_input_ref,
    grad_step_ref,
    grad_rate_ref,
    grad_maps_ref,
    beside_out_ref,
    beside2_out_ref,
    carry_ref,
    rates_ref,
    in_sum_ref,
    out_sum_ref,
    both_sum_ref,
    wide_ref,
    local,
    far,
    near,
):
    count, packs, _ = decay_step_ref.shape
    at = (pl.program_id(0) * pl.num_programs(1) + pl.program_id(1)) * pl.num_programs(2)
    at = at + pl.program_id(2)
    last = pl.num_programs(0) * pl.num_programs(1) * pl.num_programs(2) - 1
    steps = [at == step for step in (0, 10 * last // 16, 14 * last // 16)]
    pairs = [(beside_ref, beside_out_ref), (beside2_ref, beside2_out_ref)]
    finish = spread_beside(rep, steps, pairs, local, far, near)
    tile, chunk = pl.program_id(1), pl.program_id(2)
    start = (pl.num_programs(2) - 1 - chunk) * count
    valid = lax.broadcasted_iota(jnp.int32, (packs, LANES), 1) < channels - tile * LANES

    @pl.when(tile == 0)
    def _():
        spread_maps(maps_ref, wide_ref, start)
        zeros = jnp.zeros((STATE, count, packs, LANES), f32)
        in_sum_ref[:, pl.ds(start, count)] = zeros
        out_sum_ref[:, pl.ds(start, count)] = zeros
        both_sum_ref[pl.ds(start, count)] = zeros[0]

    @pl.when(chunk == 0)
    def _():
        carry_ref[...] = jnp.zeros_like(carry_ref)
        for n in range(STATE):
            rates_ref[n] = jnp.where(
                valid, jnp.broadcast_to(rate_ref[n : n + 1, :], (packs, LANES)), 0.0
            )

    def backward(back_t, carried):
        grad_states, grad_rates = carried
        t = count - 1 - back_t
        at = start + t
        decay_step = jnp.where(valid, decay_step_ref[t], 0.0)
        step = jnp.where(valid, step_ref[t], 0.0)
        inputs = jnp.where(valid, input_ref[t], 0.0)
        grad = jnp.where(valid, grad_ref[t], 0.0)
        both_sum_ref[at] += grad * inputs
        grad_input = grad_step = jnp.zeros((packs, LANES), f32)
        new_states, new_rates = [], []
        for n in range(STATE):
            decayed, rate = decayed_ref[n, t], rates_ref[n]
            grad_state = grad * wide_ref[STATE + n, at] + grad_states[n]
            out_sum_ref[n, at] += grad * decayed
            in_sum_ref[n, at] += grad_state * inputs
            grad_input = grad_input + grad_state * wide_ref[n, at]
            through = grad_state * decayed
            grad_step = grad_step + through * rate
            new_rates.append(grad_rates[n] + through * step)
            new_states.append(jnp.exp2(decay_step * rate) * grad_state)
        grad_input_ref[t] = grad_input
        grad_step_ref[t] = grad_step
        return (tuple(new_states), tuple(new_rates))

    carried = (
        tuple(carry_ref[n] for n in range(STATE)),
        tuple(carry_ref[STATE + n] for n in range(STATE)),
    )
    grad_states, grad_rates = lax.fori_loop(0, count, backward, carried)
    for n in range(STATE):
        carry_ref[n] = grad_states[n]
        carry_ref[STATE + n] = grad_rates[n]

    @pl.when(chunk == pl.num_programs(2) - 1)
    def _():
        for n in range(STATE):
            grad_rate_ref[n : n + 1, :] = jnp.sum(grad_rates[n], axis=0, keepdims=True)

    @pl.when(tile == pl.num_programs(1) - 1)
    def _():
        column = lax.broadcasted_iota(jnp.int32, (LANES, LANES), 1)
        here = pl.ds(start, count)

        def summed(value, place):
            return jnp.dot(
                value.reshape(count * packs, LANES).astype(bf16),
                (column == place).astype(bf16),
                preferred_element_type=f32,
            )

        total = summed(both_sum_ref[here], 2 * STATE)
        for n in range(STATE):
            total = total + summed(in_sum_ref[n, here], n)
            total = total + summed(out_sum_ref[n, here], STATE + n)
        grad_maps_ref[here] = total.reshape(count, packs, LANES)

    pl.when(at == last)(finish)


def scan_backward(decay_step, step, inputs, maps, grad, decayed, rate, rep, collective_id, beside):
    count, packs, channels = inputs.shape
    groups, chunks = packs // PACKS, 4
    part = count // chunks
    wide = pl.BlockSpec((part, PACKS, LANES), lambda g, i, c: (chunks - 1 - c, g, i))
    row = pl.BlockSpec((STATE, LANES), lambda g, i, c: (0, i))
    sums = pltpu.VMEM((STATE, count, PACKS, LANES), f32)
    grad_inputs, grad_step, grad_rate, grad_maps, *all_beside = pl.pallas_call(
        functools.partial(scan_back_kernel, rep, channels),
        grid=(groups, pl.cdiv(channels, LANES), chunks),
        in_specs=[
            wide,
            wide,
            wide,
            pl.BlockSpec((part, PACKS, 2 * STATE), lambda g, i, c: (chunks - 1 - c, g, 0)),
            wide,
            pl.BlockSpec(
                (STATE, part, PACKS, LANES), lambda g, i, c: (0, chunks - 1 - c, g, i)
            ),
            row,
        ]
        + [hbm_spec()] * 2,
        out_specs=[
            wide,
            wide,
            pl.BlockSpec((STATE, LANES), lambda g, i, c: (g, i)),
            pl.BlockSpec((count, PACKS, LANES), lambda g, i, c: (0, g, 0)),
        ]
        + [hbm_spec()] * 2,
        out_shape=[
            jax.ShapeDtypeStruct(inputs.shape, f32),
            jax.ShapeDtypeStruct(inputs.shape, f32),
            jax.ShapeDtypeStruct((groups * STATE, channels), f32),
            jax.ShapeDtypeStruct((count, packs, LANES), f32),
        ]
        + [jax.ShapeDtypeStruct((rep,) + x.shape, x.dtype) for x in beside],
        scratch_shapes=[
            pltpu.VMEM((2 * STATE, PACKS, LANES), f32),
            pltpu.VMEM((STATE, PACKS, LANES), f32),
            sums,
            sums,
            pltpu.VMEM((count, PACKS, LANES), f32),
            pltpu.VMEM((2 * STATE, count, PACKS, LANES), f32),
            pltpu.SemaphoreType.DMA((2,)),
            pltpu.SemaphoreType.DMA((2, 2, rep // 2)),
            pltpu.SemaphoreType.DMA((2, 2, rep // 2)),
        ],
        compiler_params=pltpu.CompilerParams(
            collective_id=collective_id,
            has_side_effects=True,
            vmem_limit_bytes=52 * 1024 * 1024,
        ),
        cost_estimate=SMALL_COST,
    )(decay_step, step, inputs, maps, grad, decayed, rate, *beside)
    grad_rate = jnp.sum(grad_rate.reshape(groups, STATE, channels), axis=0)
    in_maps, both = grad_maps[:, :, :STATE], grad_maps[:, :, 2 * STATE : 2 * STATE + 1]
    out_maps = grad_maps[:, :, STATE : 2 * STATE] + maps[:, :, :STATE] * both
    grad_maps = jnp.concatenate([in_maps, out_maps], axis=2).reshape(count * packs, 2 * STATE)
    return grad_inputs, grad_step, grad_rate, grad_maps, all_beside


def split_heads(qkv_low):
    count = qkv_low.shape[0]
    group_size = HEADS // KV_HEADS
    query_width = HEADS * HEAD_DIM
    kv_width = KV_HEADS * HEAD_DIM
    query_rows = qkv_low[:, :query_width].reshape(count, KV_HEADS, group_size, HEAD_DIM)
    key_rows = qkv_low[:, query_width : query_width + kv_width].reshape(count, KV_HEADS, HEAD_DIM)
    value_rows = qkv_low[:, query_width + kv_width :].reshape(count, KV_HEADS, HEAD_DIM)
    return (query_rows, key_rows, value_rows)


def masked_scores(query_rows, key_rows, allowed):
    attention_scores = jnp.einsum(
        "jzhx,kzx->zhjk", query_rows, key_rows, preferred_element_type=f32
    ) * HEAD_DIM ** (-0.5)
    return jnp.where(allowed[None, None], attention_scores, -1e30)


def attention_forward(qkv_low, allowed):
    count = qkv_low.shape[0]
    query_rows, key_rows, value_rows = split_heads(qkv_low)
    attention_scores = masked_scores(query_rows, key_rows, allowed)
    row_max = jnp.max(attention_scores, axis=-1, keepdims=True)
    weights_exp = jnp.exp(attention_scores - row_max)
    row_total = jnp.sum(weights_exp, axis=-1, keepdims=True)
    lowered_probabilities = (weights_exp / row_total).astype(bf16)
    attended_values = jnp.einsum(
        "lpho,ole->hlpe", lowered_probabilities, value_rows, preferred_element_type=f32
    )
    return (attended_values.reshape(count, HEADS * HEAD_DIM), row_max + jnp.log(row_total))


def attention_backward(qkv_low, grad_low, log_total, allowed):
    count = qkv_low.shape[0]
    query_rows, key_rows, value_rows = split_heads(qkv_low)
    probabilities = jnp.exp(masked_scores(query_rows, key_rows, allowed) - log_total)
    head_gradient = grad_low.reshape(count, KV_HEADS, HEADS // KV_HEADS, HEAD_DIM)
    grad_probs = jnp.einsum(
        "jzhx,kzx->zhjk", head_gradient, value_rows, preferred_element_type=f32
    )
    score_gradient = (
        probabilities * (grad_probs - jnp.sum(grad_probs * probabilities, axis=-1, keepdims=True))
    ).astype(bf16)
    scale_factor_scores = HEAD_DIM ** (-0.5)
    grad_queries = (
        jnp.einsum("lpho,ole->hlpe", score_gradient, key_rows, preferred_element_type=f32)
        * scale_factor_scores
    )
    grad_keys = (
        jnp.einsum("wniv,iwne->vwe", score_gradient, query_rows, preferred_element_type=f32)
        * scale_factor_scores
    )
    grad_values = jnp.einsum(
        "wniv,iwne->vwe", probabilities.astype(bf16), head_gradient, preferred_element_type=f32
    )
    return jnp.concatenate(
        [
            grad_queries.reshape(count, -1),
            grad_keys.reshape(count, -1),
            grad_values.reshape(count, -1),
        ],
        axis=1,
    )


def tied(value, *others):
    return lax.optimization_barrier((value,) + others)[0]


def by_row(value):
    return with_layout_constraint(value, Layout(major_to_minor=(0, 1)))


def silu_and_slope(value):
    gate = jax.nn.sigmoid(value)
    return value * gate, gate * (1.0 + value * (1.0 - gate))


def shift_down(rows, amount):
    return jnp.concatenate([jnp.zeros((amount,) + rows.shape[1:], rows.dtype), rows[:-amount]], 0)


def shift_up(rows, amount):
    return jnp.concatenate([rows[amount:], jnp.zeros((amount,) + rows.shape[1:], rows.dtype)], 0)


def per_device(
    rep,
    fsdp,
    tokens,
    cotangent,
    lengths,
    source_slot,
    norm_in,
    w_qkv,
    w_mamba_in,
    conv_weight,
    conv_bias,
    x_proj,
    dt_proj,
    dt_bias,
    a_log,
    d_skip,
    w_mamba_out,
    norm_attn,
    norm_ssm,
    w_mix_out,
    norm_ffn,
    w_gate,
    w_up,
    w_down,
):
    count, width = tokens.shape
    block_rows = count // fsdp
    piece, ff_piece = INNER // (rep * fsdp), w_gate.shape[1] // (rep * fsdp)
    channels, ff_part = fsdp * up16(piece), fsdp * up16(ff_piece)
    qkv_part = w_qkv.shape[1] // rep
    group = rep * count
    high = lax.Precision.HIGH
    me, line = lax.axis_index("rep"), lax.axis_index("fsdp")

    def my_part(value, axis):
        rest = value.shape[axis] // (rep * fsdp)
        spare = [(0, up16(rest) - rest if i == axis else 0) for i in range(value.ndim)]
        return jnp.concatenate(
            [
                jnp.pad(lax.dynamic_slice_in_dim(value, (i * rep + me) * rest, rest, axis), spare)
                for i in range(fsdp)
            ],
            axis=axis,
        )

    def my_rows(value):
        rest = value.shape[0] // rep
        part = lax.dynamic_slice_in_dim(value, me * rest, rest, 0)
        return jnp.pad(part, ((0, up16(rest) - rest), (0, 0)))

    def line_gather(value):
        return lax.all_gather(value, "fsdp", axis=0, tiled=True)

    def line_scatter(value):
        return lax.psum_scatter(value, "fsdp", scatter_dimension=0, tiled=True)

    def swapped(rows):
        lead = count if rows.shape[0] == count else rep
        return rows.transpose(1, 0, 2).reshape(group, rows.shape[2])

    early_width = -(-(qkv_part + channels) // LANES) * LANES
    gate_at = -(-(channels + qkv_part) // LANES) * LANES
    in_width = -(-(gate_at + channels) // LANES) * LANES
    part_in = by_rows(
        functools.partial(part_in_kernel, rep, fsdp, (0, channels, gate_at)),
        (w_qkv, w_mamba_in),
        in_width,
    )
    full_in = line_gather(part_in)
    mix_part = width // rep
    part_mix = lax.dynamic_slice_in_dim(w_mix_out, me * mix_part, mix_part, 1)
    mix_size = part_mix.size
    part_mix = jnp.pad(part_mix.reshape(-1), (0, -mix_size % (16 * width))).reshape(-1, width)
    part_mout, part_down = my_rows(w_mamba_out), my_rows(w_down)

    received, cot_received = line_exchange(
        fsdp,
        0,
        trades=(
            tied(tokens, part_in).reshape(fsdp, block_rows, width),
            cotangent.reshape(fsdp, block_rows, width),
        ),
    )
    w_gate, w_up, part_mout, part_mix, part_down, received = lax.optimization_barrier(
        (w_gate, w_up, part_mout, part_mix, part_down, received)
    )
    mout_mix = line_gather(jnp.concatenate([part_mout, part_mix], axis=0))
    part_gate_up = by_rows(
        functools.partial(part_gate_up_kernel, rep, fsdp), (w_gate, w_up), 2 * ff_part
    )
    full_gate_up, full_down = line_gather(part_gate_up), line_gather(part_down)
    slots = source_slot[0]
    picks = (slots[:, None] == jnp.arange(count, dtype=jnp.int32)[None, :]).astype(bf16)
    hidden_in = dot(picks, received.reshape(count, width))
    cot_rows = dot(picks, cot_received.reshape(count, width))
    cot_low = cot_rows.astype(bf16)

    ends = jnp.cumsum(lengths[0], dtype=jnp.int32)
    positions = jnp.arange(count, dtype=jnp.int32)
    passed = positions[:, None] >= ends[None, :-1]
    seg_ids = jnp.sum(passed.astype(jnp.int32), axis=1)
    in_seq = positions - jnp.max(jnp.where(passed, ends[None, :-1], 0), axis=1)
    distance = positions[:, None] - positions[None, :]
    allowed = (seg_ids[:, None] == seg_ids[None, :]) & (distance >= 0) & (distance < WINDOW)

    normed, norm_in_pull = jax.vjp(rms_norm, hidden_in, norm_in)
    marks = jnp.broadcast_to(in_seq[:, None].astype(bf16), (count, 64))
    normed_marked = jnp.concatenate([normed.astype(bf16), marks], axis=1)
    normed_sent, cot_all = rep_exchange(rep, 1, gathers=(normed_marked, cot_low))
    cot_all = cot_all.reshape(group, width)
    normed_all = normed_sent[:, :, :width].reshape(group, width)
    in_seq_all = normed_sent[:, :, width].astype(f32).T.reshape(group, 1)

    in_out = dot(swapped(normed_all.reshape(rep, count, width)), full_in)
    xs, gate_z = in_out[:, :channels], in_out[:, gate_at : gate_at + channels]
    qkv_sent = in_out[:, channels : channels + qkv_part].astype(bf16)
    qkv_sent = swapped(qkv_sent.reshape(count, rep, qkv_part))

    conv_w, conv_b = my_part(conv_weight, 1), my_part(conv_bias, 0)
    part_x_proj, part_dt_proj = my_part(x_proj, 0), my_part(dt_proj, 1)
    part_dt_bias, part_skip = my_part(dt_bias, 0), my_part(d_skip, 0)
    rate = -jnp.exp(my_part(a_log, 1))
    conv_sum = xs * conv_w[CONV - 1] + conv_b
    for k in range(1, CONV):
        earlier = jnp.where(in_seq_all >= k, shift_down(xs, k * rep), 0.0)
        conv_sum = conv_sum + earlier * conv_w[CONV - 1 - k]
    act, act_slope = silu_and_slope(conv_sum)
    proj_sent = dot(act, part_x_proj, high).astype(bf16).reshape(count, rep, -1)
    proj_sent = proj_sent.transpose(1, 0, 2)
    proj, qkv_back = rep_exchange(
        rep, 2, alls=(proj_sent,), trades=(qkv_sent.reshape(rep, count, qkv_part),)
    )
    mout_mix = hand_on(mout_mix, proj)
    mout_mix = mout_mix.reshape(fsdp, -1, width)
    full_mout = mout_mix[:, : part_mout.shape[0]].reshape(-1, width)
    mix_t = mout_mix[:, part_mout.shape[0] :].reshape(fsdp, -1)[:, :mix_size]
    mix_t = mix_t.reshape(width, mix_part).T
    qkv_low = qkv_back.transpose(1, 0, 2).reshape(count, rep * qkv_part)
    proj = proj.transpose(1, 0, 2).astype(f32)
    dt_in = proj.reshape(group, -1)[:, :DT_RANK]
    maps = proj[:, :, DT_RANK:]
    dt_sum = dot(dt_in, part_dt_proj, high) + part_dt_bias
    step = jax.nn.softplus(dt_sum)
    decay_step = jnp.where(in_seq_all == 0.0, 1e30, step * LOG2_E)
    inputs = step * act
    cube = (count, rep, channels)
    scanned, decayed, mix_t = scan_forward(
        decay_step.reshape(cube), inputs.reshape(cube), maps, rate, rep, 9, mix_t
    )
    mix_t = mix_t.reshape(width, width)
    scanned = scanned.reshape(group, channels)
    silu_z, z_slope = silu_and_slope(gate_z)
    before_gate = scanned + part_skip * act
    mixer_low = swapped((before_gate * silu_z).astype(bf16).reshape(cube))
    ssm_part = by_row(dot(mixer_low, full_mout).astype(bf16)).reshape(rep, count, width)
    (ssm_out,) = rep_exchange(rep, 3, sums=(ssm_part,))

    attended_values, log_total = attention_forward(qkv_low, allowed)
    mixed, mix_pull = jax.vjp(mix_branches, attended_values, ssm_out, norm_attn, norm_ssm)
    mixed_low = mixed.astype(bf16)
    middle = hidden_in + dot_right_t(mixed_low, mix_t)
    ffn_in, ffn_pull = jax.vjp(rms_norm, middle, norm_ffn)
    ffn_all, mixed_all = rep_exchange(rep, 4, gathers=(ffn_in.astype(bf16), mixed_low))
    ffn_all, mixed_all = ffn_all.reshape(group, width), mixed_all.reshape(group, width)

    gate_up = dot(ffn_all, full_gate_up)
    hidden, swiglu_pull = jax.vjp(swiglu, gate_up[:, :ff_part], gate_up[:, ff_part:])
    hidden_low = hidden.astype(bf16)
    grad_hidden = dot_right_t(cot_all, full_down)
    grad_gate_up = jnp.concatenate(swiglu_pull(grad_hidden), axis=1).astype(bf16)
    part_gate_up = dot_left_t(ffn_all, grad_gate_up).astype(bf16)
    own_gate_up = line_scatter(part_gate_up)
    grad_gate_up = tied(grad_gate_up, part_gate_up)
    ffn_sent = by_row(dot_right_t(grad_gate_up, full_gate_up).astype(bf16))
    part_down = dot_left_t(hidden_low, cot_all).astype(bf16)
    own_down = line_scatter(part_down)
    down_sent = by_row(dot(tied(hidden_low, part_down), full_down).astype(bf16))
    blocks = (rep, count, width)
    grad_ffn, down_out = rep_exchange(
        rep, 5, sums=(ffn_sent.reshape(blocks), down_sent.reshape(blocks))
    )
    result = middle + down_out

    grad_middle_norm, grad_norm_ffn = ffn_pull(grad_ffn)
    grad_middle = cot_rows + grad_middle_norm
    middle_low = grad_middle.astype(bf16)
    grad_mixed = dot(middle_low, mix_t)
    grad_attended, grad_ssm, grad_norm_attn, grad_norm_ssm = mix_pull(grad_mixed)
    middle_sent = middle_low.reshape(count, rep, -1).transpose(1, 0, 2)
    qkv_grad = attention_backward(qkv_low, grad_attended.astype(bf16), log_total, allowed)
    qkv_grad = qkv_grad.astype(bf16).reshape(count, rep, -1).transpose(1, 0, 2)
    ssm_all, middle_cols, qkv_cols = rep_exchange(
        rep, 6, gathers=(grad_ssm.astype(bf16),), trades=(middle_sent, qkv_grad)
    )
    qkv_cols = qkv_cols.reshape(group, qkv_part)
    ssm_all = tied(ssm_all, own_gate_up).reshape(group, width)
    grad_mixer = dot_right_t(ssm_all, full_mout).astype(bf16).reshape(rep, count, channels)
    grad_mixer = swapped(grad_mixer).astype(f32)
    part_mout = dot_left_t(mixer_low, ssm_all).astype(bf16)
    part_mix = dot_left_t(mixed_all, middle_cols.reshape(group, -1)).astype(bf16)

    grad_z = (grad_mixer * before_gate * z_slope).astype(bf16)
    grad_z = swapped(grad_z.reshape(cube))
    spare = early_width - qkv_part - channels
    early_grad = jnp.concatenate([qkv_cols, jnp.zeros((group, spare), bf16), grad_z], axis=1)
    part_early = dot_left_t(normed_all, early_grad).astype(bf16)
    grad_mixer = tied(grad_mixer, part_mout, part_mix, part_early, own_down)
    own_mout, own_mix = line_scatter(part_mout), line_scatter(part_mix)
    own_early = line_scatter(part_early)
    grad_before = grad_mixer * silu_z
    grad_skip = jnp.sum(grad_before * act, axis=0)
    grad_inputs, grad_step, grad_rate, grad_maps, (all_gate_up, all_down) = scan_backward(
        *(item.reshape(cube) for item in (decay_step, step, inputs)),
        maps,
        grad_before.reshape(cube),
        decayed,
        rate,
        rep,
        7,
        (own_gate_up, own_down),
    )
    grad_inputs = grad_inputs.reshape(group, channels)
    grad_step = grad_step.reshape(group, channels)
    grad_a_log = grad_rate * rate
    grad_step = grad_step + grad_inputs * act
    grad_dt = grad_step * jax.nn.sigmoid(dt_sum)
    grad_dt_bias = jnp.sum(grad_dt, axis=0)
    grad_dt_proj = dot_left_t(dt_in, grad_dt)
    proj_sent = jnp.concatenate(
        [dot_right_t(grad_dt, part_dt_proj), grad_maps], axis=1
    )
    proj_sent = proj_sent.astype(bf16).reshape(count, rep, -1).transpose(1, 0, 2)
    (grad_proj,) = rep_exchange(rep, 11, alls=(proj_sent,))
    grad_proj = swapped(tied(grad_proj, own_mout, own_mix))
    grad_x_proj = dot_left_t(grad_proj, act)
    grad_act = grad_before * part_skip + grad_inputs * step + dot_right_t(grad_proj, part_x_proj)
    grad_conv = grad_act * act_slope
    grad_conv_b = jnp.sum(grad_conv, axis=0)
    grad_conv_w = [jnp.sum(grad_conv * xs, axis=0)]
    grad_xs = grad_conv * conv_w[CONV - 1]
    for k in range(1, CONV):
        reached = jnp.where(in_seq_all >= k, grad_conv, 0.0)
        grad_conv_w.insert(0, jnp.sum(reached * shift_down(xs, k * rep), axis=0))
        grad_xs = grad_xs + shift_up(reached, k * rep) * conv_w[CONV - 1 - k]
    small = jnp.concatenate(
        [jnp.stack(grad_conv_w), grad_conv_b[None], grad_dt_bias[None], grad_skip[None]]
        + [grad_a_log, grad_dt_proj, grad_x_proj],
        axis=0,
    )
    n_small = fsdp * up16(-(-small.shape[0] // fsdp))
    small = jnp.pad(small, ((0, n_small - small.shape[0]), (0, 0))).astype(bf16)
    grad_xs = swapped(grad_xs.astype(bf16).reshape(cube))
    gap = jnp.zeros((group, gate_at - channels - qkv_part), bf16)
    end = jnp.zeros((group, in_width - gate_at - channels), bf16)
    in_grad = jnp.concatenate([grad_xs, qkv_cols, gap, grad_z, end], axis=1)
    normed_part = by_row(dot_right_t(in_grad, full_in).astype(bf16)).reshape(blocks)
    own_late = line_scatter(dot_left_t(normed_all, grad_xs).astype(bf16))
    (grad_normed,) = rep_exchange(rep, 8, sums=(normed_part,))
    grad_hidden_norm, grad_norm_in = norm_in_pull(grad_normed)
    grad_hidden_in = grad_middle + grad_hidden_norm

    def given_back(rows):
        return dot_left_t(picks, rows.astype(bf16)).astype(bf16).reshape(fsdp, block_rows, width)

    gains = jnp.stack([grad_norm_in, grad_norm_attn, grad_norm_ssm, grad_norm_ffn])
    gains = jnp.concatenate([gains, jnp.zeros((4, width), f32)], axis=0)
    (
        sum_gate,
        sum_up,
        sum_down,
        all_mout,
        all_mix,
        all_early,
        all_late,
        small,
        gains,
        mixed_out,
        grad_tokens,
    ) = last_exchange(
        rep,
        fsdp,
        10,
        (all_gate_up, all_down, w_gate.shape[1], w_down.shape[0]),
        (own_mout, own_mix, own_early, own_late),
        small.reshape(fsdp, -1, channels),
        gains,
        (given_back(result), given_back(grad_hidden_in)),
    )
    gains, small = jnp.sum(gains, axis=0), small.reshape(rep, n_small, channels)
    sum_mamba_in, sum_qkv, sum_mix = join_columns(
        rep,
        (all_late, all_early, all_mix),
        (w_mamba_in.shape[1], w_qkv.shape[1], width),
        (
            ((0, 0, piece, 0, fsdp), (1, early_width - channels, piece, INNER, fsdp)),
            ((1, 0, qkv_part, 0, 1),),
            ((2, 0, width // rep, 0, 1),),
        ),
    )
    sum_mout = join_rows(rep, all_mout, w_mamba_out.shape[0], width)

    (small,) = join_columns(rep, (small,), (INNER,), (((0, 0, piece, 0, fsdp),),))
    ends = [CONV, CONV + 1, CONV + 2, CONV + 3, CONV + 3 + STATE, CONV + 3 + STATE + DT_RANK]
    ends.append(ends[-1] + x_proj.shape[1])
    return (
        mixed_out.reshape(count, width),
        grad_tokens.reshape(count, width),
        gains[0],
        sum_qkv,
        sum_mamba_in,
        small[: ends[0]],
        small[ends[0]],
        small[ends[5] : ends[6]].T,
        small[ends[4] : ends[5]],
        small[ends[1]],
        small[ends[3] : ends[4]],
        small[ends[2]],
        sum_mout,
        gains[1],
        gains[2],
        sum_mix,
        gains[3],
        sum_gate.astype(f32),
        sum_up.astype(f32),
        sum_down.astype(f32).T,
    )


def solution(mesh):
    rows = P(("rep", "fsdp"), None)
    cut = P("fsdp", None)
    whole = P()
    return jax.shard_map(
        functools.partial(per_device, mesh.shape["rep"], mesh.shape["fsdp"]),
        mesh=mesh,
        in_specs=(rows,) * 4
        + (whole, cut, cut)
        + (whole,) * 7
        + (cut, whole, whole, cut, whole, cut, cut, cut),
        out_specs=(rows, rows, whole, cut, cut)
        + (whole,) * 7
        + (cut, whole, whole, cut, whole, cut, cut, cut),
        check_vma=False,
    )
```

```python
import functools

import jax
import jax.numpy as jnp
from jax import lax
from jax.experimental import pallas as pl
from jax.experimental.layout import Layout, with_layout_constraint
from jax.experimental.pallas import tpu as pltpu
from jax.sharding import PartitionSpec as P

HEADS = 25
KV_HEADS = 5
HEAD_DIM = 64
INNER = 3200
STATE = 16
DT_RANK = 100
CONV = 4
WINDOW = 1024
LANES = 128
PACKS = 8
LOG2_E = 1.4426950408889634

epsilon = 1e-06
bf16 = jnp.bfloat16
f32 = jnp.float32


def dot(left, right, precision=None):
    return jnp.dot(left, right, precision=precision, preferred_element_type=f32)


def dot_right_t(left, right):
    return lax.dot_general(left, right, (((1,), (1,)), ((), ())), preferred_element_type=f32)


def dot_left_t(left, right):
    return lax.dot_general(left, right, (((0,), (0,)), ((), ())), preferred_element_type=f32)


def rms_norm(value_rows, gain):
    return (
        value_rows
        * lax.rsqrt(jnp.mean(value_rows * value_rows, axis=-1, keepdims=True) + epsilon)
        * gain
    )


def mix_branches(attended_values, ssm_out, norm_attn, norm_ssm):
    return (rms_norm(attended_values, norm_attn) + rms_norm(ssm_out, norm_ssm)) * 0.5


def swiglu(gate_val, up_val):
    return jax.nn.silu(gate_val) * up_val


def hbm_spec():
    return pl.BlockSpec(memory_space=pl.ANY)


def vmem_spec():
    return pl.BlockSpec(memory_space=pltpu.VMEM)


SMALL_COST = pl.CostEstimate(flops=0, bytes_accessed=10**4, transcendentals=0)


def send(src, dst, sems, axis, target):
    copy = pltpu.make_async_remote_copy(
        src_ref=src,
        dst_ref=dst,
        send_sem=sems[0],
        recv_sem=sems[1],
        device_id={axis: target},
        device_id_type=pl.DeviceIdType.MESH,
    )
    copy.start()
    return copy


def meet(axis, others):
    barrier = pltpu.get_barrier_semaphore()
    for other in others:
        pl.semaphore_signal(
            barrier, inc=1, device_id={axis: other}, device_id_type=pl.DeviceIdType.MESH
        )
    pl.semaphore_wait(barrier, len(others))


def rep_kernel(rep, counts, square, *refs):
    n_gather, n_sum, n_all, n_trade = counts
    chips = rep // 2
    refs = list(refs)

    def take(n):
        taken = refs[:n]
        del refs[:n]
        return taken

    gathers, sums, alls, trades = (take(n) for n in counts)
    gathered, summed, all_summed, traded = (take(n) for n in counts)
    reduced = sums + alls
    buffers = [take(3) for _ in reduced]
    totals = summed + take(n_all)
    local, far, near, direct = refs

    me = lax.axis_index("rep")
    core = lax.rem(me, 2)
    chip = (me - core) // 2
    partner = 2 * chip + 1 - core
    ahead = [lax.rem(chip + k, chips) for k in range(chips)]
    behind = [lax.rem(chip + chips - k, chips) for k in range(chips)]
    if square:
        along_x, along_y = chip + 1 - 2 * lax.rem(chip, 2), lax.rem(chip + 2, 4)
        first = along_x + core * (along_y - along_x)
        second = along_y + core * (along_x - along_y)
        across = 3 - chip
        linked = [2 * first + core, 2 * second + core]
    else:
        linked = [2 * ahead[k] + core for k in range(1, chips)]
    if n_trade:
        meet("rep", [lax.rem(me + k, rep) for k in range(1, rep)])
    else:
        meet("rep", linked + [partner])

    kept, sent = [], []

    def keep(src, dst):
        copy = pltpu.make_async_copy(src, dst, local.at[len(kept)])
        copy.start()
        kept.append(copy)

    def far_send(src, dst, slot, k, target):
        copy = send(src, dst, (far.at[0, slot, k], far.at[1, slot, k]), "rep", 2 * target + core)
        sent.append(copy)
        return copy

    def near_send(src, dst, slot, k):
        copy = send(src, dst, (near.at[0, slot, k], near.at[1, slot, k]), "rep", partner)
        sent.append(copy)
        return copy

    def start_gather(source, out, slot):
        if square:
            far_copies = [
                far_send(source, out.at[me], slot, 1, first),
                far_send(source, out.at[me], slot, 2, second),
            ]
        else:
            far_copies = [
                far_send(source, out.at[me], slot, k, ahead[k]) for k in range(1, chips)
            ]
        near_copies = [near_send(source, out.at[me], slot, 0)]
        keep(source, out.at[me])
        return out, slot, far_copies, near_copies

    def pass_on(states):
        if square:
            for out, slot, far_copies, near_copies in states:
                block = out.at[2 * first + core]
                far_copies[0].wait_recv()
                far_copies.append(far_send(block, block, slot, 3, second))
                near_copies.append(near_send(block, block, slot, 1))
            for out, slot, far_copies, near_copies in states:
                for k, source in ((2, second), (3, across)):
                    block = out.at[2 * source + core]
                    far_copies[k - 1].wait_recv()
                    near_copies.append(near_send(block, block, slot, k))
        else:
            for out, slot, far_copies, near_copies in states:
                for k in range(1, chips):
                    block = out.at[2 * behind[k] + core]
                    far_copies[k - 1].wait_recv()
                    near_copies.append(near_send(block, block, slot, k))
        for _, _, _, near_copies in states:
            for copy in near_copies:
                copy.wait_recv()

    dests = [chip, first, across, second] if square else ahead
    partner_dests = [chip, second, across, first] if square else ahead
    order = [1, 2, 3, 0] if square else [*range(1, chips), 0]
    crossing = []
    for i, source in enumerate(reduced):
        from_partner = buffers[i][1]
        crossing.append(
            {
                k: near_send(source.at[2 * partner_dests[k] + 1 - core], from_partner.at[k], i, k)
                for k in order
            }
        )
    states = [
        start_gather(source, gathered[i], len(reduced) + n_all + i)
        for i, source in enumerate(gathers)
    ]
    trading = []
    for i, source in enumerate(trades):
        keep(source.at[me], traded[i].at[me])
        for k in range(1, rep):
            target = lax.rem(me + k, rep)
            copy = send(
                source.at[target],
                traded[i].at[me],
                (direct.at[0, i, k], direct.at[1, i, k]),
                "rep",
                target,
            )
            trading.append(copy)

    def of_chip(i, k):
        crossing[i][k].wait_recv()
        own = reduced[i][2 * dests[k] + core]
        return own.astype(f32) + buffers[i][1][k].astype(f32)

    crossed = []
    for i in range(len(reduced)):
        low, _, arrived = buffers[i]
        copies = []
        for k in (1, 2) if square else range(1, chips):
            low[k - 1] = of_chip(i, k).astype(low.dtype)
            target = first if square else ahead[k]
            copies.append(far_send(low.at[k - 1], arrived.at[k - 1], i, k, target))
        crossed.append(copies)
    if square:
        for i in range(len(reduced)):
            low, _, arrived = buffers[i]
            value = of_chip(i, 3)
            crossed[i][1].wait_recv()
            low[2] = (value + arrived[1].astype(f32)).astype(low.dtype)
            crossed[i].append(far_send(low.at[2], arrived.at[2], i, 3, second))
    for i in range(len(reduced)):
        arrived = buffers[i][2]
        total = of_chip(i, 0)
        for k in (1, 3) if square else range(1, chips):
            crossed[i][k - 1].wait_recv()
            total = total + arrived[k - 1].astype(f32)
        totals[i][...] = total.astype(totals[i].dtype)
        if i >= n_sum:
            states.append(start_gather(totals[i], all_summed[i - n_sum], n_all + i))
    pass_on(states)
    for copy in trading:
        copy.wait()
    for copy in sent:
        copy.wait_send()
    for copy in kept:
        copy.wait()


def rep_exchange(rep, collective_id, gathers=(), sums=(), alls=(), trades=()):
    chips = rep // 2
    square = rep == 8 and not alls
    counts = (len(gathers), len(sums), len(alls), len(trades))
    reduced = (*sums, *alls)
    out_shape = [jax.ShapeDtypeStruct((rep,) + x.shape, x.dtype) for x in gathers]
    out_shape += [jax.ShapeDtypeStruct(x.shape[1:], f32) for x in sums]
    out_shape += [jax.ShapeDtypeStruct(x.shape, x.dtype) for x in (*alls, *trades)]
    scratch = []
    for x in reduced:
        scratch += [
            pltpu.VMEM((n,) + x.shape[1:], x.dtype) for n in (chips - 1, chips, chips - 1)
        ]
    scratch += [pltpu.VMEM(x.shape[1:], x.dtype) for x in alls]
    n_local = sum(counts) - len(sums) + 1
    n_slots = len(reduced) + len(alls) + len(gathers) + 1
    scratch += [
        pltpu.SemaphoreType.DMA((n_local,)),
        pltpu.SemaphoreType.DMA((2, n_slots, chips)),
        pltpu.SemaphoreType.DMA((2, n_slots, chips)),
        pltpu.SemaphoreType.DMA((2, len(trades) + 1, rep)),
    ]
    return pl.pallas_call(
        functools.partial(rep_kernel, rep, counts, square),
        out_shape=out_shape,
        in_specs=[vmem_spec()] * sum(counts),
        out_specs=[hbm_spec()] * len(gathers)
        + [vmem_spec()] * len(sums)
        + [hbm_spec()] * (len(alls) + len(trades)),
        scratch_shapes=scratch,
        compiler_params=pltpu.CompilerParams(
            collective_id=collective_id,
            has_side_effects=True,
            vmem_limit_bytes=40 * 1024 * 1024,
        ),
        cost_estimate=SMALL_COST,
    )(*gathers, *sums, *alls, *trades)


def line_kernel(count, counts, *refs):
    n_gather, n_all, n_trade = counts
    n_in = sum(counts)
    ins, outs, scratch = refs[:n_in], refs[n_in : 2 * n_in], refs[2 * n_in :]
    arrived, totals = scratch[:n_all], scratch[n_all : 2 * n_all]
    local, remote = scratch[2 * n_all :]
    me = lax.axis_index("fsdp")
    others = [lax.rem(me + k, count) for k in range(1, count)]
    meet("fsdp", others)
    copies, coming = [], []

    def push(block, out, slot):
        return [
            send(block(other), out, (remote.at[0, slot, k], remote.at[1, slot, k]), "fsdp", other)
            for k, other in enumerate(others)
        ]

    def keep(block, out, slot):
        copy = pltpu.make_async_copy(block, out, local.at[slot])
        copy.start()
        copies.append(copy)

    for i in range(n_all):
        source = ins[n_gather + i]
        coming.append(push(lambda other: source.at[other], arrived[i].at[me], n_in + i))
    for i in range(n_in):
        if i < n_gather:
            keep(ins[i], outs[i].at[me], i)
            copies += push(lambda other: ins[i], outs[i].at[me], i)
        elif i >= n_gather + n_all:
            keep(ins[i].at[me], outs[i].at[me], i)
            copies += push(lambda other: ins[i].at[other], outs[i].at[me], i)
    for i in range(n_all):
        for copy in coming[i]:
            copy.wait()
        total = ins[n_gather + i][me].astype(f32)
        for other in others:
            total = total + arrived[i][other].astype(f32)
        totals[i][...] = total.astype(totals[i].dtype)
        out = outs[n_gather + i]
        keep(totals[i], out.at[me], n_gather + i)
        copies += push(lambda other: totals[i], out.at[me], n_gather + i)
    for copy in copies:
        copy.wait()


def line_exchange(count, collective_id, gathers=(), alls=(), trades=()):
    arrays = (*gathers, *alls, *trades)
    out_shape = [jax.ShapeDtypeStruct((count,) + x.shape, x.dtype) for x in gathers]
    out_shape += [jax.ShapeDtypeStruct(x.shape, x.dtype) for x in (*alls, *trades)]
    return pl.pallas_call(
        functools.partial(line_kernel, count, (len(gathers), len(alls), len(trades))),
        out_shape=out_shape,
        in_specs=[vmem_spec()] * len(arrays),
        out_specs=[hbm_spec()] * len(arrays),
        scratch_shapes=[pltpu.VMEM(x.shape, x.dtype) for x in alls]
        + [pltpu.VMEM(x.shape[1:], x.dtype) for x in alls]
        + [
            pltpu.SemaphoreType.DMA((len(arrays),)),
            pltpu.SemaphoreType.DMA((2, len(arrays) + len(alls), count)),
        ],
        compiler_params=pltpu.CompilerParams(collective_id=collective_id, has_side_effects=True),
        cost_estimate=SMALL_COST,
    )(*arrays)


def remote_copy(src, dst, sems, axis, target):
    return pltpu.make_async_remote_copy(
        src_ref=src,
        dst_ref=dst,
        send_sem=sems[0],
        recv_sem=sems[1],
        device_id={axis: target},
        device_id_type=pl.DeviceIdType.MESH,
    )


class Gathers:
    def __init__(self, rep):
        chips, self.square = rep // 2, rep == 8
        self.me = lax.axis_index("rep")
        self.core = lax.rem(self.me, 2)
        chip = (self.me - self.core) // 2
        self.partner = 2 * chip + 1 - self.core
        if self.square:
            along_x, along_y = chip + 1 - 2 * lax.rem(chip, 2), lax.rem(chip + 2, 4)
            first = along_x + self.core * (along_y - along_x)
            second = along_y + self.core * (along_x - along_y)
            hops, sources = [first, second], [first, second, 3 - chip]
        else:
            hops = [lax.rem(chip + k, chips) for k in range(1, chips)]
            sources = [lax.rem(chip + chips - k, chips) for k in range(1, chips)]
        self.hops = [2 * hop + self.core for hop in hops]
        self.sources = [2 * source + self.core for source in sources]

    def plan(self, source, out, far, near, local, i):
        blocks = [out.at[origin] for origin in self.sources]

        def over(sems, src, dst, k, target):
            return remote_copy(src, dst, (sems.at[0, i, k], sems.at[1, i, k]), "rep", target)

        own = [over(far, source, out.at[self.me], k, hop) for k, hop in enumerate(self.hops)]
        if self.square:
            own.append(over(far, blocks[0], blocks[0], 2, self.hops[1]))
        across = [over(near, block, block, k, self.partner) for k, block in enumerate(blocks)]
        across.append(over(near, source, out.at[self.me], len(blocks), self.partner))
        return own, across, pltpu.make_async_copy(source, out.at[self.me], local.at[i])

    def begin(self, plan):
        own, across, keep = plan
        for copy in own[: len(self.hops)]:
            copy.start()
        across[-1].start()
        keep.start()

    def first_hop(self, plan):
        own, across, _ = plan
        own[0].wait_recv()
        if self.square:
            own[2].start()
        across[0].start()

    def second_hop(self, plan):
        own, across, _ = plan
        for k in range(1, len(self.hops)):
            own[k].wait_recv()
            across[k].start()

    def relayed(self, plan):
        own, across, _ = plan
        if self.square:
            own[2].wait_recv()
            across[2].start()

    def end(self, plan):
        own, across, keep = plan
        for copy in across:
            copy.wait()
        for copy in own:
            copy.wait_send()
        keep.wait()


def last_kernel(rep, fsdp, square, n_gather, layout, down_rows, *refs):
    parts_gate_up, parts_down, refs = refs[0], refs[1], refs[2:]
    gathers, refs = refs[:n_gather], refs[n_gather:]
    small, gains, trades, refs = refs[0], refs[1], refs[2:4], refs[4:]
    joined_gate, joined_up, joined_down, refs = refs[0], refs[1], refs[2], refs[3:]
    gathered, refs = refs[:n_gather], refs[n_gather:]
    small_out, gains_out, traded, refs = refs[0], refs[1], refs[2:4], refs[4:]
    arrived, total, lined, gains_in, gains_sum, local, far, near, keeping, remote = refs

    line = lax.axis_index("fsdp")
    others = [lax.rem(line + k, fsdp) for k in range(1, fsdp)]
    along = Gathers(rep)

    def push(block, out, slot):
        return [
            remote_copy(
                block(other), out, (remote.at[0, slot, k], remote.at[1, slot, k]), "fsdp", other
            )
            for k, other in enumerate(others)
        ]

    gains_plan = along.plan(gains, gains_in, far, near, local, 0)
    plans = [
        along.plan(gathers[i], gathered[i], far, near, local, 1 + i) for i in range(n_gather)
    ]
    small_plan = along.plan(lined, small_out, far, near, local, 1 + n_gather)
    small_in = push(lambda other: small.at[other], arrived.at[line], 0)
    small_back = push(lambda other: total, lined.at[line], 3)
    gains_push = push(lambda other: gains_sum, gains_out.at[line], 4)
    gains_keep = pltpu.make_async_copy(gains_sum, gains_out.at[line], keeping.at[2])
    traffic = []
    for i in range(2):
        source = trades[i]
        traffic += push(lambda other: source.at[other], traded[i].at[line], 1 + i)
        traffic.append(
            pltpu.make_async_copy(source.at[line], traded[i].at[line], keeping.at[i])
        )
    step, steps = pl.program_id(0), pl.num_programs(0)

    @pl.when(step == 0)
    def _():
        barrier = pltpu.get_barrier_semaphore()
        met = [("rep", index) for index in (*along.hops, along.partner)]
        met += [("fsdp", index) for index in others]
        for axis, index in met:
            pl.semaphore_signal(
                barrier, inc=1, device_id={axis: index}, device_id_type=pl.DeviceIdType.MESH
            )
        pl.semaphore_wait(barrier, len(met))
        for copy in small_in:
            copy.start()
        along.begin(gains_plan)
        for plan in plans:
            along.begin(plan)
        for copy in traffic:
            copy.start()

    join_kernel(rep, layout, parts_gate_up, joined_gate, joined_up)
    join_rows_kernel(rep, down_rows, True, parts_down, joined_down)

    @pl.when(step == steps - 1)
    def _():
        for copy in small_in:
            copy.wait()
        value = small[line].astype(f32)
        for other in others:
            value = value + arrived[other].astype(f32)
        total[...] = value.astype(total.dtype)
        for copy in small_back:
            copy.start()
        lined[line] = total[...]
        for plan in (gains_plan, *plans):
            along.first_hop(plan)
        for plan in (gains_plan, *plans):
            along.second_hop(plan)
        along.relayed(gains_plan)
        along.end(gains_plan)
        gains_sum[...] = jnp.sum(gains_in[...], axis=0)
        for copy in gains_push:
            copy.start()
        gains_keep.start()
        for copy in small_back:
            copy.wait()
        along.begin(small_plan)
        for plan in plans:
            along.relayed(plan)
        along.first_hop(small_plan)
        along.second_hop(small_plan)
        along.relayed(small_plan)
        for plan in (*plans, small_plan):
            along.end(plan)
        for copy in (*traffic, *gains_push, gains_keep):
            copy.wait()


def last_exchange(rep, fsdp, collective_id, ffn, gathers, small, gains, trades):
    n_gather, chips = len(gathers), rep // 2
    parts_gate_up, parts_down, ff_width, ff_rows = ffn
    rows, ff_part, width = parts_gate_up.shape[1], parts_gate_up.shape[2] // 2, gains.shape[1]
    block, columns = next(n for n in (80, 40, 64, rows) if rows % n == 0), 2 * LANES
    steps, row_steps = pl.cdiv(width, columns), rows // block
    rest = ff_width // rep // fsdp
    layout = (((0, 0, rest, 0, fsdp),), ((0, ff_part, rest, 0, fsdp),))

    def row_at(i):
        return lax.div(i * row_steps, steps)

    out_shape = [jax.ShapeDtypeStruct((rows, ff_width), bf16)] * 2
    out_shape.append(jax.ShapeDtypeStruct((width, ff_rows), bf16))
    out_shape += [jax.ShapeDtypeStruct((rep,) + x.shape, x.dtype) for x in gathers]
    out_shape.append(jax.ShapeDtypeStruct((rep,) + small.shape, small.dtype))
    out_shape.append(jax.ShapeDtypeStruct((fsdp,) + gains.shape, gains.dtype))
    out_shape += [jax.ShapeDtypeStruct(x.shape, x.dtype) for x in trades]
    return pl.pallas_call(
        functools.partial(
            last_kernel, rep, fsdp, rep == 8, n_gather, layout, ff_rows // rep
        ),
        grid=(steps,),
        out_shape=out_shape,
        in_specs=[
            pl.BlockSpec((rep, block, 2 * ff_part), lambda i: (0, row_at(i), 0)),
            pl.BlockSpec((rep, parts_down.shape[1], columns), lambda i: (0, 0, i)),
        ]
        + [vmem_spec()] * (n_gather + 4),
        out_specs=[pl.BlockSpec((block, ff_width), lambda i: (row_at(i), 0))] * 2
        + [pl.BlockSpec((columns, ff_rows), lambda i: (i, 0))]
        + [hbm_spec()] * (n_gather + 4),
        scratch_shapes=[
            pltpu.VMEM(small.shape, small.dtype),
            pltpu.VMEM(small.shape[1:], small.dtype),
            pltpu.VMEM(small.shape, small.dtype),
            pltpu.VMEM((rep,) + gains.shape, gains.dtype),
            pltpu.VMEM(gains.shape, gains.dtype),
            pltpu.SemaphoreType.DMA((n_gather + 2,)),
            pltpu.SemaphoreType.DMA((2, n_gather + 2, chips)),
            pltpu.SemaphoreType.DMA((2, n_gather + 2, chips)),
            pltpu.SemaphoreType.DMA((3,)),
            pltpu.SemaphoreType.DMA((2, 5, fsdp)),
        ],
        compiler_params=pltpu.CompilerParams(
            collective_id=collective_id,
            has_side_effects=True,
            vmem_limit_bytes=48 * 1024 * 1024,
        ),
        cost_estimate=SMALL_COST,
    )(parts_gate_up, parts_down, *gathers, small, gains, *trades)


def hand_kernel(_value, _after, _out):
    pass


def hand_on(value, after):
    return pl.pallas_call(
        hand_kernel,
        out_shape=jax.ShapeDtypeStruct(value.shape, value.dtype),
        in_specs=[hbm_spec()] * 2,
        out_specs=hbm_spec(),
        input_output_aliases={0: 0},
        cost_estimate=SMALL_COST,
    )(value, after)


def windows(width, pieces, start, step, rest):
    wide = min(-(-(rest + LANES - 1) // LANES) * LANES, width)
    me = lax.axis_index("rep")
    for i in range(pieces):
        at = start + i * step + me * rest
        aligned = jnp.minimum((at // LANES) * LANES, (width - wide) // LANES * LANES)
        yield pl.multiple_of(aligned, LANES), at - aligned, wide


def up16(size):
    return -(-size // 16) * 16


def copy_parts(rep, fsdp, source, out, place, start, total):
    rest = total // (rep * fsdp)
    rows = source.shape[0]
    for aligned, shift, wide in windows(source.shape[1], fsdp, start, rep * rest, rest):
        value = source[:, pl.ds(aligned, wide)].astype(f32)
        value = pltpu.roll(value, lax.rem(wide - shift, wide), 1)[:, :rest]
        if up16(rest) > rest:
            value = jnp.concatenate([value, jnp.zeros((rows, up16(rest) - rest), f32)], axis=1)
        out[:, place : place + up16(rest)] = value.astype(bf16)
        place += up16(rest)


def part_in_kernel(rep, fsdp, spots, qkv_ref, min_ref, out_ref):
    _, qkv_at, gate_at = spots
    rows, qkv_width = qkv_ref.shape
    qkv_part = qkv_width // rep
    out_ref[...] = jnp.zeros_like(out_ref)
    copy_parts(rep, fsdp, min_ref, out_ref, 0, 0, INNER)
    copy_parts(rep, fsdp, min_ref, out_ref, gate_at, INNER, INNER)
    value = qkv_ref[...].astype(f32)
    padded = -(-qkv_width // LANES) * LANES
    value = jnp.concatenate([value, jnp.zeros((rows, padded - qkv_width), f32)], axis=1)
    shift = padded - lax.axis_index("rep") * qkv_part
    value = pltpu.roll(value, lax.rem(shift, padded), 1)
    out_ref[:, qkv_at : qkv_at + qkv_part] = value[:, :qkv_part].astype(bf16)


def part_gate_up_kernel(rep, fsdp, gate_ref, up_ref, out_ref):
    copy_parts(rep, fsdp, gate_ref, out_ref, 0, 0, gate_ref.shape[1])
    copy_parts(rep, fsdp, up_ref, out_ref, out_ref.shape[1] // 2, 0, up_ref.shape[1])


def by_rows(kernel, sources, width):
    rows = sources[0].shape[0]
    block = 80 if rows % 80 == 0 else rows
    return pl.pallas_call(
        kernel,
        grid=(rows // block,),
        in_specs=[pl.BlockSpec((block, x.shape[1]), lambda i: (i, 0)) for x in sources],
        out_specs=pl.BlockSpec((block, width), lambda i: (i, 0)),
        out_shape=jax.ShapeDtypeStruct((rows, width), bf16),
        compiler_params=pltpu.CompilerParams(vmem_limit_bytes=40 * 1024 * 1024),
        cost_estimate=SMALL_COST,
    )(*sources)


def join_kernel(rep, layout, *refs):
    sources, outs = refs[: len(refs) - len(layout)], refs[len(refs) - len(layout) :]
    for out, entries in zip(outs, layout):
        for index, first, rest, place, pieces in entries:
            for i in range(pieces):
                start = first + i * up16(rest)
                for r in range(rep):
                    at = place + (i * rep + r) * rest
                    piece = sources[index][r, :, start : start + rest]
                    out[:, at : at + rest] = piece.astype(out.dtype)


def join_rows_kernel(rep, rows, flip, source, out):
    for r in range(rep):
        if flip:
            out[:, r * rows : (r + 1) * rows] = source[r].astype(f32).T[:, :rows].astype(out.dtype)
        else:
            out[r * rows : (r + 1) * rows, :] = source[r, :rows, :].astype(f32)


def join_rows(rep, source, total, width, flip=False):
    block = 2 * LANES
    shape = (total, width)
    out_spec = pl.BlockSpec((total, block), lambda i: (0, i))
    if flip:
        shape = (width, total)
        out_spec = pl.BlockSpec((block, total), lambda i: (i, 0))
    return pl.pallas_call(
        functools.partial(join_rows_kernel, rep, total // rep, flip),
        grid=(pl.cdiv(width, block),),
        in_specs=[pl.BlockSpec((rep, source.shape[1], block), lambda i: (0, 0, i))],
        out_specs=out_spec,
        out_shape=jax.ShapeDtypeStruct(shape, f32),
        compiler_params=pltpu.CompilerParams(vmem_limit_bytes=40 * 1024 * 1024),
        cost_estimate=SMALL_COST,
    )(source)


def join_columns(rep, sources, widths, layout):
    rows = sources[0].shape[1]
    block = next(n for n in (80, 40, 64, rows) if rows % n == 0)
    return pl.pallas_call(
        functools.partial(join_kernel, rep, layout),
        grid=(rows // block,),
        in_specs=[
            pl.BlockSpec((rep, block, x.shape[2]), lambda i: (0, i, 0)) for x in sources
        ],
        out_specs=[pl.BlockSpec((block, width), lambda i: (i, 0)) for width in widths],
        out_shape=[jax.ShapeDtypeStruct((rows, width), f32) for width in widths],
        compiler_params=pltpu.CompilerParams(vmem_limit_bytes=48 * 1024 * 1024),
        cost_estimate=SMALL_COST,
    )(*sources)


def spread_beside(rep, steps, pairs, local, far, near):
    along = Gathers(rep)
    plans = [along.plan(*pair, far, near, local, i) for i, pair in enumerate(pairs)]

    @pl.when(steps[0])
    def _():
        meet("rep", [*along.hops, along.partner])
        for plan in plans:
            along.begin(plan)

    @pl.when(steps[1])
    def _():
        for plan in plans:
            along.first_hop(plan)

    @pl.when(steps[2])
    def _():
        for plan in plans:
            along.second_hop(plan)

    def finish():
        for plan in plans:
            along.relayed(plan)
        for plan in plans:
            along.end(plan)

    return finish


def spread_maps(maps_ref, wide_ref, start):
    count, packs, columns = maps_ref.shape

    def spread(i, _):
        for u in range(2):
            t = 2 * i + u
            maps = maps_ref[t]
            for n in range(columns):
                wide_ref[n, start + t] = jnp.broadcast_to(maps[:, n : n + 1], (packs, LANES))
        return 0

    lax.fori_loop(0, count // 2, spread, 0)


def scan_kernel(
    rep,
    channels,
    decay_step_ref,
    input_ref,
    maps_ref,
    rate_ref,
    beside_ref,
    out_ref,
    decayed_ref,
    beside_out_ref,
    wide_ref,
    local,
    far,
    near,
):
    count, packs, _ = decay_step_ref.shape
    valid = (
        lax.broadcasted_iota(jnp.int32, (packs, LANES), 1)
        < channels - pl.program_id(1) * LANES
    )
    rate = jnp.where(valid[:1], rate_ref[...], 0.0)
    at = pl.program_id(0) * pl.num_programs(1) + pl.program_id(1)
    last = pl.num_programs(0) * pl.num_programs(1) - 1
    steps = [at == step for step in (0, 2 * last // 3, last)]
    finish = spread_beside(rep, steps, [(beside_ref, beside_out_ref)], local, far, near)

    @pl.when(pl.program_id(1) == 0)
    def _():
        spread_maps(maps_ref, wide_ref, 0)

    def step(i, states):
        for u in range(2):
            t = 2 * i + u
            decay_step = jnp.where(valid, decay_step_ref[t], 0.0)
            inputs = jnp.where(valid, input_ref[t], 0.0)
            out = jnp.zeros((packs, LANES), f32)
            new_states = []
            for n in range(STATE):
                decayed = jnp.exp2(decay_step * rate[n : n + 1]) * states[n]
                state = decayed + wide_ref[n, t] * inputs
                out = out + state * wide_ref[STATE + n, t]
                decayed_ref[n, t] = decayed
                new_states.append(state)
            out_ref[t] = out
            states = tuple(new_states)
        return states

    lax.fori_loop(0, count // 2, step, (jnp.zeros((packs, LANES), f32),) * STATE)
    pl.when(at == last)(finish)


def scan_forward(decay_step, inputs, maps, rate, rep, collective_id, beside):
    count, packs, channels = inputs.shape
    wide = pl.BlockSpec((count, PACKS, LANES), lambda g, i: (0, g, i))
    return pl.pallas_call(
        functools.partial(scan_kernel, rep, channels),
        grid=(packs // PACKS, pl.cdiv(channels, LANES)),
        in_specs=[
            wide,
            wide,
            pl.BlockSpec((count, PACKS, 2 * STATE), lambda g, i: (0, g, 0)),
            pl.BlockSpec((STATE, LANES), lambda g, i: (0, i)),
            hbm_spec(),
        ],
        out_specs=[
            wide,
            pl.BlockSpec((STATE, count, PACKS, LANES), lambda g, i: (0, 0, g, i)),
            hbm_spec(),
        ],
        out_shape=[
            jax.ShapeDtypeStruct(inputs.shape, f32),
            jax.ShapeDtypeStruct(
                (STATE, count, packs, pl.cdiv(channels, LANES) * LANES), f32
            ),
            jax.ShapeDtypeStruct((rep,) + beside.shape, beside.dtype),
        ],
        scratch_shapes=[
            pltpu.VMEM((2 * STATE, count, PACKS, LANES), f32),
            pltpu.SemaphoreType.DMA((1,)),
            pltpu.SemaphoreType.DMA((2, 1, rep // 2)),
            pltpu.SemaphoreType.DMA((2, 1, rep // 2)),
        ],
        compiler_params=pltpu.CompilerParams(
            collective_id=collective_id,
            has_side_effects=True,
            vmem_limit_bytes=48 * 1024 * 1024,
        ),
        cost_estimate=SMALL_COST,
    )(decay_step, inputs, maps, rate, beside)


def scan_back_kernel(
    rep,
    channels,
    decay_step_ref,
    step_ref,
    input_ref,
    maps_ref,
    grad_ref,
    decayed_ref,
    rate_ref,
    beside_ref,
    beside2_ref,
    grad_input_ref,
    grad_step_ref,
    grad_rate_ref,
    grad_maps_ref,
    beside_out_ref,
    beside2_out_ref,
    carry_ref,
    rates_ref,
    in_sum_ref,
    out_sum_ref,
    both_sum_ref,
    wide_ref,
    local,
    far,
    near,
):
    count, packs, _ = decay_step_ref.shape
    at = (pl.program_id(0) * pl.num_programs(1) + pl.program_id(1)) * pl.num_programs(2)
    at = at + pl.program_id(2)
    last = pl.num_programs(0) * pl.num_programs(1) * pl.num_programs(2) - 1
    steps = [at == step for step in (0, 9 * last // 16, 12 * last // 16)]
    pairs = [(beside_ref, beside_out_ref), (beside2_ref, beside2_out_ref)]
    finish = spread_beside(rep, steps, pairs, local, far, near)
    tile, chunk = pl.program_id(1), pl.program_id(2)
    start = (pl.num_programs(2) - 1 - chunk) * count
    valid = lax.broadcasted_iota(jnp.int32, (packs, LANES), 1) < channels - tile * LANES

    @pl.when(tile == 0)
    def _():
        spread_maps(maps_ref, wide_ref, start)
        zeros = jnp.zeros((STATE, count, packs, LANES), f32)
        in_sum_ref[:, pl.ds(start, count)] = zeros
        out_sum_ref[:, pl.ds(start, count)] = zeros
        both_sum_ref[pl.ds(start, count)] = zeros[0]

    @pl.when(chunk == 0)
    def _():
        carry_ref[...] = jnp.zeros_like(carry_ref)
        for n in range(STATE):
            rates_ref[n] = jnp.where(
                valid, jnp.broadcast_to(rate_ref[n : n + 1, :], (packs, LANES)), 0.0
            )

    def backward(back_t, carried):
        grad_states, grad_rates = carried
        t = count - 1 - back_t
        at = start + t
        decay_step = jnp.where(valid, decay_step_ref[t], 0.0)
        step = jnp.where(valid, step_ref[t], 0.0)
        inputs = jnp.where(valid, input_ref[t], 0.0)
        grad = jnp.where(valid, grad_ref[t], 0.0)
        both_sum_ref[at] += grad * inputs
        grad_input = grad_step = jnp.zeros((packs, LANES), f32)
        new_states, new_rates = [], []
        for n in range(STATE):
            decayed, rate = decayed_ref[n, t], rates_ref[n]
            grad_state = grad * wide_ref[STATE + n, at] + grad_states[n]
            out_sum_ref[n, at] += grad * decayed
            in_sum_ref[n, at] += grad_state * inputs
            grad_input = grad_input + grad_state * wide_ref[n, at]
            through = grad_state * decayed
            grad_step = grad_step + through * rate
            new_rates.append(grad_rates[n] + through * step)
            new_states.append(jnp.exp2(decay_step * rate) * grad_state)
        grad_input_ref[t] = grad_input
        grad_step_ref[t] = grad_step
        return (tuple(new_states), tuple(new_rates))

    carried = (
        tuple(carry_ref[n] for n in range(STATE)),
        tuple(carry_ref[STATE + n] for n in range(STATE)),
    )
    grad_states, grad_rates = lax.fori_loop(0, count, backward, carried)
    for n in range(STATE):
        carry_ref[n] = grad_states[n]
        carry_ref[STATE + n] = grad_rates[n]

    @pl.when(chunk == pl.num_programs(2) - 1)
    def _():
        for n in range(STATE):
            grad_rate_ref[n : n + 1, :] = jnp.sum(grad_rates[n], axis=0, keepdims=True)

    @pl.when(tile == pl.num_programs(1) - 1)
    def _():
        column = lax.broadcasted_iota(jnp.int32, (LANES, LANES), 1)
        here = pl.ds(start, count)

        def summed(value, place):
            return jnp.dot(
                value.reshape(count * packs, LANES).astype(bf16),
                (column == place).astype(bf16),
                preferred_element_type=f32,
            )

        total = summed(both_sum_ref[here], 2 * STATE)
        for n in range(STATE):
            total = total + summed(in_sum_ref[n, here], n)
            total = total + summed(out_sum_ref[n, here], STATE + n)
        grad_maps_ref[here] = total.reshape(count, packs, LANES)

    pl.when(at == last)(finish)


def scan_backward(decay_step, step, inputs, maps, grad, decayed, rate, rep, collective_id, beside):
    count, packs, channels = inputs.shape
    groups, chunks = packs // PACKS, 4
    part = count // chunks
    wide = pl.BlockSpec((part, PACKS, LANES), lambda g, i, c: (chunks - 1 - c, g, i))
    row = pl.BlockSpec((STATE, LANES), lambda g, i, c: (0, i))
    sums = pltpu.VMEM((STATE, count, PACKS, LANES), f32)
    grad_inputs, grad_step, grad_rate, grad_maps, *all_beside = pl.pallas_call(
        functools.partial(scan_back_kernel, rep, channels),
        grid=(groups, pl.cdiv(channels, LANES), chunks),
        in_specs=[
            wide,
            wide,
            wide,
            pl.BlockSpec((part, PACKS, 2 * STATE), lambda g, i, c: (chunks - 1 - c, g, 0)),
            wide,
            pl.BlockSpec(
                (STATE, part, PACKS, LANES), lambda g, i, c: (0, chunks - 1 - c, g, i)
            ),
            row,
        ]
        + [hbm_spec()] * 2,
        out_specs=[
            wide,
            wide,
            pl.BlockSpec((STATE, LANES), lambda g, i, c: (g, i)),
            pl.BlockSpec((count, PACKS, LANES), lambda g, i, c: (0, g, 0)),
        ]
        + [hbm_spec()] * 2,
        out_shape=[
            jax.ShapeDtypeStruct(inputs.shape, f32),
            jax.ShapeDtypeStruct(inputs.shape, f32),
            jax.ShapeDtypeStruct((groups * STATE, channels), f32),
            jax.ShapeDtypeStruct((count, packs, LANES), f32),
        ]
        + [jax.ShapeDtypeStruct((rep,) + x.shape, x.dtype) for x in beside],
        scratch_shapes=[
            pltpu.VMEM((2 * STATE, PACKS, LANES), f32),
            pltpu.VMEM((STATE, PACKS, LANES), f32),
            sums,
            sums,
            pltpu.VMEM((count, PACKS, LANES), f32),
            pltpu.VMEM((2 * STATE, count, PACKS, LANES), f32),
            pltpu.SemaphoreType.DMA((2,)),
            pltpu.SemaphoreType.DMA((2, 2, rep // 2)),
            pltpu.SemaphoreType.DMA((2, 2, rep // 2)),
        ],
        compiler_params=pltpu.CompilerParams(
            collective_id=collective_id,
            has_side_effects=True,
            vmem_limit_bytes=52 * 1024 * 1024,
        ),
        cost_estimate=SMALL_COST,
    )(decay_step, step, inputs, maps, grad, decayed, rate, *beside)
    grad_rate = jnp.sum(grad_rate.reshape(groups, STATE, channels), axis=0)
    in_maps, both = grad_maps[:, :, :STATE], grad_maps[:, :, 2 * STATE : 2 * STATE + 1]
    out_maps = grad_maps[:, :, STATE : 2 * STATE] + maps[:, :, :STATE] * both
    grad_maps = jnp.concatenate([in_maps, out_maps], axis=2).reshape(count * packs, 2 * STATE)
    return grad_inputs, grad_step, grad_rate, grad_maps, all_beside


def split_heads(qkv_low):
    count = qkv_low.shape[0]
    group_size = HEADS // KV_HEADS
    query_width = HEADS * HEAD_DIM
    kv_width = KV_HEADS * HEAD_DIM
    query_rows = qkv_low[:, :query_width].reshape(count, KV_HEADS, group_size, HEAD_DIM)
    key_rows = qkv_low[:, query_width : query_width + kv_width].reshape(count, KV_HEADS, HEAD_DIM)
    value_rows = qkv_low[:, query_width + kv_width :].reshape(count, KV_HEADS, HEAD_DIM)
    return (query_rows, key_rows, value_rows)


def masked_scores(query_rows, key_rows, allowed):
    attention_scores = jnp.einsum(
        "jzhx,kzx->zhjk", query_rows, key_rows, preferred_element_type=f32
    ) * HEAD_DIM ** (-0.5)
    return jnp.where(allowed[None, None], attention_scores, -1e30)


def attention_forward(qkv_low, allowed):
    count = qkv_low.shape[0]
    query_rows, key_rows, value_rows = split_heads(qkv_low)
    attention_scores = masked_scores(query_rows, key_rows, allowed)
    row_max = jnp.max(attention_scores, axis=-1, keepdims=True)
    weights_exp = jnp.exp(attention_scores - row_max)
    row_total = jnp.sum(weights_exp, axis=-1, keepdims=True)
    lowered_probabilities = (weights_exp / row_total).astype(bf16)
    attended_values = jnp.einsum(
        "lpho,ole->hlpe", lowered_probabilities, value_rows, preferred_element_type=f32
    )
    return (attended_values.reshape(count, HEADS * HEAD_DIM), row_max + jnp.log(row_total))


def attention_backward(qkv_low, grad_low, log_total, allowed):
    count = qkv_low.shape[0]
    query_rows, key_rows, value_rows = split_heads(qkv_low)
    probabilities = jnp.exp(masked_scores(query_rows, key_rows, allowed) - log_total)
    head_gradient = grad_low.reshape(count, KV_HEADS, HEADS // KV_HEADS, HEAD_DIM)
    grad_probs = jnp.einsum(
        "jzhx,kzx->zhjk", head_gradient, value_rows, preferred_element_type=f32
    )
    score_gradient = (
        probabilities * (grad_probs - jnp.sum(grad_probs * probabilities, axis=-1, keepdims=True))
    ).astype(bf16)
    scale_factor_scores = HEAD_DIM ** (-0.5)
    grad_queries = (
        jnp.einsum("lpho,ole->hlpe", score_gradient, key_rows, preferred_element_type=f32)
        * scale_factor_scores
    )
    grad_keys = (
        jnp.einsum("wniv,iwne->vwe", score_gradient, query_rows, preferred_element_type=f32)
        * scale_factor_scores
    )
    grad_values = jnp.einsum(
        "wniv,iwne->vwe", probabilities.astype(bf16), head_gradient, preferred_element_type=f32
    )
    return jnp.concatenate(
        [
            grad_queries.reshape(count, -1),
            grad_keys.reshape(count, -1),
            grad_values.reshape(count, -1),
        ],
        axis=1,
    )


def tied(value, *others):
    return lax.optimization_barrier((value,) + others)[0]


def by_row(value):
    return with_layout_constraint(value, Layout(major_to_minor=(0, 1)))


def silu_and_slope(value):
    gate = jax.nn.sigmoid(value)
    return value * gate, gate * (1.0 + value * (1.0 - gate))


def shift_down(rows, amount):
    return jnp.concatenate([jnp.zeros((amount,) + rows.shape[1:], rows.dtype), rows[:-amount]], 0)


def shift_up(rows, amount):
    return jnp.concatenate([rows[amount:], jnp.zeros((amount,) + rows.shape[1:], rows.dtype)], 0)


def per_device(
    rep,
    fsdp,
    tokens,
    cotangent,
    lengths,
    source_slot,
    norm_in,
    w_qkv,
    w_mamba_in,
    conv_weight,
    conv_bias,
    x_proj,
    dt_proj,
    dt_bias,
    a_log,
    d_skip,
    w_mamba_out,
    norm_attn,
    norm_ssm,
    w_mix_out,
    norm_ffn,
    w_gate,
    w_up,
    w_down,
):
    count, width = tokens.shape
    block_rows = count // fsdp
    piece, ff_piece = INNER // (rep * fsdp), w_gate.shape[1] // (rep * fsdp)
    channels, ff_part = fsdp * up16(piece), fsdp * up16(ff_piece)
    qkv_part = w_qkv.shape[1] // rep
    group = rep * count
    high = lax.Precision.HIGH
    me, line = lax.axis_index("rep"), lax.axis_index("fsdp")

    def my_part(value, axis):
        rest = value.shape[axis] // (rep * fsdp)
        spare = [(0, up16(rest) - rest if i == axis else 0) for i in range(value.ndim)]
        return jnp.concatenate(
            [
                jnp.pad(lax.dynamic_slice_in_dim(value, (i * rep + me) * rest, rest, axis), spare)
                for i in range(fsdp)
            ],
            axis=axis,
        )

    def my_rows(value):
        rest = value.shape[0] // rep
        part = lax.dynamic_slice_in_dim(value, me * rest, rest, 0)
        return jnp.pad(part, ((0, up16(rest) - rest), (0, 0)))

    def line_gather(value):
        return lax.all_gather(value, "fsdp", axis=0, tiled=True)

    def line_scatter(value):
        return lax.psum_scatter(value, "fsdp", scatter_dimension=0, tiled=True)

    def swapped(rows):
        lead = count if rows.shape[0] == count else rep
        return rows.transpose(1, 0, 2).reshape(group, rows.shape[2])

    early_width = -(-(qkv_part + channels) // LANES) * LANES
    gate_at = -(-(channels + qkv_part) // LANES) * LANES
    in_width = -(-(gate_at + channels) // LANES) * LANES
    part_in = by_rows(
        functools.partial(part_in_kernel, rep, fsdp, (0, channels, gate_at)),
        (w_qkv, w_mamba_in),
        in_width,
    )
    full_in = line_gather(part_in)
    mix_part = width // rep
    part_mix = lax.dynamic_slice_in_dim(w_mix_out, me * mix_part, mix_part, 1)
    mix_size = part_mix.size
    part_mix = jnp.pad(part_mix.reshape(-1), (0, -mix_size % (16 * width))).reshape(-1, width)
    part_mout, part_down = my_rows(w_mamba_out), my_rows(w_down)

    received, cot_received = line_exchange(
        fsdp,
        0,
        trades=(
            tied(tokens, part_in).reshape(fsdp, block_rows, width),
            cotangent.reshape(fsdp, block_rows, width),
        ),
    )
    w_gate, w_up, part_mout, part_mix, part_down, received = lax.optimization_barrier(
        (w_gate, w_up, part_mout, part_mix, part_down, received)
    )
    mout_mix = line_gather(jnp.concatenate([part_mout, part_mix], axis=0))
    part_gate_up = by_rows(
        functools.partial(part_gate_up_kernel, rep, fsdp), (w_gate, w_up), 2 * ff_part
    )
    full_gate_up, full_down = line_gather(part_gate_up), line_gather(part_down)
    slots = source_slot[0]
    picks = (slots[:, None] == jnp.arange(count, dtype=jnp.int32)[None, :]).astype(bf16)
    hidden_in = dot(picks, received.reshape(count, width))
    cot_rows = dot(picks, cot_received.reshape(count, width))
    cot_low = cot_rows.astype(bf16)

    ends = jnp.cumsum(lengths[0], dtype=jnp.int32)
    positions = jnp.arange(count, dtype=jnp.int32)
    passed = positions[:, None] >= ends[None, :-1]
    seg_ids = jnp.sum(passed.astype(jnp.int32), axis=1)
    in_seq = positions - jnp.max(jnp.where(passed, ends[None, :-1], 0), axis=1)
    distance = positions[:, None] - positions[None, :]
    allowed = (seg_ids[:, None] == seg_ids[None, :]) & (distance >= 0) & (distance < WINDOW)

    normed, norm_in_pull = jax.vjp(rms_norm, hidden_in, norm_in)
    marks = jnp.broadcast_to(in_seq[:, None].astype(bf16), (count, 64))
    normed_marked = jnp.concatenate([normed.astype(bf16), marks], axis=1)
    normed_sent, cot_all = rep_exchange(rep, 1, gathers=(normed_marked, cot_low))
    cot_all = cot_all.reshape(group, width)
    normed_all = normed_sent[:, :, :width].reshape(group, width)
    in_seq_all = normed_sent[:, :, width].astype(f32).T.reshape(group, 1)

    in_out = dot(swapped(normed_all.reshape(rep, count, width)), full_in)
    xs, gate_z = in_out[:, :channels], in_out[:, gate_at : gate_at + channels]
    qkv_sent = in_out[:, channels : channels + qkv_part].astype(bf16)
    qkv_sent = swapped(qkv_sent.reshape(count, rep, qkv_part))

    conv_w, conv_b = my_part(conv_weight, 1), my_part(conv_bias, 0)
    part_x_proj, part_dt_proj = my_part(x_proj, 0), my_part(dt_proj, 1)
    part_dt_bias, part_skip = my_part(dt_bias, 0), my_part(d_skip, 0)
    rate = -jnp.exp(my_part(a_log, 1))
    conv_sum = xs * conv_w[CONV - 1] + conv_b
    for k in range(1, CONV):
        earlier = jnp.where(in_seq_all >= k, shift_down(xs, k * rep), 0.0)
        conv_sum = conv_sum + earlier * conv_w[CONV - 1 - k]
    act, act_slope = silu_and_slope(conv_sum)
    proj_sent = dot(act, part_x_proj, high).astype(bf16).reshape(count, rep, -1)
    proj_sent = proj_sent.transpose(1, 0, 2)
    proj, qkv_back = rep_exchange(
        rep, 2, alls=(proj_sent,), trades=(qkv_sent.reshape(rep, count, qkv_part),)
    )
    mout_mix = hand_on(mout_mix, proj)
    mout_mix = mout_mix.reshape(fsdp, -1, width)
    full_mout = mout_mix[:, : part_mout.shape[0]].reshape(-1, width)
    mix_t = mout_mix[:, part_mout.shape[0] :].reshape(fsdp, -1)[:, :mix_size]
    mix_t = mix_t.reshape(width, mix_part).T
    qkv_low = qkv_back.transpose(1, 0, 2).reshape(count, rep * qkv_part)
    proj = proj.transpose(1, 0, 2).astype(f32)
    dt_in = proj.reshape(group, -1)[:, :DT_RANK]
    maps = proj[:, :, DT_RANK:]
    dt_sum = dot(dt_in, part_dt_proj, high) + part_dt_bias
    step = jax.nn.softplus(dt_sum)
    decay_step = jnp.where(in_seq_all == 0.0, 1e30, step * LOG2_E)
    inputs = step * act
    cube = (count, rep, channels)
    scanned, decayed, mix_t = scan_forward(
        decay_step.reshape(cube), inputs.reshape(cube), maps, rate, rep, 9, mix_t
    )
    mix_t = mix_t.reshape(width, width)
    scanned = scanned.reshape(group, channels)
    silu_z, z_slope = silu_and_slope(gate_z)
    before_gate = scanned + part_skip * act
    mixer_low = swapped((before_gate * silu_z).astype(bf16).reshape(cube))
    ssm_part = by_row(dot(mixer_low, full_mout).astype(bf16)).reshape(rep, count, width)
    (ssm_out,) = rep_exchange(rep, 3, sums=(ssm_part,))

    attended_values, log_total = attention_forward(qkv_low, allowed)
    mixed, mix_pull = jax.vjp(mix_branches, attended_values, ssm_out, norm_attn, norm_ssm)
    mixed_low = mixed.astype(bf16)
    middle = hidden_in + dot_right_t(mixed_low, mix_t)
    ffn_in, ffn_pull = jax.vjp(rms_norm, middle, norm_ffn)
    ffn_all, mixed_all = rep_exchange(rep, 4, gathers=(ffn_in.astype(bf16), mixed_low))
    ffn_all, mixed_all = ffn_all.reshape(group, width), mixed_all.reshape(group, width)

    gate_up = dot(ffn_all, full_gate_up)
    hidden, swiglu_pull = jax.vjp(swiglu, gate_up[:, :ff_part], gate_up[:, ff_part:])
    hidden_low = hidden.astype(bf16)
    grad_hidden = dot_right_t(cot_all, full_down)
    grad_gate_up = jnp.concatenate(swiglu_pull(grad_hidden), axis=1).astype(bf16)
    part_gate_up = dot_left_t(ffn_all, grad_gate_up).astype(bf16)
    own_gate_up = line_scatter(part_gate_up)
    grad_gate_up = tied(grad_gate_up, part_gate_up)
    ffn_sent = by_row(dot_right_t(grad_gate_up, full_gate_up).astype(bf16))
    part_down = dot_left_t(hidden_low, cot_all).astype(bf16)
    own_down = line_scatter(part_down)
    down_sent = by_row(dot(tied(hidden_low, part_down), full_down).astype(bf16))
    blocks = (rep, count, width)
    grad_ffn, down_out = rep_exchange(
        rep, 5, sums=(ffn_sent.reshape(blocks), down_sent.reshape(blocks))
    )
    result = middle + down_out

    grad_middle_norm, grad_norm_ffn = ffn_pull(grad_ffn)
    grad_middle = cot_rows + grad_middle_norm
    middle_low = grad_middle.astype(bf16)
    grad_mixed = dot(middle_low, mix_t)
    grad_attended, grad_ssm, grad_norm_attn, grad_norm_ssm = mix_pull(grad_mixed)
    middle_sent = middle_low.reshape(count, rep, -1).transpose(1, 0, 2)
    qkv_grad = attention_backward(qkv_low, grad_attended.astype(bf16), log_total, allowed)
    qkv_grad = qkv_grad.astype(bf16).reshape(count, rep, -1).transpose(1, 0, 2)
    ssm_all, middle_cols, qkv_cols = rep_exchange(
        rep, 6, gathers=(grad_ssm.astype(bf16),), trades=(middle_sent, qkv_grad)
    )
    qkv_cols = qkv_cols.reshape(group, qkv_part)
    ssm_all = tied(ssm_all, own_gate_up).reshape(group, width)
    grad_mixer = dot_right_t(ssm_all, full_mout).astype(bf16).reshape(rep, count, channels)
    grad_mixer = swapped(grad_mixer).astype(f32)
    part_mout = dot_left_t(mixer_low, ssm_all).astype(bf16)
    part_mix = dot_left_t(mixed_all, middle_cols.reshape(group, -1)).astype(bf16)

    grad_z = (grad_mixer * before_gate * z_slope).astype(bf16)
    grad_z = swapped(grad_z.reshape(cube))
    spare = early_width - qkv_part - channels
    early_grad = jnp.concatenate([qkv_cols, jnp.zeros((group, spare), bf16), grad_z], axis=1)
    part_early = dot_left_t(normed_all, early_grad).astype(bf16)
    grad_mixer = tied(grad_mixer, part_mout, part_mix, part_early, own_down)
    own_mout, own_mix = line_scatter(part_mout), line_scatter(part_mix)
    own_early = line_scatter(part_early)
    grad_before = grad_mixer * silu_z
    grad_skip = jnp.sum(grad_before * act, axis=0)
    grad_inputs, grad_step, grad_rate, grad_maps, (all_gate_up, all_down) = scan_backward(
        *(item.reshape(cube) for item in (decay_step, step, inputs)),
        maps,
        grad_before.reshape(cube),
        decayed,
        rate,
        rep,
        7,
        (own_gate_up, own_down),
    )
    grad_inputs = grad_inputs.reshape(group, channels)
    grad_step = grad_step.reshape(group, channels)
    grad_a_log = grad_rate * rate
    grad_step = grad_step + grad_inputs * act
    grad_dt = grad_step * jax.nn.sigmoid(dt_sum)
    grad_dt_bias = jnp.sum(grad_dt, axis=0)
    grad_dt_proj = dot_left_t(dt_in, grad_dt)
    proj_sent = jnp.concatenate(
        [dot_right_t(grad_dt, part_dt_proj), grad_maps], axis=1
    )
    proj_sent = proj_sent.astype(bf16).reshape(count, rep, -1).transpose(1, 0, 2)
    (grad_proj,) = rep_exchange(rep, 11, alls=(proj_sent,))
    grad_proj = swapped(tied(grad_proj, own_mout, own_mix))
    grad_x_proj = dot_left_t(grad_proj, act)
    grad_act = grad_before * part_skip + grad_inputs * step + dot_right_t(grad_proj, part_x_proj)
    grad_conv = grad_act * act_slope
    grad_conv_b = jnp.sum(grad_conv, axis=0)
    grad_conv_w = [jnp.sum(grad_conv * xs, axis=0)]
    grad_xs = grad_conv * conv_w[CONV - 1]
    for k in range(1, CONV):
        reached = jnp.where(in_seq_all >= k, grad_conv, 0.0)
        grad_conv_w.insert(0, jnp.sum(reached * shift_down(xs, k * rep), axis=0))
        grad_xs = grad_xs + shift_up(reached, k * rep) * conv_w[CONV - 1 - k]
    small = jnp.concatenate(
        [jnp.stack(grad_conv_w), grad_conv_b[None], grad_dt_bias[None], grad_skip[None]]
        + [grad_a_log, grad_dt_proj, grad_x_proj],
        axis=0,
    )
    n_small = fsdp * up16(-(-small.shape[0] // fsdp))
    small = jnp.pad(small, ((0, n_small - small.shape[0]), (0, 0))).astype(bf16)
    grad_xs = swapped(grad_xs.astype(bf16).reshape(cube))
    gap = jnp.zeros((group, gate_at - channels - qkv_part), bf16)
    end = jnp.zeros((group, in_width - gate_at - channels), bf16)
    in_grad = jnp.concatenate([grad_xs, qkv_cols, gap, grad_z, end], axis=1)
    normed_part = by_row(dot_right_t(in_grad, full_in).astype(bf16)).reshape(blocks)
    own_late = line_scatter(dot_left_t(normed_all, grad_xs).astype(bf16))
    (grad_normed,) = rep_exchange(rep, 8, sums=(normed_part,))
    grad_hidden_norm, grad_norm_in = norm_in_pull(grad_normed)
    grad_hidden_in = grad_middle + grad_hidden_norm

    def given_back(rows):
        return dot_left_t(picks, rows.astype(bf16)).astype(bf16).reshape(fsdp, block_rows, width)

    gains = jnp.stack([grad_norm_in, grad_norm_attn, grad_norm_ssm, grad_norm_ffn])
    gains = jnp.concatenate([gains, jnp.zeros((4, width), f32)], axis=0)
    (
        sum_gate,
        sum_up,
        sum_down,
        all_mout,
        all_mix,
        all_early,
        all_late,
        small,
        gains,
        mixed_out,
        grad_tokens,
    ) = last_exchange(
        rep,
        fsdp,
        10,
        (all_gate_up, all_down, w_gate.shape[1], w_down.shape[0]),
        (own_mout, own_mix, own_early, own_late),
        small.reshape(fsdp, -1, channels),
        gains,
        (given_back(result), given_back(grad_hidden_in)),
    )
    gains, small = jnp.sum(gains, axis=0), small.reshape(rep, n_small, channels)
    sum_mamba_in, sum_qkv, sum_mix = join_columns(
        rep,
        (all_late, all_early, all_mix),
        (w_mamba_in.shape[1], w_qkv.shape[1], width),
        (
            ((0, 0, piece, 0, fsdp), (1, early_width - channels, piece, INNER, fsdp)),
            ((1, 0, qkv_part, 0, 1),),
            ((2, 0, width // rep, 0, 1),),
        ),
    )
    sum_mout = join_rows(rep, all_mout, w_mamba_out.shape[0], width)

    (small,) = join_columns(rep, (small,), (INNER,), (((0, 0, piece, 0, fsdp),),))
    ends = [CONV, CONV + 1, CONV + 2, CONV + 3, CONV + 3 + STATE, CONV + 3 + STATE + DT_RANK]
    ends.append(ends[-1] + x_proj.shape[1])
    return (
        mixed_out.reshape(count, width),
        grad_tokens.reshape(count, width),
        gains[0],
        sum_qkv,
        sum_mamba_in,
        small[: ends[0]],
        small[ends[0]],
        small[ends[5] : ends[6]].T,
        small[ends[4] : ends[5]],
        small[ends[1]],
        small[ends[3] : ends[4]],
        small[ends[2]],
        sum_mout,
        gains[1],
        gains[2],
        sum_mix,
        gains[3],
        sum_gate.astype(f32),
        sum_up.astype(f32),
        sum_down.astype(f32).T,
    )


def solution(mesh):
    rows = P(("rep", "fsdp"), None)
    cut = P("fsdp", None)
    whole = P()
    return jax.shard_map(
        functools.partial(per_device, mesh.shape["rep"], mesh.shape["fsdp"]),
        mesh=mesh,
        in_specs=(rows,) * 4
        + (whole, cut, cut)
        + (whole,) * 7
        + (cut, whole, whole, cut, whole, cut, cut, cut),
        out_specs=(rows, rows, whole, cut, cut)
        + (whole,) * 7
        + (cut, whole, whole, cut, whole, cut, cut, cut),
        check_vma=False,
    )
```
